32 devices in a mesh: samp: 4 (over y, x), chrom: 8 (over z, core).
Axes of the slice: x: 2, y: 2, z: 4, core: 2. Of those that a mesh axis runs over, the one named last changes fastest.
Arguments:
- dosages: float32 [4096, 8192], P('samp', 'chrom'), may hold values from -12 to 12
- traits: float32 [4096, 128], P('samp'), may hold values from -14 to 14
- start_coef: float32 [8192, 128], P('chrom'), may hold values from -1 to 1
- groups: int32 [8192], P('chrom'), may hold values from 0 to 15, as said below
- tested: bfloat16 [4096, 8192], P('samp', 'chrom'), may hold values from -16 to 16
- owners: int32 [8192], P('chrom'), may hold values from 0 to 15, as said below
Outputs:
- scores: float32 [8192, 128], P('chrom')
- residual: float32 [4096, 128], P('samp')
The draws below stay inside these ranges and needn't reach their ends.
Inputs may be any that keep to these rules, and one draw needn't show every extreme that they name: `groups`: training variant j belongs to group 2 * (j // 1024) + r with r from 0 to 1; every such group has a variant. `owners`: tested variant i belongs to group 2 * (i // 1024) + r with r from 0 to 1; every such group has a tested variant.
All inputs are finite; a program needn't handle non-finite values.
Results may differ from the reference program's by a relative error of at most 0.00045.
The reference program's roundings to bfloat16 on the way count: a program that leaves them out, or rounds other values in their place, can miss the bound.
Values sent between devices are 32-bit elements; how exact they have to be, the bound alone decides.
No kernel may reach another device: no remote copies, remote signals or barrier semaphores. Data moves between devices by JAX's collectives and lax.ppermute only.
A program may use at most 64 MiB of HBM per device.

```python
import math
import jax
import jax.numpy as jnp
from jax import lax

M_DEV = 1024
K = 128
TEST_DEV = 1024
GPD = 2
ITERS = 2
N = 4096
M = 8192
TESTS = 8192
N_CHROM = 8


def strong_rows(key):
    phase = jax.random.randint(jax.random.fold_in(key, 31), (), 0, 2, dtype=jnp.int32)
    rows = jnp.arange(N, dtype=jnp.int32)
    return (rows % 2 == phase).astype(jnp.float32)[:, None]


def draw_dosages(key, part):
    strong = strong_rows(key)
    spread = jnp.exp(jax.random.uniform(jax.random.fold_in(key, 41), (N, 1), jnp.float32, 0.0, math.log(4.0)))
    base = jnp.clip(jax.random.normal(jax.random.fold_in(key, 43), (N, M), jnp.float32), -4.0, 4.0)
    return base * (0.5 * (1.0 + 0.4 * strong) * spread)


def draw_traits(key, part):
    rows = jnp.arange(N, dtype=jnp.float32) / N
    level = jnp.sqrt(0.5 + 4.0 * rows)[:, None]
    strong = strong_rows(key)
    col_phase = jax.random.randint(jax.random.fold_in(key, 33), (), 0, 2, dtype=jnp.int32)
    tied = (jnp.arange(K, dtype=jnp.int32) % 2 == col_phase).astype(jnp.float32)[None, :]
    agree = strong * tied + (1.0 - strong) * (1.0 - tied)
    factor = 0.625 + 0.975 * agree
    base = jnp.clip(jax.random.normal(jax.random.fold_in(key, 35), (N, K), jnp.float32), -4.0, 4.0)
    return base * level * factor


def draw_start_coef(key, part):
    scale = jnp.exp(jax.random.uniform(jax.random.fold_in(key, 3), (M, 1), jnp.float32, jnp.log(0.3), jnp.log(3.0)))
    base = jnp.clip(jax.random.normal(jax.random.fold_in(key, 51), (M, K), jnp.float32), -5.0, 5.0)
    return base * scale / jnp.sqrt(jnp.float32(M))


def draw_tested(key, part):
    rows = jnp.arange(N, dtype=jnp.float32) / N
    level = jnp.sqrt(1.0 + 8.0 * rows)[:, None]
    base = jnp.clip(jax.random.normal(jax.random.fold_in(key, 53), (N, TESTS), jnp.float32), -5.0, 5.0)
    return (base * level).astype(jnp.bfloat16)


def owned_groups(key, count, per_dev):
    index = jnp.arange(count, dtype=jnp.int32)
    block = index // per_dev
    place = index % per_dev
    pick = jax.random.randint(key, (count,), 0, GPD, dtype=jnp.int32)
    pick = jnp.where(place == 0, 0, jnp.where(place == per_dev - 1, GPD - 1, pick))
    return (block * GPD + pick).astype(jnp.int32)


def draw_groups(key, part):
    return owned_groups(jax.random.fold_in(key, 11), M, M_DEV)


def draw_owners(key, part):
    return owned_groups(jax.random.fold_in(key, 13), TESTS, TEST_DEV)


def setup_inputs(seed: int = 0) -> dict:
    arg_keys = jax.random.split(jax.random.key(seed), 7)
    dosages = draw_dosages(jax.random.fold_in(arg_keys[6], 71), 0)
    traits = draw_traits(jax.random.fold_in(arg_keys[6], 71), 0)
    start_coef = draw_start_coef(jax.random.fold_in(arg_keys[6], 71), 0)
    groups = draw_groups(jax.random.fold_in(arg_keys[6], 71), 0)
    tested = draw_tested(jax.random.fold_in(arg_keys[6], 71), 0)
    owners = draw_owners(jax.random.fold_in(arg_keys[6], 71), 0)
    return dict(dosages=dosages, traits=traits, start_coef=start_coef, groups=groups, tested=tested, owners=owners)


def matmul(left, right):
    return jnp.dot(left, right, precision=lax.Precision.HIGHEST, preferred_element_type=jnp.float32)

def inner_rows(left, right):
    return lax.dot_general(left, right, (((0,), (0,)), ((), ())), precision=lax.Precision.HIGHEST, preferred_element_type=jnp.float32)

def reference(dosages, traits, start_coef, groups, tested, owners):
    total_rows = dosages.shape[0]
    penalty = 1.5 * math.sqrt(traits.shape[1] / total_rows)
    coefficients = start_coef
    for iteration in range(ITERS):
        residual_now = traits - matmul(dosages, coefficients)
        gradient = inner_rows(dosages, residual_now) / total_rows
        image = matmul(dosages, gradient)
        grad_sq = jnp.sum(gradient * gradient)
        image_sq = jnp.sum(image * image)
        step_size = grad_sq / (image_sq / total_rows + 1e-06)
        moved_rows = coefficients + step_size * gradient
        length = jnp.sqrt(lax.optimization_barrier(jnp.sum(moved_rows * moved_rows, axis=1, keepdims=True)))
        coefficients = moved_rows * (jnp.maximum(length - step_size * penalty, 0.0) / jnp.maximum(length, step_size * penalty))
    residual = traits - matmul(dosages, coefficients)

    def score_block(block):
        start = (block * M_DEV).astype(jnp.int32)
        dos_block = lax.dynamic_slice_in_dim(dosages, start, M_DEV, 1)
        coef_block = lax.dynamic_slice_in_dim(coefficients, start, M_DEV, 0)
        group_block = lax.dynamic_slice_in_dim(groups, start, M_DEV, 0)
        test_start = (block * TEST_DEV).astype(jnp.int32)
        test_block = lax.dynamic_slice_in_dim(tested, test_start, TEST_DEV, 1)
        owner_block = lax.dynamic_slice_in_dim(owners, test_start, TEST_DEV, 0)
        group_base = (block * GPD).astype(jnp.int32)
        picked = jnp.zeros((TEST_DEV, traits.shape[1]), jnp.float32)
        loco_pick = jnp.zeros((TEST_DEV, traits.shape[1]), jnp.float32)
        for which in range(GPD):
            mask = (group_block - group_base == which).astype(jnp.float32)[:, None]
            own_part = matmul(dos_block, coef_block * mask)
            loco_resid = residual + own_part
            loco_sq = lax.optimization_barrier(jnp.sum(loco_resid * loco_resid, axis=0))
            products = lax.dot_general(test_block, loco_resid.astype(jnp.bfloat16), (((0,), (0,)), ((), ())), preferred_element_type=jnp.float32)
            chosen = (owner_block - group_base == which).astype(jnp.float32)[:, None]
            picked = picked + chosen * products
            loco_pick = loco_pick + chosen * loco_sq[None, :]
        tested_sq = lax.optimization_barrier(jnp.sum(jnp.square(test_block.astype(jnp.float32)), axis=0))
        denom = math.sqrt(total_rows) * jnp.sqrt((tested_sq[:, None] / total_rows + 1e-06) * (loco_pick / total_rows + 1e-06))
        return picked / denom
    scores = lax.map(score_block, jnp.arange(N_CHROM, dtype=jnp.int32))
    scores = scores.reshape((TESTS, traits.shape[1]))
    return (scores, residual)
```

```python
import math

import jax
import jax.numpy as jnp
from jax import lax
from jax.sharding import PartitionSpec as P

GPD = 2
ITERS = 2


def matmul(left, right):
    return jnp.dot(left, right, precision=lax.Precision.HIGHEST, preferred_element_type=jnp.float32)


def inner_rows(left, right):
    return lax.dot_general(
        left,
        right,
        (((0,), (0,)), ((), ())),
        precision=lax.Precision.HIGHEST,
        preferred_element_type=jnp.float32,
    )


def swap(value, axis, bits):
    size = lax.axis_size(axis)
    return lax.ppermute(value, axis, [(i, i ^ bits) for i in range(size)])


def pieces(value, count):
    rows = value.shape[0] // count
    return [value[k * rows : (k + 1) * rows] for k in range(count)]


def chrom_scatter(value):
    keep, give = pieces(value, 2)
    keep = keep + swap(give, "chrom", 1)
    blocks = pieces(keep, lax.axis_size("chrom") // 2)
    got = [swap(block, "chrom", 2 * k) for k, block in enumerate(blocks) if k]
    total = blocks[0]
    for block in got:
        total = total + block
    return total


def chrom_gather(own):
    half = lax.axis_size("chrom") // 2
    first = jnp.concatenate([own] + [swap(own, "chrom", 2 * k) for k in range(1, half)])
    return jnp.concatenate([first, swap(first, "chrom", 1)])


def samp_scatter(value):
    blocks = pieces(value, lax.axis_size("samp"))
    got = [swap(block, "samp", k) for k, block in enumerate(blocks) if k]
    total = blocks[0]
    for block in got:
        total = total + block
    return total


def samp_gather(own):
    return jnp.concatenate([own] + [swap(own, "samp", k) for k in range(1, lax.axis_size("samp"))])


def all_sum(value):
    for axis in ("chrom", "samp"):
        total = value
        for k in range(1, lax.axis_size(axis)):
            total = total + swap(value, axis, k)
        value = total
    return value


def take_blocks(value, order, count, dim):
    size = value.shape[dim] // count
    return jnp.concatenate(
        [lax.dynamic_slice_in_dim(value, index * size, size, dim) for index in order], axis=dim
    )


def body(dosages, traits, start_coef, groups, tested, owners):
    n_samp, n_chrom = lax.axis_size("samp"), lax.axis_size("chrom")
    rows_dev = dosages.shape[0]
    total_rows = rows_dev * n_samp
    penalty = 1.5 * math.sqrt(traits.shape[1] / total_rows)
    my_samp, my_chrom = lax.axis_index("samp"), lax.axis_index("chrom")
    group_base = my_chrom * GPD

    row_bits = list(range(0, n_chrom, 2)) + list(range(1, n_chrom, 2))
    row_order = [my_chrom ^ j for j in row_bits]
    col_order = [my_samp ^ j for j in range(n_samp)]
    dosages = take_blocks(take_blocks(dosages, row_order, n_chrom, 0), col_order, n_samp, 1)
    traits = take_blocks(traits, row_order, n_chrom, 0)
    coefficients = take_blocks(start_coef, col_order, n_samp, 0)
    groups = take_blocks(groups, col_order, n_samp, 0)
    tested_rel = take_blocks(tested, row_order, n_chrom, 0)
    tested_rel = take_blocks(tested_rel, col_order, n_samp, 1)
    owners_rel = take_blocks(owners, col_order, n_samp, 0)

    group_masks = [(groups - group_base == which).astype(jnp.float32)[:, None] for which in range(GPD)]
    for iteration in range(ITERS):
        prediction = chrom_gather(chrom_scatter(matmul(dosages, coefficients)))
        residual_now = traits - prediction
        own_grad = samp_scatter(inner_rows(dosages, residual_now)) / total_rows
        gradient = samp_gather(own_grad)
        grad_sq = jnp.sum(own_grad * own_grad)
        image_part = chrom_scatter(matmul(dosages, gradient))
        image_sq = jnp.sum(image_part * image_part)
        sums = all_sum(jnp.stack([jnp.full((128,), grad_sq), jnp.full((128,), image_sq)]))
        grad_sq, image_sq = sums[0, 0], sums[1, 0]
        step_size = grad_sq / (image_sq / total_rows + 1e-06)
        moved_rows = coefficients + step_size * gradient
        length = jnp.sqrt(jnp.sum(moved_rows * moved_rows, axis=1, keepdims=True))
        coefficients = moved_rows * (
            jnp.maximum(length - step_size * penalty, 0.0)
            / jnp.maximum(length, step_size * penalty)
        )
    residual = traits - chrom_gather(chrom_scatter(matmul(dosages, coefficients)))
    own_parts = [matmul(dosages, coefficients * mask) for mask in group_masks]
    tested_sq = jnp.sum(jnp.square(tested_rel.astype(jnp.float32)), axis=0)
    picked = jnp.zeros((tested.shape[1], traits.shape[1]), jnp.float32)
    loco_list = []
    chosen_list = []
    for which in range(GPD):
        loco_resid = residual + own_parts[which]
        loco_list.append(jnp.sum(loco_resid * loco_resid, axis=0))
        products = lax.dot_general(
            tested_rel,
            loco_resid.astype(jnp.bfloat16),
            (((0,), (0,)), ((), ())),
            preferred_element_type=jnp.float32,
        )
        chosen = (owners_rel - group_base == which).astype(jnp.float32)[:, None]
        chosen_list.append(chosen)
        picked = picked + chosen * products
    picked = samp_scatter(picked)
    tested_sq = samp_scatter(tested_sq)
    loco_all = jnp.stack(loco_list)
    loco_all = sum([swap(loco_all, "samp", k) for k in range(1, n_samp)], loco_all)
    block = picked.shape[0]
    loco_pick = jnp.zeros_like(picked)
    for which in range(GPD):
        loco_pick = loco_pick + chosen_list[which][:block] * loco_all[which][None, :]
    denom = math.sqrt(total_rows) * jnp.sqrt(
        (tested_sq[:, None] / total_rows + 1e-06) * (loco_pick / total_rows + 1e-06)
    )
    scores = samp_gather(picked / denom)
    scores = take_blocks(scores, col_order, n_samp, 0)
    slots = [None] * n_chrom
    for place, bits in enumerate(row_bits):
        slots[bits] = place
    blocks = jnp.stack(pieces(residual, n_chrom))
    blocks = blocks[jnp.array(slots)]
    blocks = jnp.concatenate(
        [lax.dynamic_slice_in_dim(blocks, my_chrom ^ j, 1, 0) for j in range(n_chrom)]
    )
    return (scores, blocks.reshape(residual.shape))


def solution(mesh):
    placed = (
        P("samp", "chrom"),
        P("samp", None),
        P("chrom", None),
        P("chrom"),
        P("samp", "chrom"),
        P("chrom"),
    )
    return jax.shard_map(
        body,
        mesh=mesh,
        in_specs=placed,
        out_specs=(P("chrom", None), P("samp", None)),
        check_vma=False,
    )
```

```python
import math

import jax
import jax.numpy as jnp
from jax import lax
from jax.sharding import PartitionSpec as P

GPD = 2
ITERS = 2


def matmul(left, right):
    return jnp.dot(left, right, precision=lax.Precision.HIGHEST, preferred_element_type=jnp.float32)


def inner_rows(left, right):
    return lax.dot_general(
        left,
        right,
        (((0,), (0,)), ((), ())),
        precision=lax.Precision.HIGHEST,
        preferred_element_type=jnp.float32,
    )


def swap(value, axis, bits):
    size = lax.axis_size(axis)
    return lax.ppermute(value, axis, [(i, i ^ bits) for i in range(size)])


def core_groups():
    size = lax.axis_size("chrom")
    return [list(range(core, size, 2)) for core in range(2)]


def exchange(value, axis, groups=None):
    return lax.all_to_all(value, axis, 0, 0, axis_index_groups=groups, tiled=False)


def chrom_scatter(value, core):
    half = lax.axis_size("chrom") // 2
    blocks = value.reshape(half, 2, -1, value.shape[1])
    keep = lax.dynamic_index_in_dim(blocks, core, 1, keepdims=False)
    give = lax.dynamic_index_in_dim(blocks, 1 - core, 1, keepdims=False)
    keep = keep + swap(give, "chrom", 1)
    return jnp.sum(exchange(keep, "chrom", core_groups()), axis=0)


def chrom_gather(own, core):
    half = lax.axis_size("chrom") // 2
    mine = exchange(jnp.broadcast_to(own, (half,) + own.shape), "chrom", core_groups())
    other = swap(mine, "chrom", 1)
    first = jnp.where(core == 0, mine, other)
    second = jnp.where(core == 0, other, mine)
    return jnp.stack([first, second], axis=1).reshape(-1, own.shape[1])


def samp_scatter(value):
    size = lax.axis_size("samp")
    return jnp.sum(exchange(value.reshape((size, -1) + value.shape[1:]), "samp"), axis=0)


def samp_gather(own):
    size = lax.axis_size("samp")
    got = exchange(jnp.broadcast_to(own, (size,) + own.shape), "samp")
    return got.reshape((-1,) + own.shape[1:])


def all_sum(value):
    size = lax.axis_size("samp") * lax.axis_size("chrom")
    return jnp.sum(exchange(jnp.broadcast_to(value, (size,) + value.shape), ("samp", "chrom")), axis=0)


def body(dosages, traits, start_coef, groups, tested, owners):
    n_samp = lax.axis_size("samp")
    rows_dev = dosages.shape[0]
    total_rows = rows_dev * n_samp
    penalty = 1.5 * math.sqrt(traits.shape[1] / total_rows)
    my_samp, my_chrom = lax.axis_index("samp"), lax.axis_index("chrom")
    core = my_chrom % 2
    group_base = my_chrom * GPD

    coefficients = start_coef
    group_masks = [(groups - group_base == which).astype(jnp.float32)[:, None] for which in range(GPD)]
    for iteration in range(ITERS):
        prediction = chrom_gather(chrom_scatter(matmul(dosages, coefficients), core), core)
        residual_now = traits - prediction
        own_grad = samp_scatter(inner_rows(dosages, residual_now)) / total_rows
        gradient = samp_gather(own_grad)
        grad_sq = jnp.sum(own_grad * own_grad)
        image_part = chrom_scatter(matmul(dosages, gradient), core)
        image_sq = jnp.sum(image_part * image_part)
        sums = all_sum(jnp.stack([jnp.full((128,), grad_sq), jnp.full((128,), image_sq)]))
        grad_sq, image_sq = sums[0, 0], sums[1, 0]
        step_size = grad_sq / (image_sq / total_rows + 1e-06)
        moved_rows = coefficients + step_size * gradient
        length = jnp.sqrt(jnp.sum(moved_rows * moved_rows, axis=1, keepdims=True))
        coefficients = moved_rows * (
            jnp.maximum(length - step_size * penalty, 0.0)
            / jnp.maximum(length, step_size * penalty)
        )
    residual = traits - chrom_gather(chrom_scatter(matmul(dosages, coefficients), core), core)
    own_parts = [matmul(dosages, coefficients * mask) for mask in group_masks]
    tested_sq = jnp.sum(jnp.square(tested.astype(jnp.float32)), axis=0)
    picked = jnp.zeros((tested.shape[1], traits.shape[1]), jnp.float32)
    loco_list = []
    chosen_list = []
    for which in range(GPD):
        loco_resid = residual + own_parts[which]
        loco_list.append(jnp.sum(loco_resid * loco_resid, axis=0))
        products = lax.dot_general(
            tested,
            loco_resid.astype(jnp.bfloat16),
            (((0,), (0,)), ((), ())),
            preferred_element_type=jnp.float32,
        )
        chosen = (owners - group_base == which).astype(jnp.float32)[:, None]
        chosen_list.append(chosen)
        picked = picked + chosen * products
    picked = samp_scatter(picked)
    block = picked.shape[0]
    sums = jnp.concatenate([tested_sq.reshape(n_samp, -1), jnp.tile(jnp.concatenate(loco_list)[None], (n_samp, 1))], axis=1)
    sums = jnp.sum(exchange(sums, "samp"), axis=0)
    tested_sq, loco_all = sums[:block], sums[block:].reshape(GPD, -1)
    loco_pick = jnp.zeros_like(picked)
    for which in range(GPD):
        mine = lax.dynamic_slice_in_dim(chosen_list[which], my_samp * block, block, 0)
        loco_pick = loco_pick + mine * loco_all[which][None, :]
    denom = math.sqrt(total_rows) * jnp.sqrt(
        (tested_sq[:, None] / total_rows + 1e-06) * (loco_pick / total_rows + 1e-06)
    )
    return (samp_gather(picked / denom), residual)


def solution(mesh):
    placed = (
        P("samp", "chrom"),
        P("samp", None),
        P("chrom", None),
        P("chrom"),
        P("samp", "chrom"),
        P("chrom"),
    )
    return jax.shard_map(
        body,
        mesh=mesh,
        in_specs=placed,
        out_specs=(P("chrom", None), P("samp", None)),
        check_vma=False,
    )
```

```python
import functools
import math

import jax
import jax.numpy as jnp
from jax import lax
from jax.experimental import pallas as pl
from jax.experimental.pallas import tpu as pltpu
from jax.sharding import PartitionSpec as P

GPD = 2
ITERS = 2
STATS = 16
VMEM_LIMIT = 24 * 1024 * 1024


def swap(value, axis, bits):
    size = lax.axis_size(axis)
    return lax.ppermute(value, axis, [(i, i ^ bits) for i in range(size)])


def split(value):
    high = value.astype(jnp.bfloat16)
    low = (value - high.astype(jnp.float32)).astype(jnp.bfloat16)
    return high, low


def pack(value):
    return jnp.concatenate(split(value), axis=1)


def wide_dot(high, low, packed):
    total = jnp.dot(high, packed, preferred_element_type=jnp.float32)
    total = total + jnp.dot(low, packed, preferred_element_type=jnp.float32)
    traits = packed.shape[1] // 2
    return total[:, :traits] + total[:, traits:]


def whole():
    return pl.BlockSpec(memory_space=pltpu.VMEM)


def shape(dims, dtype=jnp.float32):
    return jax.ShapeDtypeStruct(dims, dtype)


def call(kernel, outs, scratch=(), flops=0, moved=0):
    def run(*operands):
        return pl.pallas_call(
            kernel,
            out_shape=outs,
            in_specs=[whole()] * len(operands),
            out_specs=jax.tree.map(lambda _: whole(), outs),
            scratch_shapes=list(scratch),
            compiler_params=pltpu.CompilerParams(vmem_limit_bytes=VMEM_LIMIT),
            cost_estimate=pl.CostEstimate(flops=flops, bytes_accessed=moved, transcendentals=0),
        )(*operands)

    return run


def halves(parts, bits):
    me = lax.axis_index("chrom")
    place, core = me // 2, me % 2
    half = parts.shape[0]
    return [parts.at[place ^ k, core ^ bits] for k in range(half)]


def store_prediction(high_ref, low_ref, packed, give_ref, keep_ref):
    for bits, out in ((1, give_ref), (0, keep_ref)):
        high = jnp.concatenate([block[...] for block in halves(high_ref, bits)])
        low = jnp.concatenate([block[...] for block in halves(low_ref, bits)])
        out[...] = wide_dot(high, low, packed).reshape(out.shape)


def first_kernel(dosage_ref, coef_ref, high_ref, low_ref, give_ref, keep_ref, packed_ref):
    step = pl.program_id(0)
    place = lax.axis_index("chrom") // 2

    @pl.when(step == 0)
    def _():
        packed_ref[...] = pack(coef_ref[...])

    highs, lows = [], []
    for k in range(dosage_ref.shape[0]):
        high, low = split(dosage_ref[place ^ k, 0])
        high_ref[place ^ k, 0] = high
        low_ref[place ^ k, 0] = low
        highs.append(high)
        lows.append(low)
    total = wide_dot(jnp.concatenate(highs), jnp.concatenate(lows), packed_ref[...])

    @pl.when(step == 0)
    def _():
        give_ref[...] = total.reshape(give_ref.shape)

    @pl.when(step == 1)
    def _():
        keep_ref[...] = total.reshape(keep_ref.shape)


def first_prediction(dosages, coefficients):
    half, _, block, cols = dosages.shape
    traits = coefficients.shape[1]

    def rows(step, core_ref):
        return (0, 1 - step + core_ref[0] * (2 * step - 1), 0, 0)

    core = (lax.axis_index("chrom") % 2).astype(jnp.int32).reshape(1)
    part = pl.BlockSpec((half, 1, block, cols), rows)
    fixed = pl.BlockSpec((half, block, traits), lambda step, core_ref: (0, 0, 0))

    def kernel(core_ref, *refs):
        first_kernel(*refs)

    return pl.pallas_call(
        kernel,
        grid_spec=pltpu.PrefetchScalarGridSpec(
            num_scalar_prefetch=1,
            grid=(2,),
            in_specs=[part, pl.BlockSpec(coefficients.shape, lambda step, core_ref: (0, 0))],
            out_specs=[part, part, fixed, fixed],
            scratch_shapes=[pltpu.VMEM((cols, 2 * traits), jnp.bfloat16)],
        ),
        out_shape=[
            shape(dosages.shape, jnp.bfloat16),
            shape(dosages.shape, jnp.bfloat16),
            shape((half, block, traits)),
            shape((half, block, traits)),
        ],
        compiler_params=pltpu.CompilerParams(vmem_limit_bytes=VMEM_LIMIT),
    )(core, dosages, coefficients)


def turn_kernel(high_ref, low_ref, high_out, low_out):
    high_out[...] = high_ref[...].T
    low_out[...] = low_ref[...].T


def turned(high, low, blocks):
    rows, cols = high.shape
    width = cols // blocks
    return pl.pallas_call(
        turn_kernel,
        grid=(blocks,),
        in_specs=[pl.BlockSpec((rows, width), lambda step: (0, step))] * 2,
        out_specs=[pl.BlockSpec((width, rows), lambda step: (step, 0))] * 2,
        out_shape=[shape((cols, rows), jnp.bfloat16)] * 2,
        compiler_params=pltpu.CompilerParams(vmem_limit_bytes=VMEM_LIMIT),
        cost_estimate=pl.CostEstimate(flops=0, bytes_accessed=16 * rows * cols, transcendentals=0),
    )(high, low)


def tested_kernel(tested_ref, turned_ref, square_ref):
    value = tested_ref[...]
    turned_ref[...] = value.T
    wide = value.astype(jnp.float32)
    square_ref[0] = jnp.sum(wide * wide, axis=0).reshape(square_ref.shape[1:])


def tested_parts(tested, blocks):
    rows, cols = tested.shape
    width = cols // blocks
    return pl.pallas_call(
        tested_kernel,
        grid=(blocks,),
        in_specs=[pl.BlockSpec((rows, width), lambda step: (0, step))],
        out_specs=[
            pl.BlockSpec((width, rows), lambda step: (step, 0)),
            pl.BlockSpec((1, width // 128, 128), lambda step: (step, 0, 0)),
        ],
        out_shape=[shape((cols, rows), jnp.bfloat16), shape((blocks, width // 128, 128))],
        compiler_params=pltpu.CompilerParams(vmem_limit_bytes=VMEM_LIMIT),
        cost_estimate=pl.CostEstimate(flops=0, bytes_accessed=8 * rows * cols, transcendentals=0),
    )(tested)


def place_rows(pieces, store):
    me = lax.axis_index("chrom")
    for bits, piece in pieces.items():
        store((me ^ bits) * piece.shape[0], piece)


def residual_order(size):
    return list(range(size))


def grad_kernel(count, *refs):
    pieces, (high_ref, low_ref), outs, packed_ref = (
        refs[:count],
        refs[count : count + 2],
        refs[count + 2 : -1],
        refs[-1],
    )
    me, samp = lax.axis_index("chrom"), lax.axis_index("samp")
    block = pieces[0].shape[0]
    for bits, piece in enumerate(pieces):
        start = pl.multiple_of((me ^ bits) * block, block)
        packed_ref[pl.ds(start, block)] = pack(piece[...])
    packed = packed_ref[...]
    for bits in reversed(range(len(outs))):
        outs[bits][...] = wide_dot(high_ref[samp ^ bits], low_ref[samp ^ bits], packed)


def image_kernel(count, *refs):
    pieces = refs[:count]
    high_ref, low_ref, grad_ref, give_ref, keep_ref, packed_ref = refs[count:]
    samp = lax.axis_index("samp")
    block = pieces[0].shape[0]
    for bits, piece in enumerate(pieces):
        start = pl.multiple_of((samp ^ bits) * block, block)
        value = piece[...]
        grad_ref[pl.ds(start, block)] = value
        packed_ref[pl.ds(start, block)] = pack(value)
    store_prediction(high_ref, low_ref, packed_ref[...], give_ref, keep_ref)


def prox_kernel(total_rows, coef_ref, grad_ref, sums_ref, high_ref, low_ref, new_ref, give_ref, keep_ref):
    sums = jnp.sum(sums_ref[...], axis=0)
    grad_sq = jnp.sum(sums[0:1], axis=1, keepdims=True)
    image_sq = jnp.sum(sums[1:2], axis=1, keepdims=True)
    step_size = grad_sq / (image_sq / total_rows + 1e-06)
    penalty = 1.5 * math.sqrt(coef_ref.shape[1] / total_rows)
    moved = coef_ref[...] + step_size * grad_ref[...]
    length = jnp.sqrt(jnp.sum(moved * moved, axis=1, keepdims=True))
    cut = step_size * penalty
    new = moved * (jnp.maximum(length - cut, 0.0) / jnp.maximum(length, cut))
    new_ref[...] = new
    store_prediction(high_ref, low_ref, pack(new), give_ref, keep_ref)


def own_kernel(coef_ref, mask_ref, high_ref, low_ref, *outs):
    high, low = high_ref[...], low_ref[...]
    coef = coef_ref[...]
    mask = mask_ref[...]
    for which, out in enumerate(outs):
        out[...] = wide_dot(high, low, pack(jnp.where(mask == which, coef, 0.0)))


def loco_kernel(count, *refs):
    pieces = refs[:count]
    own_refs = refs[count : count + GPD]
    tested_ref, square_ref, pick_ref, residual_ref = refs[count + GPD : count + GPD + 4]
    outs, loco_ref = refs[count + GPD + 4 : -1], refs[-1]
    me, samp = lax.axis_index("chrom"), lax.axis_index("samp")
    block, traits = pieces[0].shape
    squares = [jnp.zeros((1, traits), jnp.float32)] * GPD
    for bits, piece in enumerate(pieces):
        rows = pl.ds(pl.multiple_of((me ^ bits) * block, block), block)
        value = piece[...]
        residual_ref[rows] = value
        for which in range(GPD):
            loco = value + own_refs[which][rows]
            squares[which] = squares[which] + jnp.sum(loco * loco, axis=0, keepdims=True)
            loco_ref[rows, which * traits : (which + 1) * traits] = loco.astype(jnp.bfloat16)
    loco = loco_ref[...]
    for bits in reversed(range(len(outs))):
        other, out = samp ^ bits, outs[bits]
        cols = tested_ref.shape[1]
        products = jnp.dot(tested_ref[other], loco, preferred_element_type=jnp.float32)
        pick = pick_ref[other]
        chosen = products[:, :traits]
        for which in range(1, GPD):
            chosen = jnp.where(pick == which, products[:, which * traits : (which + 1) * traits], chosen)
        out[0:cols] = chosen
        out[cols : cols + STATS] = jnp.zeros((STATS, traits), jnp.float32)
        for which in range(GPD):
            out[cols + which : cols + which + 1] = squares[which]
        out[cols + 8 : cols + 8 + square_ref.shape[1]] = square_ref[other]


def score_kernel(total_rows, pick_ref, *refs):
    pieces, out = refs[:-1], refs[-1]
    total = pieces[0][...]
    for piece in pieces[1:]:
        total = total + piece[...]
    cols, traits = out.shape
    pick = pick_ref[lax.axis_index("samp")]
    loco_sq = jnp.broadcast_to(total[cols : cols + 1], (cols, traits))
    for which in range(1, GPD):
        loco_sq = jnp.where(pick == which, total[cols + which : cols + which + 1], loco_sq)
    diagonal = lax.broadcasted_iota(jnp.int32, (128, 128), 0) == lax.broadcasted_iota(jnp.int32, (128, 128), 1)
    columns = []
    for row in range(cols // 128):
        squares = total[cols + 8 + row : cols + 9 + row, :128]
        columns.append(jnp.sum(jnp.where(diagonal, squares, 0.0), axis=1, keepdims=True))
    tested_sq = jnp.concatenate(columns)
    denom = math.sqrt(total_rows) * jnp.sqrt((tested_sq / total_rows + 1e-06) * (loco_sq / total_rows + 1e-06))
    out[...] = total[:cols] / denom


def place_kernel(*refs):
    pieces, out = refs[:-1], refs[-1]
    samp = lax.axis_index("samp")
    block = pieces[0].shape[0]
    for bits, piece in enumerate(pieces):
        out[pl.ds(pl.multiple_of((samp ^ bits) * block, block), block)] = piece[...]


def chrom_scatter(give, keep):
    got = swap(give, "chrom", 1)
    count = keep.shape[0]
    sums = [keep[k] + got[k] for k in range(count)]
    total = sums[0]
    for block in [swap(sums[k], "chrom", 2 * k) for k in reversed(range(1, count))]:
        total = total + block
    return total


def chrom_gather(own):
    size = lax.axis_size("chrom")
    mine = [own] + [swap(own, "chrom", 2 * k) for k in range(1, size // 2)]
    other = [swap(block, "chrom", 1) for block in mine]
    return [block for pair in zip(mine, other) for block in pair]


def samp_swaps(pieces):
    return [swap(pieces[k], "samp", k) for k in reversed(range(1, len(pieces)))]


def body(dosages, traits, start_coef, groups, tested, owners):
    n_samp, n_chrom = lax.axis_size("samp"), lax.axis_size("chrom")
    rows, cols = dosages.shape
    tests, n_traits = tested.shape[1], traits.shape[1]
    total_rows = rows * n_samp
    me, samp = lax.axis_index("chrom"), lax.axis_index("samp")
    half, block, width, test_width = n_chrom // 2, rows // n_chrom, cols // n_samp, tests // n_samp
    flops = 2 * rows * cols * 4 * n_traits
    moved = 4 * rows * cols
    half_shape = shape((half, block, n_traits))
    packed = pltpu.VMEM((cols, 2 * n_traits), jnp.bfloat16)

    mask = jnp.broadcast_to((groups - me * GPD)[:, None], (cols, n_traits))
    pick = jnp.broadcast_to((owners - me * GPD)[:, None], (tests, n_traits)).reshape(n_samp, test_width, n_traits)
    own_traits = lax.dynamic_slice_in_dim(traits, me * block, block, 0)

    coefficients = start_coef
    high4, low4, give, keep = first_prediction(dosages.reshape(half, 2, block, cols), coefficients)
    high, low = high4.reshape(rows, cols), low4.reshape(rows, cols)
    turn_high, turn_low = turned(high, low, n_samp)
    turn_high, turn_low = (part.reshape(n_samp, width, rows) for part in (turn_high, turn_low))
    turn_tested, tested_sq = tested_parts(tested, n_samp)
    turn_tested = turn_tested.reshape(n_samp, test_width, rows)

    grad_call = call(
        functools.partial(grad_kernel, n_chrom),
        [shape((width, n_traits))] * n_samp,
        [pltpu.VMEM((rows, 2 * n_traits), jnp.bfloat16)],
        flops,
        moved,
    )
    image_call = call(
        functools.partial(image_kernel, n_samp),
        [shape((cols, n_traits)), half_shape, half_shape],
        [packed],
        flops,
        moved,
    )
    prox_call = call(
        functools.partial(prox_kernel, total_rows),
        [shape((cols, n_traits)), half_shape, half_shape],
        (),
        flops,
        moved,
    )
    for iteration in range(ITERS):
        pieces = chrom_gather(own_traits - chrom_scatter(give, keep))
        pieces = grad_call(*pieces, turn_high, turn_low)
        own_grad = pieces[0]
        for piece in samp_swaps(pieces):
            own_grad = own_grad + piece
        own_grad = own_grad / total_rows
        pieces = [own_grad] + [swap(own_grad, "samp", k) for k in range(1, n_samp)]
        gradient, give, keep = image_call(*pieces, high4, low4)
        image = chrom_scatter(give, keep)
        sums = jnp.stack([jnp.sum(own_grad * own_grad, axis=0), jnp.sum(image * image, axis=0)])
        size = n_samp * n_chrom
        sums = lax.all_to_all(jnp.broadcast_to(sums, (size,) + sums.shape), ("samp", "chrom"), 0, 0)
        coefficients, give, keep = prox_call(coefficients, gradient, sums, high4, low4)
    own_parts = call(own_kernel, [shape((rows, n_traits))] * GPD, (), GPD * flops, moved)(
        coefficients, mask, high, low
    )
    pieces = chrom_gather(own_traits - chrom_scatter(give, keep))
    residual, *pieces = call(
        functools.partial(loco_kernel, n_chrom),
        [shape((rows, n_traits))] + [shape((test_width + STATS, n_traits))] * n_samp,
        [pltpu.VMEM((rows, GPD * n_traits), jnp.bfloat16)],
        flops,
        moved,
    )(*pieces, *own_parts, turn_tested, tested_sq, pick)
    own_scores = call(functools.partial(score_kernel, total_rows), shape((test_width, n_traits)))(
        pick, pieces[0], *samp_swaps(pieces)
    )
    scores = call(place_kernel, shape((tests, n_traits)))(
        own_scores, *[swap(own_scores, "samp", k) for k in range(1, n_samp)]
    )
    return (scores, residual)


def solution(mesh):
    placed = (
        P("samp", "chrom"),
        P("samp", None),
        P("chrom", None),
        P("chrom"),
        P("samp", "chrom"),
        P("chrom"),
    )
    return jax.shard_map(
        body,
        mesh=mesh,
        in_specs=placed,
        out_specs=(P("chrom", None), P("samp", None)),
        check_vma=False,
    )
```

```python
import functools
import math

import jax
import jax.numpy as jnp
from jax import lax
from jax.experimental import pallas as pl
from jax.experimental.pallas import tpu as pltpu
from jax.sharding import PartitionSpec as P

GPD = 2
ITERS = 2
STATS = 16
VMEM_LIMIT = 14 * 1024 * 1024
FIRST_LIMIT = 60 * 1024 * 1024


def swap(value, axis, bits):
    size = lax.axis_size(axis)
    return lax.ppermute(value, axis, [(i, i ^ bits) for i in range(size)])


def split(value):
    high = value.astype(jnp.bfloat16)
    low = (value - high.astype(jnp.float32)).astype(jnp.bfloat16)
    return high, low


def pack(value):
    return jnp.concatenate(split(value), axis=1)


def wide_dot(high, low, packed):
    total = jnp.dot(high, packed, preferred_element_type=jnp.float32)
    total = total + jnp.dot(low, packed, preferred_element_type=jnp.float32)
    traits = packed.shape[1] // 2
    return total[:, :traits] + total[:, traits:]


def whole():
    return pl.BlockSpec(memory_space=pltpu.VMEM)


def anywhere():
    return pl.BlockSpec(memory_space=pl.ANY)


def shape(dims, dtype=jnp.float32):
    return jax.ShapeDtypeStruct(dims, dtype)


def call(kernel, outs, specs, scratch=(), flops=0, moved=0, limit=VMEM_LIMIT):
    return pl.pallas_call(
        kernel,
        out_shape=outs,
        in_specs=specs,
        out_specs=jax.tree.map(lambda _: whole(), outs),
        scratch_shapes=list(scratch),
        compiler_params=pltpu.CompilerParams(vmem_limit_bytes=limit),
        cost_estimate=pl.CostEstimate(flops=flops, bytes_accessed=moved, transcendentals=0),
    )


def first_kernel(bits, dosage_ref, coef_ref, high_ref, low_ref, out_ref, *rest):
    *packed_out, buffer_ref, sems = rest
    me = lax.axis_index("chrom")
    place, core = me // 2, me % 2
    half, block = buffer_ref.shape[0], buffer_ref.shape[1]
    copies = [
        pltpu.make_async_copy(dosage_ref.at[place ^ k, core ^ bits], buffer_ref.at[k], sems.at[k]) for k in range(half)
    ]
    for copy in copies:
        copy.start()
    if packed_out:
        packed_out[0][...] = pack(coef_ref[...])
        packed = packed_out[0][...]
    else:
        packed = coef_ref[...]
    for k, copy in enumerate(copies):
        copy.wait()
        high, low = split(buffer_ref[k])
        high_ref[k * block : (k + 1) * block] = high
        low_ref[k * block : (k + 1) * block] = low
    out_ref[...] = wide_dot(high_ref[...], low_ref[...], packed).reshape(out_ref.shape)


def turn_kernel(count, *refs):
    for source, target in zip(refs[:count], refs[-count:]):
        target[0] = source[...].T


def turned(parts, blocks, after):
    rows, cols = parts[0].shape
    width = cols // blocks
    return pl.pallas_call(
        functools.partial(turn_kernel, len(parts)),
        grid=(blocks,),
        in_specs=[pl.BlockSpec((rows, width), lambda step: (0, step))] * len(parts) + [anywhere()],
        out_specs=[pl.BlockSpec((1, width, rows), lambda step: (step, 0, 0))] * len(parts),
        out_shape=[shape((blocks, width, rows), jnp.bfloat16)] * len(parts),
        compiler_params=pltpu.CompilerParams(vmem_limit_bytes=VMEM_LIMIT),
        cost_estimate=pl.CostEstimate(flops=0, bytes_accessed=8 * rows * cols * len(parts), transcendentals=0),
    )(*parts, after)


def tested_kernel(tested_ref, turned_ref, square_ref):
    value = tested_ref[...]
    turned_ref[0] = value.T
    wide = value.astype(jnp.float32)
    square_ref[0] = jnp.sum(wide * wide, axis=0).reshape(square_ref.shape[1:])


def tested_parts(tested, blocks):
    rows, cols = tested.shape
    width = cols // blocks
    return pl.pallas_call(
        tested_kernel,
        grid=(blocks,),
        in_specs=[pl.BlockSpec((rows, width), lambda step: (0, step))],
        out_specs=[
            pl.BlockSpec((1, width, rows), lambda step: (step, 0, 0)),
            pl.BlockSpec((1, width // 128, 128), lambda step: (step, 0, 0)),
        ],
        out_shape=[shape((blocks, width, rows), jnp.bfloat16), shape((blocks, width // 128, 128))],
        compiler_params=pltpu.CompilerParams(vmem_limit_bytes=VMEM_LIMIT),
        cost_estimate=pl.CostEstimate(flops=0, bytes_accessed=8 * rows * cols, transcendentals=0),
    )(tested)


def rest_kernel(high_ref, low_ref, packed_ref, out_ref):
    out_ref[...] = wide_dot(high_ref[...], low_ref[...], packed_ref[...]).reshape(out_ref.shape)


def residual_kernel(count, traits_ref, *refs):
    total = refs[0][...]
    for piece in refs[1:count]:
        total = total + piece[...]
    refs[-1][...] = traits_ref[...] - total


def grad_dot(turn_refs, packed_ref, which):
    half = packed_ref.shape[0] // 2
    own = wide_dot(turn_refs[0][which], turn_refs[1][which], packed_ref[0:half])
    return own + wide_dot(turn_refs[2][which], turn_refs[3][which], packed_ref[half:])


def grad_far_kernel(count, partners, *refs):
    pieces, turn_refs, (packed_ref, *outs) = refs[:count], refs[count : count + 4], refs[count + 4 :]
    samp = lax.axis_index("samp")
    block = pieces[0].shape[0]
    for bits, piece in enumerate(pieces):
        start = ((bits % 2) * (count // 2) + bits // 2) * block
        packed_ref[start : start + block] = pack(piece[...])
    for partner, out in zip(partners, outs):
        out[...] = grad_dot(turn_refs, packed_ref, samp ^ partner)


def grad_near_kernel(partners, *refs):
    packed_ref, turn_refs, outs = refs[0], refs[1:5], refs[5:]
    samp = lax.axis_index("samp")
    for partner, out in zip(partners, outs):
        out[...] = grad_dot(turn_refs, packed_ref, samp ^ partner)


def image_kernel(count, *refs):
    pieces = refs[:count]
    high_ref, low_ref = refs[count : count + 2]
    grad_ref, packed_ref, give_ref = refs[-3:]
    samp = lax.axis_index("samp")
    block = pieces[0].shape[0]
    for bits, piece in enumerate(pieces):
        rows = pl.ds(pl.multiple_of((samp ^ bits) * block, block), block)
        value = piece[...]
        grad_ref[rows] = value
        packed_ref[rows] = pack(value)
    rest_kernel(high_ref, low_ref, packed_ref, give_ref)


def norm_kernel(count, *refs):
    grad_ref, pieces, out = refs[0], refs[1 : count + 1], refs[-1]
    total = pieces[0][...]
    for piece in pieces[1:]:
        total = total + piece[...]
    grad = grad_ref[...]
    grad_sq = jnp.sum(grad * grad, axis=0, keepdims=True)
    image_sq = jnp.sum(total * total, axis=0, keepdims=True)
    row = lax.broadcasted_iota(jnp.int32, out.shape[1:], 0)
    sums = jnp.where(row == 0, grad_sq, jnp.where(row == 1, image_sq, 0.0))
    for place in range(out.shape[0]):
        out[place] = sums


def prox_kernel(total_rows, coef_ref, grad_ref, sums_ref, high_ref, low_ref, new_ref, packed_ref, give_ref):
    sums = sums_ref[0]
    for place in range(1, sums_ref.shape[0]):
        sums = sums + sums_ref[place]
    grad_sq = jnp.sum(sums[0:1], axis=1, keepdims=True)
    image_sq = jnp.sum(sums[1:2], axis=1, keepdims=True)
    step_size = grad_sq / (image_sq / total_rows + 1e-06)
    penalty = 1.5 * math.sqrt(coef_ref.shape[1] / total_rows)
    moved = coef_ref[...] + step_size * grad_ref[...]
    length = jnp.sqrt(jnp.sum(moved * moved, axis=1, keepdims=True))
    cut = step_size * penalty
    new = moved * (jnp.maximum(length - cut, 0.0) / jnp.maximum(length, cut))
    new_ref[...] = new
    packed_ref[...] = pack(new)
    rest_kernel(high_ref, low_ref, packed_ref, give_ref)


def own_kernel(coef_ref, mask_ref, *refs):
    parts, outs = refs[:4], refs[4:]
    coef = coef_ref[...]
    mask = mask_ref[...]
    half = parts[0].shape[0]
    for which, out in enumerate(outs):
        packed = pack(jnp.where(mask == which, coef, 0.0))
        out[0:half] = wide_dot(parts[0][...], parts[1][...], packed)
        out[half:] = wide_dot(parts[2][...], parts[3][...], packed)


def score_products(partner, out, tested_ref, square_ref, pick_ref, loco_ref, sums_ref):
    cols, traits = tested_ref.shape[1], out.shape[1]
    products = jnp.dot(tested_ref[partner], loco_ref[...], preferred_element_type=jnp.float32)
    pick = pick_ref[partner]
    chosen = products[:, :traits]
    for which in range(1, GPD):
        chosen = jnp.where(pick == which, products[:, which * traits : (which + 1) * traits], chosen)
    out[0:cols] = chosen
    out[cols : cols + 8] = sums_ref[...]
    out[cols + 8 : cols + STATS] = jnp.zeros((STATS - 8, traits), jnp.float32)
    out[cols + 8 : cols + 8 + square_ref.shape[1]] = square_ref[partner]


def loco_kernel(count, partners, *refs):
    pieces, own_refs = refs[:count], refs[count : count + GPD]
    tested_ref, square_ref, pick_ref, residual_ref, loco_ref, sums_ref = refs[count + GPD : count + GPD + 6]
    outs = refs[count + GPD + 6 :]
    me, samp = lax.axis_index("chrom"), lax.axis_index("samp")
    block, traits = pieces[0].shape
    sums_ref[...] = jnp.zeros_like(sums_ref)
    for bits, piece in enumerate(pieces):
        rows = pl.ds(pl.multiple_of((me ^ bits) * block, block), block)
        start = ((bits % 2) * (count // 2) + bits // 2) * block
        value = piece[...]
        residual_ref[rows] = value
        for which in range(GPD):
            loco = value + own_refs[which][start : start + block]
            sums_ref[which : which + 1] += jnp.sum(loco * loco, axis=0, keepdims=True)
            loco_ref[rows, which * traits : (which + 1) * traits] = loco.astype(jnp.bfloat16)
    for partner, out in zip(partners, outs):
        score_products(samp ^ partner, out, tested_ref, square_ref, pick_ref, loco_ref, sums_ref)


def loco_near_kernel(partners, *refs):
    samp = lax.axis_index("samp")
    for partner, out in zip(partners, refs[5:]):
        score_products(samp ^ partner, out, *refs[:5])


def score_kernel(total_rows, pick_ref, *refs):
    pieces, out = refs[:-1], refs[-1]
    total = pieces[0][...]
    for piece in pieces[1:]:
        total = total + piece[...]
    cols, traits = out.shape
    pick = pick_ref[lax.axis_index("samp")]
    loco_sq = jnp.broadcast_to(total[cols : cols + 1], (cols, traits))
    for which in range(1, GPD):
        loco_sq = jnp.where(pick == which, total[cols + which : cols + which + 1], loco_sq)
    diagonal = lax.broadcasted_iota(jnp.int32, (128, 128), 0) == lax.broadcasted_iota(jnp.int32, (128, 128), 1)
    columns = []
    for row in range(cols // 128):
        squares = total[cols + 8 + row : cols + 9 + row, :128]
        columns.append(jnp.sum(jnp.where(diagonal, squares, 0.0), axis=1, keepdims=True))
    tested_sq = jnp.concatenate(columns)
    denom = math.sqrt(total_rows) * jnp.sqrt((tested_sq / total_rows + 1e-06) * (loco_sq / total_rows + 1e-06))
    out[...] = total[:cols] / denom


def place_kernel(*refs):
    pieces, out = refs[:-1], refs[-1]
    samp = lax.axis_index("samp")
    block = pieces[0].shape[0]
    for bits, piece in enumerate(pieces):
        out[pl.ds(pl.multiple_of((samp ^ bits) * block, block), block)] = piece[...]


def chrom_scatter(give, keep):
    got = swap(give, "chrom", 1)
    count = keep.shape[0]
    sums = [keep[k] + got[k] for k in range(count)]
    return [sums[0]] + [swap(sums[k], "chrom", 2 * k) for k in reversed(range(1, count))]


def chrom_gather(own):
    count = lax.axis_size("chrom") // 2
    far = [swap(own, "chrom", 2 * k) for k in reversed(range(1, count))]
    mine = [own] + far[::-1]
    other = [swap(block, "chrom", 1) for block in mine]
    return [block for pair in zip(mine, other) for block in pair]


def samp_order(size):
    return list(reversed(range(size)))


def samp_gather(own):
    size = lax.axis_size("samp")
    return [own] + [swap(own, "samp", k) for k in samp_order(size)[:-1]][::-1]


def body(dosages, traits, start_coef, groups, tested, owners):
    n_samp, n_chrom = lax.axis_size("samp"), lax.axis_size("chrom")
    rows, cols = dosages.shape
    tests, n_traits = tested.shape[1], traits.shape[1]
    total_rows = rows * n_samp
    me = lax.axis_index("chrom")
    half, block, width, test_width = n_chrom // 2, rows // n_chrom, cols // n_samp, tests // n_samp
    flops = 4 * rows * cols * n_traits
    moved = 2 * rows * cols
    order = samp_order(n_samp)
    far, near = order[: n_samp // 2], order[n_samp // 2 :]

    part = shape((rows // 2, cols), jnp.bfloat16)
    half_out = shape((half, block, n_traits))
    packed_cols = shape((cols, 2 * n_traits), jnp.bfloat16)
    packed_rows = shape((rows, 2 * n_traits), jnp.bfloat16)
    grad_block = shape((width, n_traits))
    score_block = shape((test_width + STATS, n_traits))
    coef_out = shape((cols, n_traits))
    buffers = [pltpu.VMEM((half, block, cols), jnp.float32), pltpu.SemaphoreType.DMA((half,))]

    mask = jnp.broadcast_to((groups - me * GPD)[:, None], (cols, n_traits))
    pick = jnp.broadcast_to((owners - me * GPD)[:, None], (tests, n_traits)).reshape(n_samp, test_width, n_traits)
    own_traits = lax.dynamic_slice_in_dim(traits, me * block, block, 0)

    def rest(high, low, packed):
        return call(rest_kernel, half_out, [whole()] * 3, (), flops, moved)(high, low, packed)

    def own_residual(summands, after=()):
        return call(
            functools.partial(residual_kernel, len(summands)),
            shape((block, n_traits)),
            [whole()] * (1 + len(summands)) + [anywhere()] * len(after),
        )(own_traits, *summands, *after)

    def first(bits, coefficients, outs):
        return call(
            functools.partial(first_kernel, bits),
            [part, part, half_out] + outs,
            [pl.BlockSpec(memory_space=pltpu.HBM), whole()],
            buffers,
            flops,
            2 * moved,
            FIRST_LIMIT,
        )(dosages.reshape(half, 2, block, cols), coefficients)

    coefficients = start_coef
    high1, low1, give, packed = first(1, coefficients, [packed_cols])
    high0, low0, keep = first(0, packed, [])
    summands = chrom_scatter(give, keep)
    turns = turned([high0, low0, high1, low1], n_samp, summands[0])
    turn_tested, tested_sq = tested_parts(tested, n_samp)

    for iteration in range(ITERS):
        own = own_residual(summands, turns if iteration == 0 else ())
        pieces = chrom_gather(own)
        packed, *far_out = call(
            functools.partial(grad_far_kernel, n_chrom, far),
            [packed_rows] + [grad_block] * len(far),
            [whole()] * (n_chrom + 4),
            (),
            flops,
            moved,
        )(*pieces, *turns)
        near_out = call(
            functools.partial(grad_near_kernel, near), [grad_block] * len(near), [whole()] * 5, (), flops, moved
        )(packed, *turns)
        own_grad = near_out[-1]
        for partner, piece in zip(order, far_out + list(near_out[:-1])):
            own_grad = own_grad + swap(piece, "samp", partner)
        own_grad = own_grad / total_rows
        pieces = samp_gather(own_grad)
        after = (turn_tested, tested_sq, mask, pick) if iteration == 0 else ()
        gradient, packed, give = call(
            functools.partial(image_kernel, n_samp),
            [coef_out, packed_cols, half_out],
            [whole()] * (n_samp + 2) + [anywhere()] * len(after),
            (),
            flops,
            moved,
        )(*pieces, high1, low1, *after)
        summands = chrom_scatter(give, rest(high0, low0, packed))
        size = n_samp * n_chrom
        sums = call(
            functools.partial(norm_kernel, half), shape((size, 8, n_traits)), [whole()] * (half + 1)
        )(own_grad, *summands)
        sums = lax.all_to_all(sums, ("samp", "chrom"), 0, 0)
        coefficients, packed, give = call(
            functools.partial(prox_kernel, total_rows),
            [coef_out, packed_cols, half_out],
            [whole()] * 5,
            (),
            flops,
            moved,
        )(coefficients, gradient, sums, high1, low1)
        summands = chrom_scatter(give, rest(high0, low0, packed))

    own_parts = call(own_kernel, [shape((rows, n_traits))] * GPD, [whole()] * 6, (), 4 * flops, 4 * moved)(
        coefficients, mask, high0, low0, high1, low1
    )
    pieces = chrom_gather(own_residual(summands, own_parts))
    residual, loco, loco_sq, *far_out = call(
        functools.partial(loco_kernel, n_chrom, far),
        [shape((rows, n_traits)), shape((rows, GPD * n_traits), jnp.bfloat16), shape((8, n_traits))]
        + [score_block] * len(far),
        [whole()] * (n_chrom + GPD + 3),
        (),
        flops,
        moved,
    )(*pieces, *own_parts, turn_tested, tested_sq, pick)
    near_out = call(
        functools.partial(loco_near_kernel, near), [score_block] * len(near), [whole()] * 5, (), flops // 2, moved
    )(turn_tested, tested_sq, pick, loco, loco_sq)
    received = [swap(piece, "samp", partner) for partner, piece in zip(order, far_out + list(near_out[:-1]))]
    own_scores = call(
        functools.partial(score_kernel, total_rows), shape((test_width, n_traits)), [whole()] * (n_samp + 1)
    )(pick, near_out[-1], *received)
    scores = call(place_kernel, shape((tests, n_traits)), [whole()] * n_samp)(*samp_gather(own_scores))
    return (scores, residual)


def solution(mesh):
    placed = (
        P("samp", "chrom"),
        P("samp", None),
        P("chrom", None),
        P("chrom"),
        P("samp", "chrom"),
        P("chrom"),
    )
    return jax.shard_map(
        body,
        mesh=mesh,
        in_specs=placed,
        out_specs=(P("chrom", None), P("samp", None)),
        check_vma=False,
    )
```

```python
import functools
import math

import jax
import jax.numpy as jnp
from jax import lax
from jax.experimental import pallas as pl
from jax.experimental.pallas import tpu as pltpu
from jax.sharding import PartitionSpec as P

GPD = 2
ITERS = 2
STATS = 16
VMEM_LIMIT = 14 * 1024 * 1024


def swap(value, axis, bits):
    size = lax.axis_size(axis)
    return lax.ppermute(value, axis, [(i, i ^ bits) for i in range(size)])


def split(value):
    high = value.astype(jnp.bfloat16)
    low = (value - high.astype(jnp.float32)).astype(jnp.bfloat16)
    return high, low


def pack(value):
    return jnp.concatenate(split(value), axis=1)


def wide_dot(high, low, packed):
    total = jnp.dot(high, packed, preferred_element_type=jnp.float32)
    total = total + jnp.dot(low, packed, preferred_element_type=jnp.float32)
    traits = packed.shape[1] // 2
    return total[:, :traits] + total[:, traits:]


def whole():
    return pl.BlockSpec(memory_space=pltpu.VMEM)


def anywhere():
    return pl.BlockSpec(memory_space=pl.ANY)


def shape(dims, dtype=jnp.float32):
    return jax.ShapeDtypeStruct(dims, dtype)


def call(kernel, outs, specs, scratch=(), flops=0, moved=0):
    return pl.pallas_call(
        kernel,
        out_shape=outs,
        in_specs=specs,
        out_specs=jax.tree.map(lambda _: whole(), outs),
        scratch_shapes=list(scratch),
        compiler_params=pltpu.CompilerParams(vmem_limit_bytes=VMEM_LIMIT),
        cost_estimate=pl.CostEstimate(flops=flops, bytes_accessed=moved, transcendentals=0),
    )


def split_rows(source_ref, ready, packed_ref, high_ref, low_ref, out_ref):
    half, block = source_ref.shape[0], source_ref.shape[1]
    group = max(1, half // 2)
    for first in range(0, half, group):
        for k in range(first, first + group):
            ready(k)
            high, low = split(source_ref[k])
            high_ref[k * block : (k + 1) * block] = high
            low_ref[k * block : (k + 1) * block] = low
        rows = slice(first * block, (first + group) * block)
        total = wide_dot(high_ref[rows], low_ref[rows], packed_ref[...])
        out_ref[first : first + group] = total.reshape((group,) + out_ref.shape[1:])


def first_kernel(dosage_ref, coef_ref, high_ref, low_ref, out_ref, packed_ref, kept_ref, buffer_ref, coef_buffer, sems):
    me = lax.axis_index("chrom")
    place, core = me // 2, me % 2
    half = buffer_ref.shape[0]
    coef_copy = pltpu.make_async_copy(coef_ref, coef_buffer, sems.at[2 * half])
    copies = [
        pltpu.make_async_copy(dosage_ref.at[place ^ k, core ^ bits], target.at[k], sems.at[bits * half + k])
        for bits, target in ((1, buffer_ref), (0, kept_ref))
        for k in range(half)
    ]
    coef_copy.start()
    for copy in copies:
        copy.start()
    coef_copy.wait()
    packed_ref[...] = pack(coef_buffer[...])
    split_rows(buffer_ref, lambda k: copies[k].wait(), packed_ref, high_ref, low_ref, out_ref)
    for copy in copies[half:]:
        copy.wait()


def second_kernel(kept_ref, packed_ref, high_ref, low_ref, out_ref):
    split_rows(kept_ref, lambda k: None, packed_ref, high_ref, low_ref, out_ref)


def turn_kernel(count, *refs):
    for source, target in zip(refs[:count], refs[-count:]):
        target[0] = source[...].T


def turned(parts, blocks, after):
    rows, cols = parts[0].shape
    width = cols // blocks
    return pl.pallas_call(
        functools.partial(turn_kernel, len(parts)),
        grid=(blocks,),
        in_specs=[pl.BlockSpec((rows, width), lambda step: (0, step))] * len(parts) + [anywhere()],
        out_specs=[pl.BlockSpec((1, width, rows), lambda step: (step, 0, 0))] * len(parts),
        out_shape=[shape((blocks, width, rows), jnp.bfloat16)] * len(parts),
        compiler_params=pltpu.CompilerParams(vmem_limit_bytes=VMEM_LIMIT),
        cost_estimate=pl.CostEstimate(flops=0, bytes_accessed=8 * rows * cols * len(parts), transcendentals=0),
    )(*parts, after)


def tested_kernel(tested_ref, turned_ref, square_ref):
    value = tested_ref[...]
    turned_ref[0] = value.T
    wide = value.astype(jnp.float32)
    square_ref[0] = jnp.sum(wide * wide, axis=0).reshape(square_ref.shape[1:])


def tested_parts(tested, blocks):
    rows, cols = tested.shape
    width = cols // blocks
    return pl.pallas_call(
        tested_kernel,
        grid=(blocks,),
        in_specs=[pl.BlockSpec((rows, width), lambda step: (0, step))],
        out_specs=[
            pl.BlockSpec((1, width, rows), lambda step: (step, 0, 0)),
            pl.BlockSpec((1, width // 128, 128), lambda step: (step, 0, 0)),
        ],
        out_shape=[shape((blocks, width, rows), jnp.bfloat16), shape((blocks, width // 128, 128))],
        compiler_params=pltpu.CompilerParams(vmem_limit_bytes=VMEM_LIMIT),
        cost_estimate=pl.CostEstimate(flops=0, bytes_accessed=8 * rows * cols, transcendentals=0),
    )(tested)


def rest_kernel(high_ref, low_ref, packed_ref, out_ref):
    out_ref[...] = wide_dot(high_ref[...], low_ref[...], packed_ref[...]).reshape(out_ref.shape)


def residual_kernel(count, traits_ref, *refs):
    total = refs[0][...]
    for piece in refs[1:count]:
        total = total + piece[...]
    refs[-1][...] = traits_ref[...] - total


def grad_dot(turn_refs, packed_ref, which):
    half = packed_ref.shape[0] // 2
    own = wide_dot(turn_refs[0][which], turn_refs[1][which], packed_ref[0:half])
    return own + wide_dot(turn_refs[2][which], turn_refs[3][which], packed_ref[half:])


def grad_far_kernel(count, partners, *refs):
    pieces, turn_refs, (packed_ref, *outs) = refs[:count], refs[count : count + 4], refs[count + 4 :]
    samp = lax.axis_index("samp")
    block = pieces[0].shape[0]
    for bits, piece in enumerate(pieces):
        start = ((bits % 2) * (count // 2) + bits // 2) * block
        packed_ref[start : start + block] = pack(piece[...])
    for partner, out in zip(partners, outs):
        out[...] = grad_dot(turn_refs, packed_ref, samp ^ partner)


def grad_near_kernel(partners, *refs):
    packed_ref, turn_refs, outs = refs[0], refs[1:5], refs[5:]
    samp = lax.axis_index("samp")
    for partner, out in zip(partners, outs):
        out[...] = grad_dot(turn_refs, packed_ref, samp ^ partner)


def image_kernel(count, *refs):
    pieces = refs[:count]
    high_ref, low_ref = refs[count : count + 2]
    grad_ref, packed_ref, give_ref = refs[-3:]
    samp = lax.axis_index("samp")
    block = pieces[0].shape[0]
    for bits, piece in enumerate(pieces):
        rows = pl.ds(pl.multiple_of((samp ^ bits) * block, block), block)
        value = piece[...]
        grad_ref[rows] = value
        packed_ref[rows] = pack(value)
    rest_kernel(high_ref, low_ref, packed_ref, give_ref)


def norm_kernel(count, *refs):
    grad_ref, pieces, out = refs[0], refs[1 : count + 1], refs[-1]
    total = pieces[0][...]
    for piece in pieces[1:]:
        total = total + piece[...]
    grad = grad_ref[...]
    grad_sq = jnp.sum(grad * grad, axis=0, keepdims=True)
    image_sq = jnp.sum(total * total, axis=0, keepdims=True)
    sums = jnp.concatenate([grad_sq, image_sq])
    for place in range(out.shape[0]):
        out[place] = sums


def prox_kernel(total_rows, coef_ref, grad_ref, sums_ref, high_ref, low_ref, new_ref, packed_ref, give_ref):
    sums = sums_ref[0]
    for place in range(1, sums_ref.shape[0]):
        sums = sums + sums_ref[place]
    grad_sq = jnp.sum(sums[0:1], axis=1, keepdims=True)
    image_sq = jnp.sum(sums[1:2], axis=1, keepdims=True)
    step_size = grad_sq / (image_sq / total_rows + 1e-06)
    penalty = 1.5 * math.sqrt(coef_ref.shape[1] / total_rows)
    moved = coef_ref[...] + step_size * grad_ref[...]
    length = jnp.sqrt(jnp.sum(moved * moved, axis=1, keepdims=True))
    cut = step_size * penalty
    new = moved * (jnp.maximum(length - cut, 0.0) / jnp.maximum(length, cut))
    new_ref[...] = new
    packed_ref[...] = pack(new)
    rest_kernel(high_ref, low_ref, packed_ref, give_ref)


def own_kernel(coef_ref, mask_ref, *refs):
    parts, outs = refs[:4], refs[4:]
    coef = coef_ref[...]
    mask = mask_ref[...]
    half = parts[0].shape[0]
    for which, out in enumerate(outs):
        packed = pack(jnp.where(mask == which, coef, 0.0))
        out[0:half] = wide_dot(parts[0][...], parts[1][...], packed)
        out[half:] = wide_dot(parts[2][...], parts[3][...], packed)


def score_products(partner, out, tested_ref, square_ref, pick_ref, loco_ref, sums_ref):
    cols, traits = tested_ref.shape[1], out.shape[1]
    products = jnp.dot(tested_ref[partner], loco_ref[...], preferred_element_type=jnp.float32)
    pick = pick_ref[partner]
    chosen = products[:, :traits]
    for which in range(1, GPD):
        chosen = jnp.where(pick == which, products[:, which * traits : (which + 1) * traits], chosen)
    out[0:cols] = chosen
    out[cols : cols + 8] = sums_ref[...]
    out[cols + 8 : cols + STATS] = jnp.zeros((STATS - 8, traits), jnp.float32)
    out[cols + 8 : cols + 8 + square_ref.shape[1]] = square_ref[partner]


def loco_kernel(count, partners, *refs):
    pieces, own_refs = refs[:count], refs[count : count + GPD]
    tested_ref, square_ref, pick_ref, residual_ref, loco_ref, sums_ref = refs[count + GPD : count + GPD + 6]
    outs = refs[count + GPD + 6 :]
    me, samp = lax.axis_index("chrom"), lax.axis_index("samp")
    block, traits = pieces[0].shape
    sums_ref[...] = jnp.zeros_like(sums_ref)
    for bits, piece in enumerate(pieces):
        rows = pl.ds(pl.multiple_of((me ^ bits) * block, block), block)
        start = ((bits % 2) * (count // 2) + bits // 2) * block
        value = piece[...]
        residual_ref[rows] = value
        for which in range(GPD):
            loco = value + own_refs[which][start : start + block]
            sums_ref[which : which + 1] += jnp.sum(loco * loco, axis=0, keepdims=True)
            loco_ref[rows, which * traits : (which + 1) * traits] = loco.astype(jnp.bfloat16)
    for partner, out in zip(partners, outs):
        score_products(samp ^ partner, out, tested_ref, square_ref, pick_ref, loco_ref, sums_ref)


def loco_near_kernel(partners, *refs):
    samp = lax.axis_index("samp")
    for partner, out in zip(partners, refs[5:]):
        score_products(samp ^ partner, out, *refs[:5])


def score_kernel(total_rows, pick_ref, *refs):
    pieces, out = refs[:-1], refs[-1]
    total = pieces[0][...]
    for piece in pieces[1:]:
        total = total + piece[...]
    cols, traits = out.shape
    pick = pick_ref[lax.axis_index("samp")]
    loco_sq = jnp.broadcast_to(total[cols : cols + 1], (cols, traits))
    for which in range(1, GPD):
        loco_sq = jnp.where(pick == which, total[cols + which : cols + which + 1], loco_sq)
    diagonal = lax.broadcasted_iota(jnp.int32, (128, 128), 0) == lax.broadcasted_iota(jnp.int32, (128, 128), 1)
    columns = []
    for row in range(cols // 128):
        squares = total[cols + 8 + row : cols + 9 + row, :128]
        columns.append(jnp.sum(jnp.where(diagonal, squares, 0.0), axis=1, keepdims=True))
    tested_sq = jnp.concatenate(columns)
    denom = math.sqrt(total_rows) * jnp.sqrt((tested_sq / total_rows + 1e-06) * (loco_sq / total_rows + 1e-06))
    out[...] = total[:cols] / denom


def place_kernel(*refs):
    pieces, out = refs[:-1], refs[-1]
    samp = lax.axis_index("samp")
    block = pieces[0].shape[0]
    for bits, piece in enumerate(pieces):
        out[pl.ds(pl.multiple_of((samp ^ bits) * block, block), block)] = piece[...]


def chrom_scatter(give, keep):
    got = swap(give, "chrom", 1)
    count = keep.shape[0]
    sums = [keep[k] + got[k] for k in range(count)]
    return [sums[0]] + [swap(sums[k], "chrom", 2 * k) for k in reversed(range(1, count))]


def chrom_gather(own):
    count = lax.axis_size("chrom") // 2
    far = [swap(own, "chrom", 2 * k) for k in reversed(range(1, count))]
    mine = [own] + far[::-1]
    other = [swap(block, "chrom", 1) for block in mine]
    return [block for pair in zip(mine, other) for block in pair]


def samp_order(size):
    return list(reversed(range(size)))


def samp_gather(own):
    size = lax.axis_size("samp")
    return [own] + [swap(own, "samp", k) for k in samp_order(size)[:-1]][::-1]


def body(dosages, traits, start_coef, groups, tested, owners):
    n_samp, n_chrom = lax.axis_size("samp"), lax.axis_size("chrom")
    rows, cols = dosages.shape
    tests, n_traits = tested.shape[1], traits.shape[1]
    total_rows = rows * n_samp
    me = lax.axis_index("chrom")
    half, block, width, test_width = n_chrom // 2, rows // n_chrom, cols // n_samp, tests // n_samp
    flops = 4 * rows * cols * n_traits
    moved = 2 * rows * cols
    order = samp_order(n_samp)
    far, near = order[:-1], order[-1:]

    part = shape((rows // 2, cols), jnp.bfloat16)
    half_out = shape((half, block, n_traits))
    packed_cols = shape((cols, 2 * n_traits), jnp.bfloat16)
    packed_rows = shape((rows, 2 * n_traits), jnp.bfloat16)
    grad_block = shape((width, n_traits))
    score_block = shape((test_width + STATS, n_traits))
    coef_out = shape((cols, n_traits))
    mask = jnp.broadcast_to((groups - me * GPD)[:, None], (cols, n_traits))
    pick = jnp.broadcast_to((owners - me * GPD)[:, None], (tests, n_traits)).reshape(n_samp, test_width, n_traits)
    own_traits = lax.dynamic_slice_in_dim(traits, me * block, block, 0)

    def rest(high, low, packed):
        return call(rest_kernel, half_out, [whole()] * 3, (), flops, moved)(high, low, packed)

    def own_residual(summands, after=()):
        return call(
            functools.partial(residual_kernel, len(summands)),
            shape((block, n_traits)),
            [whole()] * (1 + len(summands)) + [anywhere()] * len(after),
        )(own_traits, *summands, *after)

    coefficients = start_coef
    kept_shape = (half, block, cols)
    high1, low1, give, packed, kept = call(
        first_kernel,
        [part, part, half_out, packed_cols, shape(kept_shape)],
        [pl.BlockSpec(memory_space=pltpu.HBM)] * 2,
        [pltpu.VMEM(kept_shape, jnp.float32), pltpu.VMEM(coefficients.shape, jnp.float32), pltpu.SemaphoreType.DMA((n_chrom + 1,))],
        flops,
        4 * moved,
    )(
        pltpu.with_memory_space_constraint(dosages.reshape(half, 2, block, cols), pltpu.HBM),
        pltpu.with_memory_space_constraint(coefficients, pltpu.HBM),
    )
    high0, low0, keep = call(second_kernel, [part, part, half_out], [whole()] * 2, (), flops, moved)(kept, packed)
    summands = chrom_scatter(give, keep)
    turns = turned([high0, low0, high1, low1], n_samp, summands[0])
    turn_tested, tested_sq = tested_parts(tested, n_samp)

    for iteration in range(ITERS):
        own = own_residual(summands, turns if iteration == 0 else ())
        pieces = chrom_gather(own)
        packed, *far_out = call(
            functools.partial(grad_far_kernel, n_chrom, far),
            [packed_rows] + [grad_block] * len(far),
            [whole()] * (n_chrom + 4),
            (),
            flops,
            moved,
        )(*pieces, *turns)
        near_out = call(
            functools.partial(grad_near_kernel, near), [grad_block] * len(near), [whole()] * 5, (), flops, moved
        )(packed, *turns)
        own_grad = near_out[-1]
        for partner, piece in zip(order, far_out + list(near_out[:-1])):
            own_grad = own_grad + swap(piece, "samp", partner)
        own_grad = own_grad / total_rows
        pieces = samp_gather(own_grad)
        after = (turn_tested, tested_sq, mask, pick) if iteration == 0 else ()
        gradient, packed, give = call(
            functools.partial(image_kernel, n_samp),
            [coef_out, packed_cols, half_out],
            [whole()] * (n_samp + 2) + [anywhere()] * len(after),
            (),
            flops,
            moved,
        )(*pieces, high1, low1, *after)
        summands = chrom_scatter(give, rest(high0, low0, packed))
        size = n_samp * n_chrom
        sums = call(
            functools.partial(norm_kernel, half), shape((size, 2, n_traits)), [whole()] * (half + 1)
        )(own_grad, *summands)
        sums = lax.all_to_all(sums, ("samp", "chrom"), 0, 0)
        coefficients, packed, give = call(
            functools.partial(prox_kernel, total_rows),
            [coef_out, packed_cols, half_out],
            [whole()] * 5,
            (),
            flops,
            moved,
        )(coefficients, gradient, sums, high1, low1)
        summands = chrom_scatter(give, rest(high0, low0, packed))

    own_parts = call(own_kernel, [shape((rows, n_traits))] * GPD, [whole()] * 6, (), 4 * flops, 4 * moved)(
        coefficients, mask, high0, low0, high1, low1
    )
    pieces = chrom_gather(own_residual(summands, own_parts))
    residual, loco, loco_sq, *far_out = call(
        functools.partial(loco_kernel, n_chrom, far),
        [shape((rows, n_traits)), shape((rows, GPD * n_traits), jnp.bfloat16), shape((8, n_traits))]
        + [score_block] * len(far),
        [whole()] * (n_chrom + GPD + 3),
        (),
        flops,
        moved,
    )(*pieces, *own_parts, turn_tested, tested_sq, pick)
    near_out = call(
        functools.partial(loco_near_kernel, near), [score_block] * len(near), [whole()] * 5, (), flops // 2, moved
    )(turn_tested, tested_sq, pick, loco, loco_sq)
    received = [swap(piece, "samp", partner) for partner, piece in zip(order, far_out + list(near_out[:-1]))]
    own_scores = call(
        functools.partial(score_kernel, total_rows), shape((test_width, n_traits)), [whole()] * (n_samp + 1)
    )(pick, near_out[-1], *received)
    scores = call(place_kernel, shape((tests, n_traits)), [whole()] * n_samp)(*samp_gather(own_scores))
    return (scores, residual)


def solution(mesh):
    placed = (
        P("samp", "chrom"),
        P("samp", None),
        P("chrom", None),
        P("chrom"),
        P("samp", "chrom"),
        P("chrom"),
    )
    return jax.shard_map(
        body,
        mesh=mesh,
        in_specs=placed,
        out_specs=(P("chrom", None), P("samp", None)),
        check_vma=False,
    )
```

```python
import functools
import math

import jax
import jax.numpy as jnp
from jax import lax
from jax.experimental import pallas as pl
from jax.experimental.pallas import tpu as pltpu
from jax.sharding import PartitionSpec as P

GPD = 2
ITERS = 2
STATS = 16
VMEM_LIMIT = 10 * 1024 * 1024


def swap(value, axis, bits):
    size = lax.axis_size(axis)
    return lax.ppermute(value, axis, [(i, i ^ bits) for i in range(size)])


def split(value):
    high = value.astype(jnp.bfloat16)
    low = (value - high.astype(jnp.float32)).astype(jnp.bfloat16)
    return high, low


def pack(value):
    return jnp.concatenate(split(value), axis=1)


def wide_dot(high, low, packed):
    total = jnp.dot(high, packed, preferred_element_type=jnp.float32)
    total = total + jnp.dot(low, packed, preferred_element_type=jnp.float32)
    traits = packed.shape[1] // 2
    return total[:, :traits] + total[:, traits:]


def whole():
    return pl.BlockSpec(memory_space=pltpu.VMEM)


def anywhere():
    return pl.BlockSpec(memory_space=pl.ANY)


def shape(dims, dtype=jnp.float32):
    return jax.ShapeDtypeStruct(dims, dtype)


def call(kernel, outs, specs, scratch=(), flops=0, moved=0):
    return pl.pallas_call(
        kernel,
        out_shape=outs,
        in_specs=specs,
        out_specs=jax.tree.map(lambda _: whole(), outs),
        scratch_shapes=list(scratch),
        compiler_params=pltpu.CompilerParams(vmem_limit_bytes=VMEM_LIMIT),
        cost_estimate=pl.CostEstimate(flops=flops, bytes_accessed=moved, transcendentals=0),
    )


def split_rows(source_ref, ready, packed_ref, high_ref, low_ref, out_ref):
    half, block = source_ref.shape[0], source_ref.shape[1]
    group = max(1, half // 2)
    for first in range(0, half, group):
        for k in range(first, first + group):
            ready(k)
            high, low = split(source_ref[k])
            high_ref[k * block : (k + 1) * block] = high
            low_ref[k * block : (k + 1) * block] = low
        rows = slice(first * block, (first + group) * block)
        total = wide_dot(high_ref[rows], low_ref[rows], packed_ref[...])
        out_ref[first : first + group] = total.reshape((group,) + out_ref.shape[1:])


def first_kernel(dosage_ref, coef_ref, high_ref, low_ref, out_ref, packed_ref, kept_ref, buffer_ref, coef_buffer, sems):
    me = lax.axis_index("chrom")
    place, core = me // 2, me % 2
    half = buffer_ref.shape[0]
    coef_copy = pltpu.make_async_copy(coef_ref, coef_buffer, sems.at[2 * half])
    copies = [
        pltpu.make_async_copy(dosage_ref.at[place ^ k, core ^ bits], target.at[k], sems.at[bits * half + k])
        for bits, target in ((1, buffer_ref), (0, kept_ref))
        for k in range(half)
    ]
    coef_copy.start()
    for copy in copies:
        copy.start()
    coef_copy.wait()
    packed_ref[...] = pack(coef_buffer[...])
    split_rows(buffer_ref, lambda k: copies[k].wait(), packed_ref, high_ref, low_ref, out_ref)
    for copy in copies[half:]:
        copy.wait()


def second_kernel(kept_ref, packed_ref, high_ref, low_ref, out_ref):
    split_rows(kept_ref, lambda k: None, packed_ref, high_ref, low_ref, out_ref)


def square_kernel(tested_ref, square_ref):
    for place in range(square_ref.shape[0]):
        width = square_ref.shape[1] * square_ref.shape[2]
        value = tested_ref[:, place * width : (place + 1) * width].astype(jnp.float32)
        square_ref[place] = jnp.sum(value * value, axis=0).reshape(square_ref.shape[1:])


def column(row):
    down = lax.broadcasted_iota(jnp.int32, (128, 128), 0)
    across = lax.broadcasted_iota(jnp.int32, (128, 128), 1)
    return jnp.sum(jnp.where(down == across, row, 0.0), axis=1, keepdims=True)


def columns(ref):
    return jnp.concatenate([column(ref[k : k + 1]) for k in range(ref.shape[0])])


def rest_kernel(high_ref, low_ref, packed_ref, out_ref):
    out_ref[...] = wide_dot(high_ref[...], low_ref[...], packed_ref[...]).reshape(out_ref.shape)


def residual_kernel(count, traits_ref, *refs):
    total = refs[0][...]
    for piece in refs[1:count]:
        total = total + piece[...]
    refs[-1][...] = traits_ref[...] - total


def grad_dot(packed_ref, parts, which, width):
    half = packed_ref.shape[1] // 2
    cols = pl.ds(pl.multiple_of(which * width, width), width)
    total = None
    for place, part in enumerate(parts):
        left = packed_ref[:, (place // 2) * half : (place // 2 + 1) * half]
        term = jnp.dot(left, part[:, cols], preferred_element_type=jnp.float32)
        total = term if total is None else total + term
    traits = packed_ref.shape[0] // 2
    return (total[:traits] + total[traits:]).T


def grad_far_kernel(count, partners, *refs):
    pieces, parts, (packed_ref, *outs) = refs[:count], refs[count : count + 4], refs[count + 4 : -1]
    rows_ref = refs[-1]
    samp = lax.axis_index("samp")
    block = pieces[0].shape[0]
    for bits, piece in enumerate(pieces):
        start = ((bits % 2) * (count // 2) + bits // 2) * block
        rows_ref[start : start + block] = pack(piece[...])
    packed_ref[...] = rows_ref[...].T
    for partner, out in zip(partners, outs):
        out[...] = grad_dot(packed_ref, parts, samp ^ partner, out.shape[0])


def grad_near_kernel(partners, *refs):
    packed_ref, parts, outs = refs[0], refs[1:5], refs[5:]
    samp = lax.axis_index("samp")
    for partner, out in zip(partners, outs):
        out[...] = grad_dot(packed_ref, parts, samp ^ partner, out.shape[0])


def image_kernel(count, *refs):
    pieces = refs[:count]
    high_ref, low_ref = refs[count : count + 2]
    grad_ref, packed_ref, give_ref = refs[-3:]
    samp = lax.axis_index("samp")
    block = pieces[0].shape[0]
    for bits, piece in enumerate(pieces):
        rows = pl.ds(pl.multiple_of((samp ^ bits) * block, block), block)
        value = piece[...]
        grad_ref[rows] = value
        packed_ref[rows] = pack(value)
    rest_kernel(high_ref, low_ref, packed_ref, give_ref)


def norm_kernel(count, *refs):
    grad_ref, pieces, out = refs[0], refs[1 : count + 1], refs[-1]
    total = pieces[0][...]
    for piece in pieces[1:]:
        total = total + piece[...]
    grad = grad_ref[...]
    grad_sq = jnp.sum(grad * grad, axis=0, keepdims=True)
    image_sq = jnp.sum(total * total, axis=0, keepdims=True)
    sums = jnp.concatenate([grad_sq, image_sq])
    for place in range(out.shape[0]):
        out[place] = sums


def prox_kernel(total_rows, coef_ref, grad_ref, sums_ref, high_ref, low_ref, new_ref, packed_ref, give_ref):
    sums = sums_ref[0]
    for place in range(1, sums_ref.shape[0]):
        sums = sums + sums_ref[place]
    grad_sq = jnp.sum(sums[0:1], axis=1, keepdims=True)
    image_sq = jnp.sum(sums[1:2], axis=1, keepdims=True)
    step_size = grad_sq / (image_sq / total_rows + 1e-06)
    penalty = 1.5 * math.sqrt(coef_ref.shape[1] / total_rows)
    moved = coef_ref[...] + step_size * grad_ref[...]
    length = jnp.sqrt(jnp.sum(moved * moved, axis=1, keepdims=True))
    cut = step_size * penalty
    new = moved * (jnp.maximum(length - cut, 0.0) / jnp.maximum(length, cut))
    new_ref[...] = new
    packed_ref[...] = pack(new)
    rest_kernel(high_ref, low_ref, packed_ref, give_ref)


def own_kernel(coef_ref, group_ref, *refs):
    parts, outs = refs[:4], refs[4:]
    coef = coef_ref[...]
    base = lax.axis_index("chrom") * GPD
    local = columns((group_ref[...] - base).astype(jnp.float32))
    half = parts[0].shape[0]
    for which, out in enumerate(outs):
        packed = pack(jnp.where(local == which, coef, 0.0))
        out[0:half] = wide_dot(parts[0][...], parts[1][...], packed)
        out[half:] = wide_dot(parts[2][...], parts[3][...], packed)


def score_products(partner, out, tested_ref, square_ref, owner_ref, loco_ref, sums_ref):
    width, traits = out.shape[0] - STATS, out.shape[1]
    cols = pl.ds(pl.multiple_of(partner * width, width), width)
    products = jnp.dot(loco_ref[...], tested_ref[:, cols], preferred_element_type=jnp.float32)
    local = owner_ref[partner] - lax.axis_index("chrom") * GPD
    chosen = products[:traits]
    for which in range(1, GPD):
        chosen = jnp.where(local == which, products[which * traits : (which + 1) * traits], chosen)
    out[0:width] = chosen.T
    out[width : width + 8] = sums_ref[...]
    out[width + 8 : width + STATS] = jnp.zeros((STATS - 8, traits), jnp.float32)
    out[width + 8 : width + 8 + square_ref.shape[1]] = square_ref[partner]


def loco_kernel(count, partners, *refs):
    pieces, own_refs = refs[:count], refs[count : count + GPD]
    tested_ref, square_ref, owner_ref, residual_ref, loco_ref, sums_ref = refs[count + GPD : count + GPD + 6]
    outs, rows_ref = refs[count + GPD + 6 : -1], refs[-1]
    me, samp = lax.axis_index("chrom"), lax.axis_index("samp")
    block, traits = pieces[0].shape
    sums_ref[...] = jnp.zeros_like(sums_ref)
    for bits, piece in enumerate(pieces):
        rows = pl.ds(pl.multiple_of((me ^ bits) * block, block), block)
        start = ((bits % 2) * (count // 2) + bits // 2) * block
        value = piece[...]
        residual_ref[rows] = value
        for which in range(GPD):
            loco = value + own_refs[which][start : start + block]
            sums_ref[which : which + 1] += jnp.sum(loco * loco, axis=0, keepdims=True)
            rows_ref[rows, which * traits : (which + 1) * traits] = loco.astype(jnp.bfloat16)
    loco_ref[...] = rows_ref[...].T
    for partner, out in zip(partners, outs):
        score_products(samp ^ partner, out, tested_ref, square_ref, owner_ref, loco_ref, sums_ref)


def loco_near_kernel(partners, *refs):
    samp = lax.axis_index("samp")
    for partner, out in zip(partners, refs[5:]):
        score_products(samp ^ partner, out, *refs[:5])


def score_kernel(total_rows, owner_ref, *refs):
    pieces, out = refs[:-1], refs[-1]
    total = pieces[0][...]
    for piece in pieces[1:]:
        total = total + piece[...]
    cols, traits = out.shape
    base = lax.axis_index("chrom") * GPD
    owner = (owner_ref[lax.axis_index("samp")] - base).astype(jnp.float32)
    local = jnp.concatenate([column(owner[:, k * 128 : (k + 1) * 128]) for k in range(cols // 128)])
    loco_sq = jnp.broadcast_to(total[cols : cols + 1], (cols, traits))
    for which in range(1, GPD):
        loco_sq = jnp.where(local == which, total[cols + which : cols + which + 1], loco_sq)
    tested_sq = columns(total[cols + 8 : cols + 8 + cols // 128])
    denom = math.sqrt(total_rows) * jnp.sqrt((tested_sq / total_rows + 1e-06) * (loco_sq / total_rows + 1e-06))
    out[...] = total[:cols] / denom


def place_kernel(*refs):
    pieces, out = refs[:-1], refs[-1]
    samp = lax.axis_index("samp")
    block = pieces[0].shape[0]
    for bits, piece in enumerate(pieces):
        out[pl.ds(pl.multiple_of((samp ^ bits) * block, block), block)] = piece[...]


def chrom_scatter(give, keep):
    got = swap(give, "chrom", 1)
    count = keep.shape[0]
    sums = [keep[k] + got[k] for k in range(count)]
    return [sums[0]] + [swap(sums[k], "chrom", 2 * k) for k in reversed(range(1, count))]


def chrom_gather(own):
    count = lax.axis_size("chrom") // 2
    far = [swap(own, "chrom", 2 * k) for k in reversed(range(1, count))]
    mine = [own] + far[::-1]
    other = [swap(block, "chrom", 1) for block in mine]
    return [block for pair in zip(mine, other) for block in pair]


def samp_order(size):
    return list(reversed(range(size)))


def samp_gather(own):
    size = lax.axis_size("samp")
    return [own] + [swap(own, "samp", k) for k in samp_order(size)[:-1]][::-1]


def body(dosages, traits, start_coef, groups, tested, owners):
    n_samp, n_chrom = lax.axis_size("samp"), lax.axis_size("chrom")
    rows, cols = dosages.shape
    tests, n_traits = tested.shape[1], traits.shape[1]
    total_rows = rows * n_samp
    me = lax.axis_index("chrom")
    half, block, width, test_width = n_chrom // 2, rows // n_chrom, cols // n_samp, tests // n_samp
    flops = 4 * rows * cols * n_traits
    moved = 2 * rows * cols
    order = samp_order(n_samp)
    far, near = order[:-1], order[-1:]

    part = shape((rows // 2, cols), jnp.bfloat16)
    half_out = shape((half, block, n_traits))
    packed_cols = shape((cols, 2 * n_traits), jnp.bfloat16)
    packed_rows = shape((2 * n_traits, rows), jnp.bfloat16)
    rows_buffer = [pltpu.VMEM((rows, 2 * n_traits), jnp.bfloat16)]
    grad_block = shape((width, n_traits))
    score_block = shape((test_width + STATS, n_traits))
    coef_out = shape((cols, n_traits))
    group_rows = groups.reshape(cols // 128, 128)
    owner_rows = owners.reshape(n_samp, 1, test_width)
    own_traits = lax.dynamic_slice_in_dim(traits, me * block, block, 0)

    def rest(high, low, packed):
        return call(rest_kernel, half_out, [whole()] * 3, (), flops, moved)(high, low, packed)

    def own_residual(summands, after=()):
        return call(
            functools.partial(residual_kernel, len(summands)),
            shape((block, n_traits)),
            [whole()] * (1 + len(summands)) + [anywhere()] * len(after),
        )(own_traits, *summands, *after)

    coefficients = start_coef
    kept_shape = (half, block, cols)
    high1, low1, give, packed, kept = call(
        first_kernel,
        [part, part, half_out, packed_cols, shape(kept_shape)],
        [pl.BlockSpec(memory_space=pltpu.HBM)] * 2,
        [pltpu.VMEM(kept_shape, jnp.float32), pltpu.VMEM(coefficients.shape, jnp.float32), pltpu.SemaphoreType.DMA((n_chrom + 1,))],
        flops,
        4 * moved,
    )(
        pltpu.with_memory_space_constraint(dosages.reshape(half, 2, block, cols), pltpu.HBM),
        pltpu.with_memory_space_constraint(coefficients, pltpu.HBM),
    )
    high0, low0, keep = call(second_kernel, [part, part, half_out], [whole()] * 2, (), flops, moved)(kept, packed)
    summands = chrom_scatter(give, keep)
    parts = [high0, low0, high1, low1]
    tested_sq = call(square_kernel, shape((n_samp, test_width // 128, 128)), [whole()], (), 0, 2 * rows * tests)(tested)

    for iteration in range(ITERS):
        own = own_residual(summands)
        pieces = chrom_gather(own)
        packed, *far_out = call(
            functools.partial(grad_far_kernel, n_chrom, far),
            [packed_rows] + [grad_block] * len(far),
            [whole()] * (n_chrom + 4),
            rows_buffer,
            flops,
            moved,
        )(*pieces, *parts)
        near_out = call(
            functools.partial(grad_near_kernel, near), [grad_block] * len(near), [whole()] * 5, (), flops, moved
        )(packed, *parts)
        own_grad = near_out[-1]
        for partner, piece in zip(order, far_out + list(near_out[:-1])):
            own_grad = own_grad + swap(piece, "samp", partner)
        own_grad = own_grad / total_rows
        pieces = samp_gather(own_grad)
        after = (tested_sq,) if iteration == 0 else ()
        gradient, packed, give = call(
            functools.partial(image_kernel, n_samp),
            [coef_out, packed_cols, half_out],
            [whole()] * (n_samp + 2) + [anywhere()] * len(after),
            (),
            flops,
            moved,
        )(*pieces, high1, low1, *after)
        summands = chrom_scatter(give, rest(high0, low0, packed))
        size = n_samp * n_chrom
        sums = call(
            functools.partial(norm_kernel, half), shape((size, 2, n_traits)), [whole()] * (half + 1)
        )(own_grad, *summands)
        sums = lax.all_to_all(sums, ("samp", "chrom"), 0, 0)
        coefficients, packed, give = call(
            functools.partial(prox_kernel, total_rows),
            [coef_out, packed_cols, half_out],
            [whole()] * 5,
            (),
            flops,
            moved,
        )(coefficients, gradient, sums, high1, low1)
        summands = chrom_scatter(give, rest(high0, low0, packed))

    own_parts = call(own_kernel, [shape((rows, n_traits))] * GPD, [whole()] * 6, (), 4 * flops, 4 * moved)(
        coefficients, group_rows, *parts
    )
    pieces = chrom_gather(own_residual(summands, own_parts))
    residual, loco, loco_sq, *far_out = call(
        functools.partial(loco_kernel, n_chrom, far),
        [shape((rows, n_traits)), shape((GPD * n_traits, rows), jnp.bfloat16), shape((8, n_traits))]
        + [score_block] * len(far),
        [whole()] * (n_chrom + GPD + 3),
        [pltpu.VMEM((rows, GPD * n_traits), jnp.bfloat16)],
        flops,
        moved,
    )(*pieces, *own_parts, tested, tested_sq, owner_rows)
    near_out = call(
        functools.partial(loco_near_kernel, near), [score_block] * len(near), [whole()] * 5, (), flops // 2, moved
    )(tested, tested_sq, owner_rows, loco, loco_sq)
    received = [swap(piece, "samp", partner) for partner, piece in zip(order, far_out + list(near_out[:-1]))]
    own_scores = call(
        functools.partial(score_kernel, total_rows), shape((test_width, n_traits)), [whole()] * (n_samp + 1)
    )(owner_rows, near_out[-1], *received)
    scores = call(place_kernel, shape((tests, n_traits)), [whole()] * n_samp)(*samp_gather(own_scores))
    return (scores, residual)


def solution(mesh):
    placed = (
        P("samp", "chrom"),
        P("samp", None),
        P("chrom", None),
        P("chrom"),
        P("samp", "chrom"),
        P("chrom"),
    )
    return jax.shard_map(
        body,
        mesh=mesh,
        in_specs=placed,
        out_specs=(P("chrom", None), P("samp", None)),
        check_vma=False,
    )
```

```python
import functools
import math

import jax
import jax.numpy as jnp
from jax import lax
from jax.experimental import pallas as pl
from jax.experimental.pallas import tpu as pltpu
from jax.sharding import PartitionSpec as P

GPD = 2
ITERS = 2
STATS = 16
VMEM_LIMIT = 12 * 1024 * 1024


def swap(value, axis, bits):
    size = lax.axis_size(axis)
    return lax.ppermute(value, axis, [(i, i ^ bits) for i in range(size)])


def split(value):
    high = value.astype(jnp.bfloat16)
    low = (value - high.astype(jnp.float32)).astype(jnp.bfloat16)
    return high, low


def pack(value):
    return jnp.concatenate(split(value), axis=1)


def wide_dot(high, low, packed):
    total = jnp.dot(high, packed, preferred_element_type=jnp.float32)
    total = total + jnp.dot(low, packed, preferred_element_type=jnp.float32)
    traits = packed.shape[1] // 2
    return total[:, :traits] + total[:, traits:]


def whole():
    return pl.BlockSpec(memory_space=pltpu.VMEM)


def anywhere():
    return pl.BlockSpec(memory_space=pl.ANY)


def shape(dims, dtype=jnp.float32):
    return jax.ShapeDtypeStruct(dims, dtype)


def call(kernel, outs, specs, scratch=(), flops=0, moved=0):
    return pl.pallas_call(
        kernel,
        out_shape=outs,
        in_specs=specs,
        out_specs=jax.tree.map(lambda _: whole(), outs),
        scratch_shapes=list(scratch),
        compiler_params=pltpu.CompilerParams(vmem_limit_bytes=VMEM_LIMIT),
        cost_estimate=pl.CostEstimate(flops=flops, bytes_accessed=moved, transcendentals=0),
    )


def first_kernel(
    dosage_ref,
    coef_ref,
    high1_ref,
    low1_ref,
    high0_ref,
    low0_ref,
    give_ref,
    packed_ref,
    buffer_ref,
    coef_buffer,
    sems,
):
    me = lax.axis_index("chrom")
    place, core = me // 2, me % 2
    half, block = buffer_ref.shape[1], buffer_ref.shape[2]
    coef_copy = pltpu.make_async_copy(coef_ref, coef_buffer, sems.at[2 * half])
    copies = {
        (bits, k): pltpu.make_async_copy(
            dosage_ref.at[place ^ k, core ^ bits], buffer_ref.at[bits, k], sems.at[bits * half + k]
        )
        for bits in (1, 0)
        for k in range(half)
    }
    coef_copy.start()
    for copy in copies.values():
        copy.start()
    coef_copy.wait()
    packed_ref[...] = pack(coef_buffer[...])
    group = max(1, half // 2)

    def split_block(bits, k, high_ref, low_ref):
        copies[bits, k].wait()
        high, low = split(buffer_ref[bits, k])
        high_ref[k * block : (k + 1) * block] = high
        low_ref[k * block : (k + 1) * block] = low

    for first in range(0, half, group):
        for k in range(first, first + group):
            split_block(1, k, high1_ref, low1_ref)
        rows = slice(first * block, (first + group) * block)
        total = wide_dot(high1_ref[rows], low1_ref[rows], packed_ref[...])
        give_ref[first : first + group] = total.reshape((group,) + give_ref.shape[1:])
    for k in range(half):
        split_block(0, k, high0_ref, low0_ref)


def square_kernel(tested_ref, square_ref):
    for place in range(square_ref.shape[0]):
        width = square_ref.shape[1] * square_ref.shape[2]
        value = tested_ref[:, place * width : (place + 1) * width].astype(jnp.float32)
        square_ref[place] = jnp.sum(value * value, axis=0).reshape(square_ref.shape[1:])


def column(row):
    down = lax.broadcasted_iota(jnp.int32, (128, 128), 0)
    across = lax.broadcasted_iota(jnp.int32, (128, 128), 1)
    return jnp.sum(jnp.where(down == across, row, 0.0), axis=1, keepdims=True)


def columns(ref):
    return jnp.concatenate([column(ref[k : k + 1]) for k in range(ref.shape[0])])


def rest_kernel(high_ref, low_ref, packed_ref, out_ref):
    out_ref[...] = wide_dot(high_ref[...], low_ref[...], packed_ref[...]).reshape(out_ref.shape)


def residual_kernel(count, traits_ref, *refs):
    total = refs[0][...]
    for piece in refs[1:count]:
        total = total + piece[...]
    refs[-1][...] = traits_ref[...] - total


def grad_dot(packed_ref, parts, which, width):
    half = packed_ref.shape[1] // 2
    cols = pl.ds(pl.multiple_of(which * width, width), width)
    total = None
    for place, part in enumerate(parts):
        left = packed_ref[:, (place // 2) * half : (place // 2 + 1) * half]
        term = jnp.dot(left, part[:, cols], preferred_element_type=jnp.float32)
        total = term if total is None else total + term
    traits = packed_ref.shape[0] // 2
    return (total[:traits] + total[traits:]).T


def grad_far_kernel(count, partners, *refs):
    pieces, parts, (packed_ref, *outs) = refs[:count], refs[count : count + 4], refs[count + 4 : -1]
    rows_ref = refs[-1]
    samp = lax.axis_index("samp")
    block = pieces[0].shape[0]
    for bits, piece in zip(chrom_order(count), pieces):
        start = ((bits % 2) * (count // 2) + bits // 2) * block
        rows_ref[start : start + block] = pack(piece[...])
    packed_ref[...] = rows_ref[...].T
    for partner, out in zip(partners, outs):
        out[...] = grad_dot(packed_ref, parts, samp ^ partner, out.shape[0])


def grad_near_kernel(partners, *refs):
    packed_ref, parts, outs = refs[0], refs[1:5], refs[5:]
    samp = lax.axis_index("samp")
    for partner, out in zip(partners, outs):
        out[...] = grad_dot(packed_ref, parts, samp ^ partner, out.shape[0])


def image_kernel(count, *refs):
    pieces = refs[:count]
    high_ref, low_ref = refs[count : count + 2]
    grad_ref, packed_ref, give_ref = refs[-3:]
    samp = lax.axis_index("samp")
    block = pieces[0].shape[0]
    for bits, piece in enumerate(pieces):
        rows = pl.ds(pl.multiple_of((samp ^ bits) * block, block), block)
        value = piece[...]
        grad_ref[rows] = value
        packed_ref[rows] = pack(value)
    rest_kernel(high_ref, low_ref, packed_ref, give_ref)


def norm_kernel(count, *refs):
    grad_ref, pieces, out = refs[0], refs[1 : count + 1], refs[-1]
    total = pieces[0][...]
    for piece in pieces[1:]:
        total = total + piece[...]
    grad = grad_ref[...]
    out[0:1] = jnp.sum(grad * grad, axis=0, keepdims=True)
    out[1:2] = jnp.sum(total * total, axis=0, keepdims=True)


def spread_kernel(own_ref, other_ref, out_ref):
    total = own_ref[...] + other_ref[...]
    for place in range(out_ref.shape[0]):
        out_ref[place] = total


def prox_kernel(total_rows, coef_ref, grad_ref, sums_ref, high_ref, low_ref, new_ref, packed_ref, give_ref):
    sums = sums_ref[0]
    for place in range(1, sums_ref.shape[0]):
        sums = sums + sums_ref[place]
    grad_sq = jnp.sum(sums[0:1], axis=1, keepdims=True)
    image_sq = jnp.sum(sums[1:2], axis=1, keepdims=True)
    step_size = grad_sq / (image_sq / total_rows + 1e-06)
    penalty = 1.5 * math.sqrt(coef_ref.shape[1] / total_rows)
    moved = coef_ref[...] + step_size * grad_ref[...]
    length = jnp.sqrt(jnp.sum(moved * moved, axis=1, keepdims=True))
    cut = step_size * penalty
    new = moved * (jnp.maximum(length - cut, 0.0) / jnp.maximum(length, cut))
    new_ref[...] = new
    packed_ref[...] = pack(new)
    rest_kernel(high_ref, low_ref, packed_ref, give_ref)


def own_kernel(coef_ref, group_ref, *refs):
    parts, outs = refs[:4], refs[4:]
    coef = coef_ref[...]
    base = lax.axis_index("chrom") * GPD
    local = columns((group_ref[...] - base).astype(jnp.float32))
    half = parts[0].shape[0]
    for which, out in enumerate(outs):
        packed = pack(jnp.where(local == which, coef, 0.0))
        out[0:half] = wide_dot(parts[0][...], parts[1][...], packed)
        out[half:] = wide_dot(parts[2][...], parts[3][...], packed)


def score_products(partner, out, tested_ref, square_ref, owner_ref, loco_ref, sums_ref):
    width, traits = out.shape[0] - STATS, out.shape[1]
    cols = pl.ds(pl.multiple_of(partner * width, width), width)
    products = jnp.dot(loco_ref[...], tested_ref[:, cols], preferred_element_type=jnp.float32)
    local = owner_ref[partner] - lax.axis_index("chrom") * GPD
    chosen = products[:traits]
    for which in range(1, GPD):
        chosen = jnp.where(local == which, products[which * traits : (which + 1) * traits], chosen)
    out[0:width] = chosen.T
    out[width : width + 8] = sums_ref[...]
    out[width + 8 : width + STATS] = jnp.zeros((STATS - 8, traits), jnp.float32)
    out[width + 8 : width + 8 + square_ref.shape[1]] = square_ref[partner]


def loco_kernel(count, partners, *refs):
    pieces, own_refs = refs[:count], refs[count : count + GPD]
    tested_ref, square_ref, owner_ref, loco_ref, sums_ref = refs[count + GPD : count + GPD + 5]
    outs, rows_ref = refs[count + GPD + 5 : -1], refs[-1]
    me, samp = lax.axis_index("chrom"), lax.axis_index("samp")
    block, traits = pieces[0].shape
    sums_ref[...] = jnp.zeros_like(sums_ref)
    for bits, piece in zip(chrom_order(count), pieces):
        rows = pl.ds(pl.multiple_of((me ^ bits) * block, block), block)
        start = ((bits % 2) * (count // 2) + bits // 2) * block
        value = piece[...]
        for which in range(GPD):
            loco = value + own_refs[which][start : start + block]
            sums_ref[which : which + 1] += jnp.sum(loco * loco, axis=0, keepdims=True)
            rows_ref[rows, which * traits : (which + 1) * traits] = loco.astype(jnp.bfloat16)
    loco_ref[...] = rows_ref[...].T
    for partner, out in zip(partners, outs):
        score_products(samp ^ partner, out, tested_ref, square_ref, owner_ref, loco_ref, sums_ref)


def loco_near_kernel(count, partners, *refs):
    pieces, operands, residual_ref, outs = refs[:count], refs[count : count + 5], refs[count + 5], refs[count + 6 :]
    me, samp = lax.axis_index("chrom"), lax.axis_index("samp")
    block = pieces[0].shape[0]
    for bits, piece in zip(chrom_order(count), pieces):
        residual_ref[pl.ds(pl.multiple_of((me ^ bits) * block, block), block)] = piece[...]
    for partner, out in zip(partners, outs):
        score_products(samp ^ partner, out, *operands)


def score_kernel(total_rows, owner_ref, *refs):
    pieces, out = refs[:-1], refs[-1]
    total = pieces[0][...]
    for piece in pieces[1:]:
        total = total + piece[...]
    cols, traits = out.shape
    base = lax.axis_index("chrom") * GPD
    owner = (owner_ref[lax.axis_index("samp")] - base).astype(jnp.float32)
    local = jnp.concatenate([column(owner[:, k * 128 : (k + 1) * 128]) for k in range(cols // 128)])
    loco_sq = jnp.broadcast_to(total[cols : cols + 1], (cols, traits))
    for which in range(1, GPD):
        loco_sq = jnp.where(local == which, total[cols + which : cols + which + 1], loco_sq)
    tested_sq = columns(total[cols + 8 : cols + 8 + cols // 128])
    denom = math.sqrt(total_rows) * jnp.sqrt((tested_sq / total_rows + 1e-06) * (loco_sq / total_rows + 1e-06))
    out[...] = total[:cols] / denom


def place_kernel(*refs):
    pieces, out = refs[:-1], refs[-1]
    samp = lax.axis_index("samp")
    block = pieces[0].shape[0]
    for bits, piece in enumerate(pieces):
        out[pl.ds(pl.multiple_of((samp ^ bits) * block, block), block)] = piece[...]


def chrom_scatter(give, keep):
    got = swap(give, "chrom", 1)
    count = keep.shape[0]
    sums = [keep[k] + got[k] for k in range(count)]
    return [sums[0]] + [swap(sums[k], "chrom", 2 * k) for k in range(1, count)]


def chrom_gather(own):
    count = lax.axis_size("chrom") // 2
    blocks = []
    for k in range(count):
        block = swap(own, "chrom", 2 * k) if k else own
        blocks += [block, swap(block, "chrom", 1)]
    return blocks


def chrom_order(size):
    return [2 * k + bits for k in range(size // 2) for bits in range(2)]


def samp_order(size):
    return list(reversed(range(size)))


def samp_gather(own):
    size = lax.axis_size("samp")
    return [own] + [swap(own, "samp", k) for k in samp_order(size)[:-1]][::-1]


def body(dosages, traits, start_coef, groups, tested, owners):
    n_samp, n_chrom = lax.axis_size("samp"), lax.axis_size("chrom")
    rows, cols = dosages.shape
    tests, n_traits = tested.shape[1], traits.shape[1]
    total_rows = rows * n_samp
    me = lax.axis_index("chrom")
    half, block, width, test_width = n_chrom // 2, rows // n_chrom, cols // n_samp, tests // n_samp
    flops = 4 * rows * cols * n_traits
    moved = 2 * rows * cols
    order = samp_order(n_samp)
    far, near = order[:-1], order[-1:]

    part = shape((rows // 2, cols), jnp.bfloat16)
    half_out = shape((half, block, n_traits))
    packed_cols = shape((cols, 2 * n_traits), jnp.bfloat16)
    packed_rows = shape((2 * n_traits, rows), jnp.bfloat16)
    rows_buffer = [pltpu.VMEM((rows, 2 * n_traits), jnp.bfloat16)]
    grad_block = shape((width, n_traits))
    score_block = shape((test_width + STATS, n_traits))
    coef_out = shape((cols, n_traits))
    group_rows = groups.reshape(cols // 128, 128)
    owner_rows = owners.reshape(n_samp, 1, test_width)
    own_traits = lax.dynamic_slice_in_dim(traits, me * block, block, 0)

    def rest(high, low, packed):
        return call(rest_kernel, half_out, [whole()] * 3, (), flops, moved)(high, low, packed)

    def own_residual(summands, after=()):
        return call(
            functools.partial(residual_kernel, len(summands)),
            shape((block, n_traits)),
            [whole()] * (1 + len(summands)) + [anywhere()] * len(after),
        )(own_traits, *summands, *after)

    coefficients = start_coef
    high1, low1, high0, low0, give, packed = call(
        first_kernel,
        [part] * 4 + [half_out, packed_cols],
        [pl.BlockSpec(memory_space=pltpu.HBM)] * 2,
        [
            pltpu.VMEM((2, half, block, cols), jnp.float32),
            pltpu.VMEM(coefficients.shape, jnp.float32),
            pltpu.SemaphoreType.DMA((n_chrom + 1,)),
        ],
        flops,
        4 * moved,
    )(
        pltpu.with_memory_space_constraint(dosages.reshape(half, 2, block, cols), pltpu.HBM),
        pltpu.with_memory_space_constraint(coefficients, pltpu.HBM),
    )
    keep = rest(high0, low0, packed)
    summands = chrom_scatter(give, keep)
    parts = [high0, low0, high1, low1]
    tested_sq = call(square_kernel, shape((n_samp, test_width // 128, 128)), [whole()], (), 0, 2 * rows * tests)(tested)

    for iteration in range(ITERS):
        own = own_residual(summands)
        pieces = chrom_gather(own)
        packed, *far_out = call(
            functools.partial(grad_far_kernel, n_chrom, far),
            [packed_rows] + [grad_block] * len(far),
            [whole()] * (n_chrom + 4),
            rows_buffer,
            flops,
            moved,
        )(*pieces, *parts)
        near_out = call(
            functools.partial(grad_near_kernel, near), [grad_block] * len(near), [whole()] * 5, (), flops, moved
        )(packed, *parts)
        own_grad = near_out[-1]
        for partner, piece in zip(order, far_out + list(near_out[:-1])):
            own_grad = own_grad + swap(piece, "samp", partner)
        own_grad = own_grad / total_rows
        pieces = samp_gather(own_grad)
        after = (tested_sq,) if iteration == 0 else ()
        gradient, packed, give = call(
            functools.partial(image_kernel, n_samp),
            [coef_out, packed_cols, half_out],
            [whole()] * (n_samp + 2) + [anywhere()] * len(after),
            (),
            flops,
            moved,
        )(*pieces, high1, low1, *after)
        summands = chrom_scatter(give, rest(high0, low0, packed))
        size = n_samp * half
        sums = call(functools.partial(norm_kernel, half), shape((2, n_traits)), [whole()] * (half + 1))(
            own_grad, *summands
        )
        sums = call(spread_kernel, shape((size, 2, n_traits)), [whole()] * 2)(sums, swap(sums, "chrom", 1))
        cores = [list(range(core, n_samp * n_chrom, 2)) for core in range(2)]
        sums = lax.all_to_all(sums, ("samp", "chrom"), 0, 0, axis_index_groups=cores)
        coefficients, packed, give = call(
            functools.partial(prox_kernel, total_rows),
            [coef_out, packed_cols, half_out],
            [whole()] * 5,
            (),
            flops,
            moved,
        )(coefficients, gradient, sums, high1, low1)
        summands = chrom_scatter(give, rest(high0, low0, packed))

    own_parts = call(own_kernel, [shape((rows, n_traits))] * GPD, [whole()] * 6, (), 4 * flops, 4 * moved)(
        coefficients, group_rows, *parts
    )
    pieces = chrom_gather(own_residual(summands, own_parts))
    loco, loco_sq, *far_out = call(
        functools.partial(loco_kernel, n_chrom, far),
        [shape((GPD * n_traits, rows), jnp.bfloat16), shape((8, n_traits))]
        + [score_block] * len(far),
        [whole()] * (n_chrom + GPD + 3),
        [pltpu.VMEM((rows, GPD * n_traits), jnp.bfloat16)],
        flops,
        moved,
    )(*pieces, *own_parts, tested, tested_sq, owner_rows)
    residual, *near_out = call(
        functools.partial(loco_near_kernel, n_chrom, near),
        [shape((rows, n_traits))] + [score_block] * len(near),
        [whole()] * (n_chrom + 5),
        (),
        flops // 2,
        moved,
    )(*pieces, tested, tested_sq, owner_rows, loco, loco_sq)
    received = [swap(piece, "samp", partner) for partner, piece in zip(order, far_out + list(near_out[:-1]))]
    own_scores = call(
        functools.partial(score_kernel, total_rows), shape((test_width, n_traits)), [whole()] * (n_samp + 1)
    )(owner_rows, near_out[-1], *received)
    scores = call(place_kernel, shape((tests, n_traits)), [whole()] * n_samp)(*samp_gather(own_scores))
    return (scores, residual)


def solution(mesh):
    placed = (
        P("samp", "chrom"),
        P("samp", None),
        P("chrom", None),
        P("chrom"),
        P("samp", "chrom"),
        P("chrom"),
    )
    return jax.shard_map(
        body,
        mesh=mesh,
        in_specs=placed,
        out_specs=(P("chrom", None), P("samp", None)),
        check_vma=False,
    )
```

```python
import functools
import math

import jax
import jax.numpy as jnp
from jax import lax
from jax.experimental import pallas as pl
from jax.experimental.pallas import tpu as pltpu
from jax.sharding import PartitionSpec as P

GPD = 2
ITERS = 2
STATS = 16
VMEM_LIMIT = 10 * 1024 * 1024


def swap(value, axis, bits):
    size = lax.axis_size(axis)
    return lax.ppermute(value, axis, [(i, i ^ bits) for i in range(size)])


def split(value):
    high = value.astype(jnp.bfloat16)
    low = (value - high.astype(jnp.float32)).astype(jnp.bfloat16)
    return high, low


def pack(value):
    return jnp.concatenate(split(value), axis=1)


def wide_dot(high, low, packed):
    total = jnp.dot(high, packed, preferred_element_type=jnp.float32)
    total = total + jnp.dot(low, packed, preferred_element_type=jnp.float32)
    traits = packed.shape[1] // 2
    return total[:, :traits] + total[:, traits:]


def whole():
    return pl.BlockSpec(memory_space=pltpu.VMEM)


def anywhere():
    return pl.BlockSpec(memory_space=pl.ANY)


def shape(dims, dtype=jnp.float32):
    return jax.ShapeDtypeStruct(dims, dtype)


def call(kernel, outs, specs, scratch=(), flops=0, moved=0):
    return pl.pallas_call(
        kernel,
        out_shape=outs,
        in_specs=specs,
        out_specs=jax.tree.map(lambda _: whole(), outs),
        scratch_shapes=list(scratch),
        compiler_params=pltpu.CompilerParams(vmem_limit_bytes=VMEM_LIMIT),
        cost_estimate=pl.CostEstimate(flops=flops, bytes_accessed=moved, transcendentals=0),
    )


def split_rows(source_ref, ready, packed_ref, high_ref, low_ref, out_ref):
    half, block = source_ref.shape[0], source_ref.shape[1]
    group = max(1, half // 2)
    for first in range(0, half, group):
        for k in range(first, first + group):
            ready(k)
            high, low = split(source_ref[k])
            high_ref[k * block : (k + 1) * block] = high
            low_ref[k * block : (k + 1) * block] = low
        rows = slice(first * block, (first + group) * block)
        total = wide_dot(high_ref[rows], low_ref[rows], packed_ref[...])
        out_ref[first : first + group] = total.reshape((group,) + out_ref.shape[1:])


def first_kernel(dosage_ref, coef_ref, high_ref, low_ref, out_ref, packed_ref, kept_ref, buffer_ref, coef_buffer, sems):
    me = lax.axis_index("chrom")
    place, core = me // 2, me % 2
    half = buffer_ref.shape[0]
    coef_copy = pltpu.make_async_copy(coef_ref, coef_buffer, sems.at[2 * half])
    copies = [
        pltpu.make_async_copy(dosage_ref.at[place ^ k, core ^ bits], target.at[k], sems.at[bits * half + k])
        for bits, target in ((1, buffer_ref), (0, kept_ref))
        for k in range(half)
    ]
    coef_copy.start()
    for copy in copies[:half]:
        copy.start()
    coef_copy.wait()
    packed_ref[...] = pack(coef_buffer[...])

    def ready(k):
        copies[k].wait()
        if k == half // 2:
            for copy in copies[half:]:
                copy.start()

    split_rows(buffer_ref, ready, packed_ref, high_ref, low_ref, out_ref)
    for copy in copies[half:]:
        copy.wait()


def second_kernel(kept_ref, packed_ref, high_ref, low_ref, out_ref):
    split_rows(kept_ref, lambda k: None, packed_ref, high_ref, low_ref, out_ref)


def square_kernel(tested_ref, square_ref):
    for place in range(square_ref.shape[0]):
        width = square_ref.shape[1] * square_ref.shape[2]
        value = tested_ref[:, place * width : (place + 1) * width].astype(jnp.float32)
        square_ref[place] = jnp.sum(value * value, axis=0).reshape(square_ref.shape[1:])


def column(row):
    down = lax.broadcasted_iota(jnp.int32, (128, 128), 0)
    across = lax.broadcasted_iota(jnp.int32, (128, 128), 1)
    return jnp.sum(jnp.where(down == across, row, 0.0), axis=1, keepdims=True)


def columns(ref):
    return jnp.concatenate([column(ref[k : k + 1]) for k in range(ref.shape[0])])


def rest_kernel(high_ref, low_ref, packed_ref, out_ref):
    out_ref[...] = wide_dot(high_ref[...], low_ref[...], packed_ref[...]).reshape(out_ref.shape)


def residual_kernel(count, traits_ref, *refs):
    out = refs[-1]
    block = out.shape[0]
    total = refs[0][...]
    for piece in refs[1:count]:
        total = total + piece[...]
    start = pl.multiple_of(lax.axis_index("chrom") * block, block)
    out[...] = traits_ref[pl.ds(start, block)] - total


def grad_dot(packed_ref, parts, which, width):
    half = packed_ref.shape[1] // 2
    cols = pl.ds(pl.multiple_of(which * width, width), width)
    total = None
    for place, part in enumerate(parts):
        left = packed_ref[:, (place // 2) * half : (place // 2 + 1) * half]
        term = jnp.dot(left, part[:, cols], preferred_element_type=jnp.float32)
        total = term if total is None else total + term
    traits = packed_ref.shape[0] // 2
    return (total[:traits] + total[traits:]).T


def grad_far_kernel(count, partners, *refs):
    pieces, parts, (packed_ref, *outs) = refs[:count], refs[count : count + 4], refs[count + 4 : -1]
    rows_ref = refs[-1]
    samp = lax.axis_index("samp")
    block = pieces[0].shape[0]
    for bits, piece in enumerate(pieces):
        start = ((bits % 2) * (count // 2) + bits // 2) * block
        rows_ref[start : start + block] = pack(piece[...])
    packed_ref[...] = rows_ref[...].T
    for partner, out in zip(partners, outs):
        out[...] = grad_dot(packed_ref, parts, samp ^ partner, out.shape[0])


def grad_near_kernel(partners, *refs):
    packed_ref, parts, outs = refs[0], refs[1:5], refs[5:]
    samp = lax.axis_index("samp")
    for partner, out in zip(partners, outs):
        out[...] = grad_dot(packed_ref, parts, samp ^ partner, out.shape[0])


def image_kernel(count, *refs):
    pieces = refs[:count]
    high_ref, low_ref = refs[count : count + 2]
    grad_ref, packed_ref, give_ref = refs[-3:]
    samp = lax.axis_index("samp")
    block = pieces[0].shape[0]
    for bits, piece in enumerate(pieces):
        rows = pl.ds(pl.multiple_of((samp ^ bits) * block, block), block)
        value = piece[...]
        grad_ref[rows] = value
        packed_ref[rows] = pack(value)
    rest_kernel(high_ref, low_ref, packed_ref, give_ref)


def norm_kernel(count, *refs):
    grad_ref, pieces, out = refs[0], refs[1 : count + 1], refs[-1]
    total = pieces[0][...]
    for piece in pieces[1:]:
        total = total + piece[...]
    grad = grad_ref[...]
    grad_sq = jnp.sum(grad * grad, axis=0, keepdims=True)
    image_sq = jnp.sum(total * total, axis=0, keepdims=True)
    sums = jnp.concatenate([grad_sq, image_sq])
    for place in range(out.shape[0]):
        out[place] = sums


def prox_kernel(total_rows, coef_ref, grad_ref, sums_ref, high_ref, low_ref, new_ref, packed_ref, give_ref):
    sums = sums_ref[0]
    for place in range(1, sums_ref.shape[0]):
        sums = sums + sums_ref[place]
    grad_sq = jnp.sum(sums[0:1], axis=1, keepdims=True)
    image_sq = jnp.sum(sums[1:2], axis=1, keepdims=True)
    step_size = grad_sq / (image_sq / total_rows + 1e-06)
    penalty = 1.5 * math.sqrt(coef_ref.shape[1] / total_rows)
    moved = coef_ref[...] + step_size * grad_ref[...]
    length = jnp.sqrt(jnp.sum(moved * moved, axis=1, keepdims=True))
    cut = step_size * penalty
    new = moved * (jnp.maximum(length - cut, 0.0) / jnp.maximum(length, cut))
    new_ref[...] = new
    packed_ref[...] = pack(new)
    rest_kernel(high_ref, low_ref, packed_ref, give_ref)


def own_kernel(coef_ref, group_ref, *refs):
    parts, outs = refs[:4], refs[4:]
    coef = coef_ref[...]
    base = lax.axis_index("chrom") * GPD
    local = columns((group_ref[...] - base).astype(jnp.float32))
    half = parts[0].shape[0]
    for which, out in enumerate(outs):
        packed = pack(jnp.where(local == which, coef, 0.0))
        out[0:half] = wide_dot(parts[0][...], parts[1][...], packed)
        out[half:] = wide_dot(parts[2][...], parts[3][...], packed)


def score_products(partner, out, tested_ref, square_ref, owner_ref, loco_ref, sums_ref):
    width, traits = out.shape[0] - STATS, out.shape[1]
    cols = pl.ds(pl.multiple_of(partner * width, width), width)
    products = jnp.dot(loco_ref[...], tested_ref[:, cols], preferred_element_type=jnp.float32)
    local = owner_ref[partner] - lax.axis_index("chrom") * GPD
    chosen = products[:traits]
    for which in range(1, GPD):
        chosen = jnp.where(local == which, products[which * traits : (which + 1) * traits], chosen)
    out[0:width] = chosen.T
    out[width : width + 8] = sums_ref[...]
    out[width + 8 : width + STATS] = jnp.zeros((STATS - 8, traits), jnp.float32)
    out[width + 8 : width + 8 + square_ref.shape[1]] = square_ref[partner]


def loco_kernel(count, partners, *refs):
    pieces, own_refs = refs[:count], refs[count : count + GPD]
    tested_ref, square_ref, owner_ref, loco_ref, sums_ref = refs[count + GPD : count + GPD + 5]
    outs, rows_ref = refs[count + GPD + 5 : -1], refs[-1]
    me, samp = lax.axis_index("chrom"), lax.axis_index("samp")
    block, traits = pieces[0].shape
    sums_ref[...] = jnp.zeros_like(sums_ref)
    for bits, piece in enumerate(pieces):
        rows = pl.ds(pl.multiple_of((me ^ bits) * block, block), block)
        start = ((bits % 2) * (count // 2) + bits // 2) * block
        value = piece[...]
        for which in range(GPD):
            loco = value + own_refs[which][start : start + block]
            sums_ref[which : which + 1] += jnp.sum(loco * loco, axis=0, keepdims=True)
            rows_ref[rows, which * traits : (which + 1) * traits] = loco.astype(jnp.bfloat16)
    loco_ref[...] = rows_ref[...].T
    for partner, out in zip(partners, outs):
        score_products(samp ^ partner, out, tested_ref, square_ref, owner_ref, loco_ref, sums_ref)


def loco_near_kernel(count, partners, *refs):
    pieces, operands, residual_ref, outs = refs[:count], refs[count : count + 5], refs[count + 5], refs[count + 6 :]
    me, samp = lax.axis_index("chrom"), lax.axis_index("samp")
    block = pieces[0].shape[0]
    for bits, piece in enumerate(pieces):
        residual_ref[pl.ds(pl.multiple_of((me ^ bits) * block, block), block)] = piece[...]
    for partner, out in zip(partners, outs):
        score_products(samp ^ partner, out, *operands)


def score_kernel(total_rows, owner_ref, *refs):
    pieces, out = refs[:-1], refs[-1]
    total = pieces[0][...]
    for piece in pieces[1:]:
        total = total + piece[...]
    cols, traits = out.shape
    base = lax.axis_index("chrom") * GPD
    owner = (owner_ref[lax.axis_index("samp")] - base).astype(jnp.float32)
    local = jnp.concatenate([column(owner[:, k * 128 : (k + 1) * 128]) for k in range(cols // 128)])
    loco_sq = jnp.broadcast_to(total[cols : cols + 1], (cols, traits))
    for which in range(1, GPD):
        loco_sq = jnp.where(local == which, total[cols + which : cols + which + 1], loco_sq)
    tested_sq = columns(total[cols + 8 : cols + 8 + cols // 128])
    denom = math.sqrt(total_rows) * jnp.sqrt((tested_sq / total_rows + 1e-06) * (loco_sq / total_rows + 1e-06))
    out[...] = total[:cols] / denom


def place_kernel(*refs):
    pieces, out = refs[:-1], refs[-1]
    samp = lax.axis_index("samp")
    block = pieces[0].shape[0]
    for bits, piece in enumerate(pieces):
        out[pl.ds(pl.multiple_of((samp ^ bits) * block, block), block)] = piece[...]


def chip_kernel(keep_ref, got_ref, *outs):
    for k, out in enumerate(outs):
        out[...] = keep_ref[k] + got_ref[k]


def mean_kernel(total_rows, *refs):
    total = refs[0][...]
    for piece in refs[1:-1]:
        total = total + piece[...]
    refs[-1][...] = total / total_rows


def chrom_scatter(give, keep):
    got = swap(give, "chrom", 1)
    count = keep.shape[0]
    sums = call(chip_kernel, [shape(keep.shape[1:])] * count, [whole()] * 2)(keep, got)
    return [sums[0]] + [swap(sums[k], "chrom", 2 * k) for k in reversed(range(1, count))]


def chrom_gather(own):
    blocks = []
    for k in range(lax.axis_size("chrom") // 2):
        block = swap(own, "chrom", 2 * k) if k else own
        blocks += [block, swap(block, "chrom", 1)]
    return blocks


def samp_order(size):
    return list(reversed(range(size)))


def samp_gather(own):
    size = lax.axis_size("samp")
    return [own] + [swap(own, "samp", k) for k in samp_order(size)[:-1]][::-1]


def body(dosages, traits, start_coef, groups, tested, owners):
    n_samp, n_chrom = lax.axis_size("samp"), lax.axis_size("chrom")
    rows, cols = dosages.shape
    tests, n_traits = tested.shape[1], traits.shape[1]
    total_rows = rows * n_samp
    half, block, width, test_width = n_chrom // 2, rows // n_chrom, cols // n_samp, tests // n_samp
    flops = 4 * rows * cols * n_traits
    moved = 2 * rows * cols
    order = samp_order(n_samp)
    far, near = order[:-1], order[-1:]

    part = shape((rows // 2, cols), jnp.bfloat16)
    half_out = shape((half, block, n_traits))
    packed_cols = shape((cols, 2 * n_traits), jnp.bfloat16)
    packed_rows = shape((2 * n_traits, rows), jnp.bfloat16)
    rows_buffer = [pltpu.VMEM((rows, 2 * n_traits), jnp.bfloat16)]
    grad_block = shape((width, n_traits))
    score_block = shape((test_width + STATS, n_traits))
    coef_out = shape((cols, n_traits))
    group_rows = groups.reshape(cols // 128, 128)
    owner_rows = owners.reshape(n_samp, 1, test_width)

    def rest(high, low, packed):
        return call(rest_kernel, half_out, [whole()] * 3, (), flops, moved)(high, low, packed)

    def own_residual(summands, after=()):
        return call(
            functools.partial(residual_kernel, len(summands)),
            shape((block, n_traits)),
            [whole()] * (1 + len(summands)) + [anywhere()] * len(after),
        )(traits, *summands, *after)

    coefficients = start_coef
    kept_shape = (half, block, cols)
    high1, low1, give, packed, kept = call(
        first_kernel,
        [part, part, half_out, packed_cols, shape(kept_shape)],
        [pl.BlockSpec(memory_space=pltpu.HBM)] * 2,
        [pltpu.VMEM(kept_shape, jnp.float32), pltpu.VMEM(coefficients.shape, jnp.float32), pltpu.SemaphoreType.DMA((n_chrom + 1,))],
        flops,
        4 * moved,
    )(
        pltpu.with_memory_space_constraint(dosages.reshape(half, 2, block, cols), pltpu.HBM),
        pltpu.with_memory_space_constraint(coefficients, pltpu.HBM),
    )
    high0, low0, keep = call(second_kernel, [part, part, half_out], [whole()] * 2, (), flops, moved)(kept, packed)
    summands = chrom_scatter(give, keep)
    parts = [high0, low0, high1, low1]
    tested_sq = call(square_kernel, shape((n_samp, test_width // 128, 128)), [whole()], (), 0, 2 * rows * tests)(tested)

    for iteration in range(ITERS):
        own = own_residual(summands)
        pieces = chrom_gather(own)
        packed, *far_out = call(
            functools.partial(grad_far_kernel, n_chrom, far),
            [packed_rows] + [grad_block] * len(far),
            [whole()] * (n_chrom + 4),
            rows_buffer,
            flops,
            moved,
        )(*pieces, *parts)
        near_out = call(
            functools.partial(grad_near_kernel, near), [grad_block] * len(near), [whole()] * 5, (), flops, moved
        )(packed, *parts)
        received = [swap(piece, "samp", partner) for partner, piece in zip(order, far_out)]
        own_grad = call(functools.partial(mean_kernel, total_rows), grad_block, [whole()] * n_samp)(
            near_out[-1], *received
        )
        pieces = samp_gather(own_grad)
        after = (tested_sq,) if iteration == 0 else ()
        gradient, packed, give = call(
            functools.partial(image_kernel, n_samp),
            [coef_out, packed_cols, half_out],
            [whole()] * (n_samp + 2) + [anywhere()] * len(after),
            (),
            flops,
            moved,
        )(*pieces, high1, low1, *after)
        summands = chrom_scatter(give, rest(high0, low0, packed))
        size = n_samp * n_chrom
        sums = call(
            functools.partial(norm_kernel, half), shape((size, 2, n_traits)), [whole()] * (half + 1)
        )(own_grad, *summands)
        sums = lax.all_to_all(sums, ("samp", "chrom"), 0, 0)
        coefficients, packed, give = call(
            functools.partial(prox_kernel, total_rows),
            [coef_out, packed_cols, half_out],
            [whole()] * 5,
            (),
            flops,
            moved,
        )(coefficients, gradient, sums, high1, low1)
        summands = chrom_scatter(give, rest(high0, low0, packed))

    own_parts = call(own_kernel, [shape((rows, n_traits))] * GPD, [whole()] * 6, (), 4 * flops, 4 * moved)(
        coefficients, group_rows, *parts
    )
    pieces = chrom_gather(own_residual(summands, own_parts))
    loco, loco_sq, *far_out = call(
        functools.partial(loco_kernel, n_chrom, far),
        [shape((GPD * n_traits, rows), jnp.bfloat16), shape((8, n_traits))]
        + [score_block] * len(far),
        [whole()] * (n_chrom + GPD + 3),
        [pltpu.VMEM((rows, GPD * n_traits), jnp.bfloat16)],
        flops,
        moved,
    )(*pieces, *own_parts, tested, tested_sq, owner_rows)
    residual, *near_out = call(
        functools.partial(loco_near_kernel, n_chrom, near),
        [shape((rows, n_traits))] + [score_block] * len(near),
        [whole()] * (n_chrom + 5),
        (),
        flops // 2,
        moved,
    )(*pieces, tested, tested_sq, owner_rows, loco, loco_sq)
    received = [swap(piece, "samp", partner) for partner, piece in zip(order, far_out)]
    own_scores = call(
        functools.partial(score_kernel, total_rows), shape((test_width, n_traits)), [whole()] * (n_samp + 1)
    )(owner_rows, near_out[-1], *received)
    scores = call(place_kernel, shape((tests, n_traits)), [whole()] * n_samp)(*samp_gather(own_scores))
    return (scores, residual)


def solution(mesh):
    placed = (
        P("samp", "chrom"),
        P("samp", None),
        P("chrom", None),
        P("chrom"),
        P("samp", "chrom"),
        P("chrom"),
    )
    return jax.shard_map(
        body,
        mesh=mesh,
        in_specs=placed,
        out_specs=(P("chrom", None), P("samp", None)),
        check_vma=False,
    )
```

```python
import functools
import math

import jax
import jax.numpy as jnp
from jax import lax
from jax.experimental import pallas as pl
from jax.experimental.pallas import tpu as pltpu
from jax.sharding import PartitionSpec as P

GPD = 2
ITERS = 2
STATS = 16
PARTS = 2
VMEM_LIMIT = 10 * 1024 * 1024


def swap(value, axis, bits):
    size = lax.axis_size(axis)
    return lax.ppermute(value, axis, [(i, i ^ bits) for i in range(size)])


def split(value):
    high = value.astype(jnp.bfloat16)
    low = (value - high.astype(jnp.float32)).astype(jnp.bfloat16)
    return high, low


def pack(value):
    return jnp.concatenate(split(value), axis=1)


def wide_dot(high, low, packed):
    total = jnp.dot(high, packed, preferred_element_type=jnp.float32)
    total = total + jnp.dot(low, packed, preferred_element_type=jnp.float32)
    traits = packed.shape[1] // 2
    return total[:, :traits] + total[:, traits:]


def whole():
    return pl.BlockSpec(memory_space=pltpu.VMEM)


def anywhere():
    return pl.BlockSpec(memory_space=pl.ANY)


def shape(dims, dtype=jnp.float32):
    return jax.ShapeDtypeStruct(dims, dtype)


def call(kernel, outs, specs, scratch=(), flops=0, moved=0):
    return pl.pallas_call(
        kernel,
        out_shape=outs,
        in_specs=specs,
        out_specs=jax.tree.map(lambda _: whole(), outs),
        scratch_shapes=list(scratch),
        compiler_params=pltpu.CompilerParams(vmem_limit_bytes=VMEM_LIMIT),
        cost_estimate=pl.CostEstimate(flops=flops, bytes_accessed=moved, transcendentals=0),
    )


def split_rows(source_ref, ready, packed_ref, high_ref, low_ref, out_ref):
    half, block = source_ref.shape[0], source_ref.shape[1]
    group = max(1, half // 2)
    for first in range(0, half, group):
        for k in range(first, first + group):
            ready(k)
            high, low = split(source_ref[k])
            high_ref[k * block : (k + 1) * block] = high
            low_ref[k * block : (k + 1) * block] = low
        rows = slice(first * block, (first + group) * block)
        total = wide_dot(high_ref[rows], low_ref[rows], packed_ref[...])
        out_ref[first : first + group] = total.reshape((group,) + out_ref.shape[1:])


def first_kernel(dosage_ref, coef_ref, high_ref, low_ref, out_ref, packed_ref, kept_ref, buffer_ref, coef_buffer, sems):
    me = lax.axis_index("chrom")
    place, core = me // 2, me % 2
    half = buffer_ref.shape[0]
    coef_copy = pltpu.make_async_copy(coef_ref, coef_buffer, sems.at[2 * half * PARTS])
    part = buffer_ref.shape[1] // PARTS
    copies = [
        [
            pltpu.make_async_copy(
                dosage_ref.at[place ^ k, core ^ bits, pl.ds(p * part, part)],
                target.at[k, pl.ds(p * part, part)],
                sems.at[(bits * half + k) * PARTS + p],
            )
            for p in range(PARTS)
        ]
        for bits, target in ((1, buffer_ref), (0, kept_ref))
        for k in range(half)
    ]
    coef_copy.start()
    for group in copies:
        for copy in group:
            copy.start()

    def ready(k):
        for copy in copies[k]:
            copy.wait()

    coef_copy.wait()
    packed_ref[...] = pack(coef_buffer[...])
    split_rows(buffer_ref, ready, packed_ref, high_ref, low_ref, out_ref)
    for group in copies[half:]:
        for copy in group:
            copy.wait()


def second_kernel(kept_ref, packed_ref, high_ref, low_ref, out_ref):
    split_rows(kept_ref, lambda k: None, packed_ref, high_ref, low_ref, out_ref)


def square_kernel(tested_ref, square_ref):
    for place in range(square_ref.shape[0]):
        width = square_ref.shape[1] * square_ref.shape[2]
        value = tested_ref[:, place * width : (place + 1) * width].astype(jnp.float32)
        square_ref[place] = jnp.sum(value * value, axis=0).reshape(square_ref.shape[1:])


def column(row):
    down = lax.broadcasted_iota(jnp.int32, (128, 128), 0)
    across = lax.broadcasted_iota(jnp.int32, (128, 128), 1)
    return jnp.sum(jnp.where(down == across, row, 0.0), axis=1, keepdims=True)


def columns(ref):
    return jnp.concatenate([column(ref[k : k + 1]) for k in range(ref.shape[0])])


def rest_kernel(high_ref, low_ref, packed_ref, out_ref):
    out_ref[...] = wide_dot(high_ref[...], low_ref[...], packed_ref[...]).reshape(out_ref.shape)


def residual_kernel(count, traits_ref, *refs):
    out = refs[-1]
    block = out.shape[0]
    total = refs[0][...]
    for piece in refs[1:count]:
        total = total + piece[...]
    start = pl.multiple_of(lax.axis_index("chrom") * block, block)
    out[...] = traits_ref[pl.ds(start, block)] - total


def grad_dot(packed_ref, parts, which, width):
    half = packed_ref.shape[1] // 2
    cols = pl.ds(pl.multiple_of(which * width, width), width)
    total = None
    for place, part in enumerate(parts):
        left = packed_ref[:, (place // 2) * half : (place // 2 + 1) * half]
        term = jnp.dot(left, part[:, cols], preferred_element_type=jnp.float32)
        total = term if total is None else total + term
    traits = packed_ref.shape[0] // 2
    return (total[:traits] + total[traits:]).T


def grad_far_kernel(count, partners, *refs):
    pieces, parts, (packed_ref, *outs) = refs[:count], refs[count : count + 4], refs[count + 4 : -1]
    rows_ref = refs[-1]
    samp = lax.axis_index("samp")
    block = pieces[0].shape[0]
    for bits, piece in zip(chrom_order(count), pieces):
        start = ((bits % 2) * (count // 2) + bits // 2) * block
        rows_ref[start : start + block] = pack(piece[...])
    packed_ref[...] = rows_ref[...].T
    for partner, out in zip(partners, outs):
        out[...] = grad_dot(packed_ref, parts, samp ^ partner, out.shape[0])


def grad_near_kernel(partners, *refs):
    packed_ref, parts, outs = refs[0], refs[1:5], refs[5:]
    samp = lax.axis_index("samp")
    for partner, out in zip(partners, outs):
        out[...] = grad_dot(packed_ref, parts, samp ^ partner, out.shape[0])


def image_kernel(count, *refs):
    pieces = refs[:count]
    high_ref, low_ref = refs[count : count + 2]
    grad_ref, packed_ref, give_ref = refs[-3:]
    samp = lax.axis_index("samp")
    block = pieces[0].shape[0]
    for bits, piece in enumerate(pieces):
        rows = pl.ds(pl.multiple_of((samp ^ bits) * block, block), block)
        value = piece[...]
        grad_ref[rows] = value
        packed_ref[rows] = pack(value)
    rest_kernel(high_ref, low_ref, packed_ref, give_ref)


def norm_kernel(count, *refs):
    grad_ref, pieces, out = refs[0], refs[1 : count + 1], refs[-1]
    total = pieces[0][...]
    for piece in pieces[1:]:
        total = total + piece[...]
    grad = grad_ref[...]
    grad_sq = jnp.sum(grad * grad, axis=0, keepdims=True)
    image_sq = jnp.sum(total * total, axis=0, keepdims=True)
    sums = jnp.concatenate([grad_sq, image_sq])
    for place in range(out.shape[0]):
        out[place] = sums


def prox_kernel(total_rows, coef_ref, grad_ref, sums_ref, high_ref, low_ref, new_ref, packed_ref, give_ref):
    sums = sums_ref[0]
    for place in range(1, sums_ref.shape[0]):
        sums = sums + sums_ref[place]
    grad_sq = jnp.sum(sums[0:1], axis=1, keepdims=True)
    image_sq = jnp.sum(sums[1:2], axis=1, keepdims=True)
    step_size = grad_sq / (image_sq / total_rows + 1e-06)
    penalty = 1.5 * math.sqrt(coef_ref.shape[1] / total_rows)
    moved = coef_ref[...] + step_size * grad_ref[...]
    length = jnp.sqrt(jnp.sum(moved * moved, axis=1, keepdims=True))
    cut = step_size * penalty
    new = moved * (jnp.maximum(length - cut, 0.0) / jnp.maximum(length, cut))
    new_ref[...] = new
    packed_ref[...] = pack(new)
    rest_kernel(high_ref, low_ref, packed_ref, give_ref)


def own_kernel(coef_ref, group_ref, *refs):
    parts, outs = refs[:4], refs[4:]
    coef = coef_ref[...]
    base = lax.axis_index("chrom") * GPD
    local = columns((group_ref[...] - base).astype(jnp.float32))
    half = parts[0].shape[0]
    for which, out in enumerate(outs):
        packed = pack(jnp.where(local == which, coef, 0.0))
        out[0:half] = wide_dot(parts[0][...], parts[1][...], packed)
        out[half:] = wide_dot(parts[2][...], parts[3][...], packed)


def score_products(partner, out, tested_ref, square_ref, owner_ref, loco_ref, sums_ref):
    width, traits = out.shape[0] - STATS, out.shape[1]
    cols = pl.ds(pl.multiple_of(partner * width, width), width)
    products = jnp.dot(loco_ref[...], tested_ref[:, cols], preferred_element_type=jnp.float32)
    local = owner_ref[partner] - lax.axis_index("chrom") * GPD
    chosen = products[:traits]
    for which in range(1, GPD):
        chosen = jnp.where(local == which, products[which * traits : (which + 1) * traits], chosen)
    out[0:width] = chosen.T
    out[width : width + 8] = sums_ref[...]
    out[width + 8 : width + STATS] = jnp.zeros((STATS - 8, traits), jnp.float32)
    out[width + 8 : width + 8 + square_ref.shape[1]] = square_ref[partner]


def loco_kernel(count, partners, *refs):
    pieces, own_refs = refs[:count], refs[count : count + GPD]
    tested_ref, square_ref, owner_ref, loco_ref, sums_ref = refs[count + GPD : count + GPD + 5]
    outs, rows_ref = refs[count + GPD + 5 : -1], refs[-1]
    me, samp = lax.axis_index("chrom"), lax.axis_index("samp")
    block, traits = pieces[0].shape
    sums_ref[...] = jnp.zeros_like(sums_ref)
    for bits, piece in zip(chrom_order(count), pieces):
        rows = pl.ds(pl.multiple_of((me ^ bits) * block, block), block)
        start = ((bits % 2) * (count // 2) + bits // 2) * block
        value = piece[...]
        for which in range(GPD):
            loco = value + own_refs[which][start : start + block]
            sums_ref[which : which + 1] += jnp.sum(loco * loco, axis=0, keepdims=True)
            rows_ref[rows, which * traits : (which + 1) * traits] = loco.astype(jnp.bfloat16)
    loco_ref[...] = rows_ref[...].T
    for partner, out in zip(partners, outs):
        score_products(samp ^ partner, out, tested_ref, square_ref, owner_ref, loco_ref, sums_ref)


def loco_near_kernel(count, partners, *refs):
    pieces, operands, residual_ref, outs = refs[:count], refs[count : count + 5], refs[count + 5], refs[count + 6 :]
    me, samp = lax.axis_index("chrom"), lax.axis_index("samp")
    block = pieces[0].shape[0]
    for bits, piece in zip(chrom_order(count), pieces):
        residual_ref[pl.ds(pl.multiple_of((me ^ bits) * block, block), block)] = piece[...]
    for partner, out in zip(partners, outs):
        score_products(samp ^ partner, out, *operands)


def score_kernel(total_rows, owner_ref, *refs):
    pieces, out = refs[:-1], refs[-1]
    total = pieces[0][...]
    for piece in pieces[1:]:
        total = total + piece[...]
    cols, traits = out.shape
    base = lax.axis_index("chrom") * GPD
    owner = (owner_ref[lax.axis_index("samp")] - base).astype(jnp.float32)
    local = jnp.concatenate([column(owner[:, k * 128 : (k + 1) * 128]) for k in range(cols // 128)])
    loco_sq = jnp.broadcast_to(total[cols : cols + 1], (cols, traits))
    for which in range(1, GPD):
        loco_sq = jnp.where(local == which, total[cols + which : cols + which + 1], loco_sq)
    tested_sq = columns(total[cols + 8 : cols + 8 + cols // 128])
    denom = math.sqrt(total_rows) * jnp.sqrt((tested_sq / total_rows + 1e-06) * (loco_sq / total_rows + 1e-06))
    out[...] = total[:cols] / denom


def place_kernel(*refs):
    pieces, out = refs[:-1], refs[-1]
    samp = lax.axis_index("samp")
    block = pieces[0].shape[0]
    for bits, piece in enumerate(pieces):
        out[pl.ds(pl.multiple_of((samp ^ bits) * block, block), block)] = piece[...]


def chip_kernel(keep_ref, got_ref, *outs):
    for k, out in enumerate(outs):
        out[...] = keep_ref[k] + got_ref[k]


def mean_kernel(total_rows, *refs):
    total = refs[0][...]
    for piece in refs[1:-1]:
        total = total + piece[...]
    refs[-1][...] = total / total_rows


def chrom_scatter(give, keep):
    got = swap(give, "chrom", 1)
    count = keep.shape[0]
    sums = call(chip_kernel, [shape(keep.shape[1:])] * count, [whole()] * 2)(keep, got)
    return [sums[0]] + [swap(sums[k], "chrom", 2 * k) for k in reversed(range(1, count))]


def chrom_order(size):
    return list(reversed(range(size)))


def chrom_gather(own):
    size = lax.axis_size("chrom")
    direct = {bits: swap(own, "chrom", bits) for bits in chrom_order(size)[:-1] if bits < 4 or bits % 2 == 0}
    direct[0] = own
    return [direct[bits] if bits in direct else swap(direct[bits - 1], "chrom", 1) for bits in chrom_order(size)]


def samp_order(size):
    return list(reversed(range(size)))


def samp_gather(own):
    size = lax.axis_size("samp")
    return [own] + [swap(own, "samp", k) for k in samp_order(size)[:-1]][::-1]


def body(dosages, traits, start_coef, groups, tested, owners):
    n_samp, n_chrom = lax.axis_size("samp"), lax.axis_size("chrom")
    rows, cols = dosages.shape
    tests, n_traits = tested.shape[1], traits.shape[1]
    total_rows = rows * n_samp
    half, block, width, test_width = n_chrom // 2, rows // n_chrom, cols // n_samp, tests // n_samp
    flops = 4 * rows * cols * n_traits
    moved = 2 * rows * cols
    order = samp_order(n_samp)
    far, near = order[:-1], order[-1:]

    part = shape((rows // 2, cols), jnp.bfloat16)
    half_out = shape((half, block, n_traits))
    packed_cols = shape((cols, 2 * n_traits), jnp.bfloat16)
    packed_rows = shape((2 * n_traits, rows), jnp.bfloat16)
    rows_buffer = [pltpu.VMEM((rows, 2 * n_traits), jnp.bfloat16)]
    grad_block = shape((width, n_traits))
    score_block = shape((test_width + STATS, n_traits))
    coef_out = shape((cols, n_traits))
    group_rows = groups.reshape(cols // 128, 128)
    owner_rows = owners.reshape(n_samp, 1, test_width)

    def rest(high, low, packed):
        return call(rest_kernel, half_out, [whole()] * 3, (), flops, moved)(high, low, packed)

    def own_residual(summands, after=()):
        return call(
            functools.partial(residual_kernel, len(summands)),
            shape((block, n_traits)),
            [whole()] * (1 + len(summands)) + [anywhere()] * len(after),
        )(traits, *summands, *after)

    coefficients = start_coef
    kept_shape = (half, block, cols)
    high1, low1, give, packed, kept = call(
        first_kernel,
        [part, part, half_out, packed_cols, shape(kept_shape)],
        [pl.BlockSpec(memory_space=pltpu.HBM)] * 2,
        [pltpu.VMEM(kept_shape, jnp.float32), pltpu.VMEM(coefficients.shape, jnp.float32), pltpu.SemaphoreType.DMA((n_chrom * PARTS + 1,))],
        flops,
        4 * moved,
    )(
        pltpu.with_memory_space_constraint(dosages.reshape(half, 2, block, cols), pltpu.HBM),
        pltpu.with_memory_space_constraint(coefficients, pltpu.HBM),
    )
    high0, low0, keep = call(second_kernel, [part, part, half_out], [whole()] * 2, (), flops, moved)(kept, packed)
    summands = chrom_scatter(give, keep)
    parts = [high0, low0, high1, low1]
    tested_sq = call(square_kernel, shape((n_samp, test_width // 128, 128)), [whole()], (), 0, 2 * rows * tests)(tested)

    for iteration in range(ITERS):
        own = own_residual(summands)
        pieces = chrom_gather(own)
        packed, *far_out = call(
            functools.partial(grad_far_kernel, n_chrom, far),
            [packed_rows] + [grad_block] * len(far),
            [whole()] * (n_chrom + 4),
            rows_buffer,
            flops,
            moved,
        )(*pieces, *parts)
        near_out = call(
            functools.partial(grad_near_kernel, near), [grad_block] * len(near), [whole()] * 5, (), flops, moved
        )(packed, *parts)
        received = [swap(piece, "samp", partner) for partner, piece in zip(order, far_out)]
        own_grad = call(functools.partial(mean_kernel, total_rows), grad_block, [whole()] * n_samp)(
            near_out[-1], *received[::-1]
        )
        pieces = samp_gather(own_grad)
        after = (tested_sq,) if iteration == 0 else ()
        gradient, packed, give = call(
            functools.partial(image_kernel, n_samp),
            [coef_out, packed_cols, half_out],
            [whole()] * (n_samp + 2) + [anywhere()] * len(after),
            (),
            flops,
            moved,
        )(*pieces, high1, low1, *after)
        summands = chrom_scatter(give, rest(high0, low0, packed))
        size = n_samp * n_chrom
        sums = call(
            functools.partial(norm_kernel, half), shape((size, 2, n_traits)), [whole()] * (half + 1)
        )(own_grad, *summands)
        sums = lax.all_to_all(sums, ("samp", "chrom"), 0, 0)
        coefficients, packed, give = call(
            functools.partial(prox_kernel, total_rows),
            [coef_out, packed_cols, half_out],
            [whole()] * 5,
            (),
            flops,
            moved,
        )(coefficients, gradient, sums, high1, low1)
        summands = chrom_scatter(give, rest(high0, low0, packed))

    own_parts = call(own_kernel, [shape((rows, n_traits))] * GPD, [whole()] * 6, (), 4 * flops, 4 * moved)(
        coefficients, group_rows, *parts
    )
    pieces = chrom_gather(own_residual(summands, own_parts))
    loco, loco_sq, *far_out = call(
        functools.partial(loco_kernel, n_chrom, far),
        [shape((GPD * n_traits, rows), jnp.bfloat16), shape((8, n_traits))]
        + [score_block] * len(far),
        [whole()] * (n_chrom + GPD + 3),
        [pltpu.VMEM((rows, GPD * n_traits), jnp.bfloat16)],
        flops,
        moved,
    )(*pieces, *own_parts, tested, tested_sq, owner_rows)
    residual, *near_out = call(
        functools.partial(loco_near_kernel, n_chrom, near),
        [shape((rows, n_traits))] + [score_block] * len(near),
        [whole()] * (n_chrom + 5),
        (),
        flops // 2,
        moved,
    )(*pieces, tested, tested_sq, owner_rows, loco, loco_sq)
    received = [swap(piece, "samp", partner) for partner, piece in zip(order, far_out)]
    own_scores = call(
        functools.partial(score_kernel, total_rows), shape((test_width, n_traits)), [whole()] * (n_samp + 1)
    )(owner_rows, near_out[-1], *received[::-1])
    scores = call(place_kernel, shape((tests, n_traits)), [whole()] * n_samp)(*samp_gather(own_scores))
    return (scores, residual)


def solution(mesh):
    placed = (
        P("samp", "chrom"),
        P("samp", None),
        P("chrom", None),
        P("chrom"),
        P("samp", "chrom"),
        P("chrom"),
    )
    return jax.shard_map(
        body,
        mesh=mesh,
        in_specs=placed,
        out_specs=(P("chrom", None), P("samp", None)),
        check_vma=False,
    )
```

```python
import functools
import math

import jax
import jax.numpy as jnp
from jax import lax
from jax.experimental import pallas as pl
from jax.experimental.pallas import tpu as pltpu
from jax.sharding import PartitionSpec as P

GPD = 2
ITERS = 2
STATS = 16
PARTS = 2
GIVEN = 2
VMEM_LIMIT = 10 * 1024 * 1024


def swap(value, axis, bits):
    size = lax.axis_size(axis)
    return lax.ppermute(value, axis, [(i, i ^ bits) for i in range(size)])


def split(value):
    high = value.astype(jnp.bfloat16)
    low = (value - high.astype(jnp.float32)).astype(jnp.bfloat16)
    return high, low


def pack(value):
    return jnp.concatenate(split(value), axis=1)


def wide_dot(high, low, packed):
    total = jnp.dot(high, packed, preferred_element_type=jnp.float32)
    total = total + jnp.dot(low, packed, preferred_element_type=jnp.float32)
    traits = packed.shape[1] // 2
    return total[:, :traits] + total[:, traits:]


def whole():
    return pl.BlockSpec(memory_space=pltpu.VMEM)


def anywhere():
    return pl.BlockSpec(memory_space=pl.ANY)


def shape(dims, dtype=jnp.float32):
    return jax.ShapeDtypeStruct(dims, dtype)


def call(kernel, outs, specs, scratch=(), flops=0, moved=0):
    return pl.pallas_call(
        kernel,
        out_shape=outs,
        in_specs=specs,
        out_specs=jax.tree.map(lambda _: whole(), outs),
        scratch_shapes=list(scratch),
        compiler_params=pltpu.CompilerParams(vmem_limit_bytes=VMEM_LIMIT),
        cost_estimate=pl.CostEstimate(flops=flops, bytes_accessed=moved, transcendentals=0),
    )


def store_places(total, out_refs, first=0):
    block = out_refs[0].shape[1]
    for k in range(total.shape[0] // block):
        place = first + k
        for out in out_refs:
            if 0 <= place < out.shape[0]:
                out[place] = total[k * block : (k + 1) * block]
            place -= out.shape[0]


def split_rows(source_ref, ready, packed_ref, high_ref, low_ref, out_refs):
    half, block = source_ref.shape[0], source_ref.shape[1]
    group = max(1, half // 2)
    for first in range(0, half, group):
        for k in range(first, first + group):
            ready(k)
            high, low = split(source_ref[k])
            high_ref[k * block : (k + 1) * block] = high
            low_ref[k * block : (k + 1) * block] = low
        rows = slice(first * block, (first + group) * block)
        total = wide_dot(high_ref[rows], low_ref[rows], packed_ref[...])
        store_places(total, out_refs, first)


def first_kernel(dosage_ref, coef_ref, high_ref, low_ref, *refs):
    *out_refs, packed_ref, kept_ref, buffer_ref, coef_buffer, sems = refs
    me = lax.axis_index("chrom")
    place, core = me // 2, me % 2
    half = buffer_ref.shape[0]
    coef_copy = pltpu.make_async_copy(coef_ref, coef_buffer, sems.at[2 * half * PARTS])
    part = buffer_ref.shape[1] // PARTS
    copies = [
        [
            pltpu.make_async_copy(
                dosage_ref.at[place ^ k, core ^ bits, pl.ds(p * part, part)],
                target.at[k, pl.ds(p * part, part)],
                sems.at[(bits * half + k) * PARTS + p],
            )
            for p in range(PARTS)
        ]
        for bits, target in ((1, buffer_ref), (0, kept_ref))
        for k in range(half)
    ]
    coef_copy.start()
    for group in copies:
        for copy in group:
            copy.start()

    def ready(k):
        for copy in copies[k]:
            copy.wait()

    coef_copy.wait()
    packed_ref[...] = pack(coef_buffer[...])
    split_rows(buffer_ref, ready, packed_ref, high_ref, low_ref, out_refs)
    for group in copies[half:]:
        for copy in group:
            copy.wait()


def second_kernel(kept_ref, packed_ref, high_ref, low_ref, out_ref):
    split_rows(kept_ref, lambda k: None, packed_ref, high_ref, low_ref, [out_ref])


def square_kernel(tested_ref, square_ref):
    for place in range(square_ref.shape[0]):
        width = square_ref.shape[1] * square_ref.shape[2]
        value = tested_ref[:, place * width : (place + 1) * width].astype(jnp.float32)
        square_ref[place] = jnp.sum(value * value, axis=0).reshape(square_ref.shape[1:])


def column(row):
    down = lax.broadcasted_iota(jnp.int32, (128, 128), 0)
    across = lax.broadcasted_iota(jnp.int32, (128, 128), 1)
    return jnp.sum(jnp.where(down == across, row, 0.0), axis=1, keepdims=True)


def columns(ref):
    return jnp.concatenate([column(ref[k : k + 1]) for k in range(ref.shape[0])])


def rest_kernel(high_ref, low_ref, packed_ref, *out_refs):
    store_places(wide_dot(high_ref[...], low_ref[...], packed_ref[...]), out_refs)


def residual_kernel(count, traits_ref, *refs):
    out = refs[-1]
    block = out.shape[0]
    total = refs[0][...]
    for piece in refs[1:count]:
        total = total + piece[...]
    start = pl.multiple_of(lax.axis_index("chrom") * block, block)
    out[...] = traits_ref[pl.ds(start, block)] - total


def grad_dot(packed_ref, parts, which, width):
    half = packed_ref.shape[1] // 2
    cols = pl.ds(pl.multiple_of(which * width, width), width)
    total = None
    for place, part in enumerate(parts):
        left = packed_ref[:, (place // 2) * half : (place // 2 + 1) * half]
        term = jnp.dot(left, part[:, cols], preferred_element_type=jnp.float32)
        total = term if total is None else total + term
    traits = packed_ref.shape[0] // 2
    return (total[:traits] + total[traits:]).T


def grad_far_kernel(count, partners, *refs):
    pieces, parts, (packed_ref, *outs) = refs[:count], refs[count : count + 4], refs[count + 4 : -1]
    rows_ref = refs[-1]
    samp = lax.axis_index("samp")
    block = pieces[0].shape[0]
    for bits, piece in zip(chrom_order(count), pieces):
        start = ((bits % 2) * (count // 2) + bits // 2) * block
        rows_ref[start : start + block] = pack(piece[...])
    packed_ref[...] = rows_ref[...].T
    for partner, out in zip(partners, outs):
        out[...] = grad_dot(packed_ref, parts, samp ^ partner, out.shape[0])


def grad_near_kernel(partners, *refs):
    packed_ref, parts, outs = refs[0], refs[1:5], refs[5:]
    samp = lax.axis_index("samp")
    for partner, out in zip(partners, outs):
        out[...] = grad_dot(packed_ref, parts, samp ^ partner, out.shape[0])


def image_kernel(count, *refs):
    pieces = refs[:count]
    high_ref, low_ref = refs[count : count + 2]
    grad_ref, packed_ref, *give_refs = refs[-2 - GIVEN :]
    samp = lax.axis_index("samp")
    block = pieces[0].shape[0]
    for bits, piece in enumerate(pieces):
        rows = pl.ds(pl.multiple_of((samp ^ bits) * block, block), block)
        value = piece[...]
        grad_ref[rows] = value
        packed_ref[rows] = pack(value)
    rest_kernel(high_ref, low_ref, packed_ref, *give_refs)


def norm_kernel(count, *refs):
    grad_ref, pieces, out = refs[0], refs[1 : count + 1], refs[-1]
    total = pieces[0][...]
    for piece in pieces[1:]:
        total = total + piece[...]
    grad = grad_ref[...]
    grad_sq = jnp.sum(grad * grad, axis=0, keepdims=True)
    image_sq = jnp.sum(total * total, axis=0, keepdims=True)
    sums = jnp.concatenate([grad_sq, image_sq])
    for place in range(out.shape[0]):
        out[place] = sums


def prox_kernel(total_rows, coef_ref, grad_ref, sums_ref, high_ref, low_ref, new_ref, packed_ref, *give_refs):
    sums = sums_ref[0]
    for place in range(1, sums_ref.shape[0]):
        sums = sums + sums_ref[place]
    grad_sq = jnp.sum(sums[0:1], axis=1, keepdims=True)
    image_sq = jnp.sum(sums[1:2], axis=1, keepdims=True)
    step_size = grad_sq / (image_sq / total_rows + 1e-06)
    penalty = 1.5 * math.sqrt(coef_ref.shape[1] / total_rows)
    moved = coef_ref[...] + step_size * grad_ref[...]
    length = jnp.sqrt(jnp.sum(moved * moved, axis=1, keepdims=True))
    cut = step_size * penalty
    new = moved * (jnp.maximum(length - cut, 0.0) / jnp.maximum(length, cut))
    new_ref[...] = new
    packed_ref[...] = pack(new)
    rest_kernel(high_ref, low_ref, packed_ref, *give_refs)


def own_kernel(coef_ref, group_ref, *refs):
    parts, outs = refs[:4], refs[4:]
    coef = coef_ref[...]
    base = lax.axis_index("chrom") * GPD
    local = columns((group_ref[...] - base).astype(jnp.float32))
    half = parts[0].shape[0]
    for which, out in enumerate(outs):
        packed = pack(jnp.where(local == which, coef, 0.0))
        out[0:half] = wide_dot(parts[0][...], parts[1][...], packed)
        out[half:] = wide_dot(parts[2][...], parts[3][...], packed)


def score_products(partner, out, tested_ref, square_ref, owner_ref, loco_ref, sums_ref):
    width, traits = out.shape[0] - STATS, out.shape[1]
    cols = pl.ds(pl.multiple_of(partner * width, width), width)
    products = jnp.dot(loco_ref[...], tested_ref[:, cols], preferred_element_type=jnp.float32)
    local = owner_ref[partner] - lax.axis_index("chrom") * GPD
    chosen = products[:traits]
    for which in range(1, GPD):
        chosen = jnp.where(local == which, products[which * traits : (which + 1) * traits], chosen)
    out[0:width] = chosen.T
    out[width : width + 8] = sums_ref[...]
    out[width + 8 : width + STATS] = jnp.zeros((STATS - 8, traits), jnp.float32)
    out[width + 8 : width + 8 + square_ref.shape[1]] = square_ref[partner]


def loco_kernel(count, partners, *refs):
    pieces, own_refs = refs[:count], refs[count : count + GPD]
    tested_ref, square_ref, owner_ref, loco_ref, sums_ref = refs[count + GPD : count + GPD + 5]
    outs, rows_ref = refs[count + GPD + 5 : -1], refs[-1]
    me, samp = lax.axis_index("chrom"), lax.axis_index("samp")
    block, traits = pieces[0].shape
    sums_ref[...] = jnp.zeros_like(sums_ref)
    for bits, piece in zip(chrom_order(count), pieces):
        rows = pl.ds(pl.multiple_of((me ^ bits) * block, block), block)
        start = ((bits % 2) * (count // 2) + bits // 2) * block
        value = piece[...]
        for which in range(GPD):
            loco = value + own_refs[which][start : start + block]
            sums_ref[which : which + 1] += jnp.sum(loco * loco, axis=0, keepdims=True)
            rows_ref[rows, which * traits : (which + 1) * traits] = loco.astype(jnp.bfloat16)
    loco_ref[...] = rows_ref[...].T
    for partner, out in zip(partners, outs):
        score_products(samp ^ partner, out, tested_ref, square_ref, owner_ref, loco_ref, sums_ref)


def loco_near_kernel(count, partners, *refs):
    pieces, operands, residual_ref, outs = refs[:count], refs[count : count + 5], refs[count + 5], refs[count + 6 :]
    me, samp = lax.axis_index("chrom"), lax.axis_index("samp")
    block = pieces[0].shape[0]
    for bits, piece in zip(chrom_order(count), pieces):
        residual_ref[pl.ds(pl.multiple_of((me ^ bits) * block, block), block)] = piece[...]
    for partner, out in zip(partners, outs):
        score_products(samp ^ partner, out, *operands)


def score_kernel(total_rows, owner_ref, *refs):
    pieces, out = refs[:-1], refs[-1]
    total = pieces[0][...]
    for piece in pieces[1:]:
        total = total + piece[...]
    cols, traits = out.shape
    base = lax.axis_index("chrom") * GPD
    owner = (owner_ref[lax.axis_index("samp")] - base).astype(jnp.float32)
    local = jnp.concatenate([column(owner[:, k * 128 : (k + 1) * 128]) for k in range(cols // 128)])
    loco_sq = jnp.broadcast_to(total[cols : cols + 1], (cols, traits))
    for which in range(1, GPD):
        loco_sq = jnp.where(local == which, total[cols + which : cols + which + 1], loco_sq)
    tested_sq = columns(total[cols + 8 : cols + 8 + cols // 128])
    denom = math.sqrt(total_rows) * jnp.sqrt((tested_sq / total_rows + 1e-06) * (loco_sq / total_rows + 1e-06))
    out[...] = total[:cols] / denom


def place_kernel(*refs):
    pieces, out, sems = refs[:-2], refs[-2], refs[-1]
    samp = lax.axis_index("samp")
    block = pieces[0].shape[0]
    copies = [
        pltpu.make_async_copy(
            piece, out.at[pl.ds(pl.multiple_of((samp ^ bits) * block, block), block)], sems.at[bits]
        )
        for bits, piece in enumerate(pieces)
    ]
    for copy in copies:
        copy.start()
    for copy in copies:
        copy.wait()


def chip_kernel(first, keep_ref, got_ref, *outs):
    for k, out in enumerate(outs):
        out[...] = keep_ref[first + k] + got_ref[k]


def mean_kernel(total_rows, *refs):
    total = refs[0][...]
    for piece in refs[1:-1]:
        total = total + piece[...]
    refs[-1][...] = total / total_rows


def chrom_scatter(gives, keep):
    sums, first = [], keep.shape[0]
    for part in gives[::-1]:
        count = part.shape[0]
        first -= count
        kernel = functools.partial(chip_kernel, first)
        sums = list(call(kernel, [shape(keep.shape[1:])] * count, [whole()] * 2)(keep, swap(part, "chrom", 1))) + sums
    return [sums[0]] + [swap(sums[k], "chrom", 2 * k) for k in reversed(range(1, len(sums)))]


def chrom_order(size):
    return list(reversed(range(size)))


def chrom_gather(own):
    size = lax.axis_size("chrom")
    direct = {bits: swap(own, "chrom", bits) for bits in chrom_order(size)[:-1] if bits < 4 or bits % 2 == 0}
    direct[0] = own
    return [direct[bits] if bits in direct else swap(direct[bits - 1], "chrom", 1) for bits in chrom_order(size)]


def samp_order(size):
    return list(reversed(range(size)))


def samp_gather(own):
    size = lax.axis_size("samp")
    return [own] + [swap(own, "samp", k) for k in samp_order(size)[:-1]][::-1]


def body(dosages, traits, start_coef, groups, tested, owners):
    n_samp, n_chrom = lax.axis_size("samp"), lax.axis_size("chrom")
    rows, cols = dosages.shape
    tests, n_traits = tested.shape[1], traits.shape[1]
    total_rows = rows * n_samp
    half, block, width, test_width = n_chrom // 2, rows // n_chrom, cols // n_samp, tests // n_samp
    flops = 4 * rows * cols * n_traits
    moved = 2 * rows * cols
    order = samp_order(n_samp)
    far, near = order[:-1], order[-1:]

    part = shape((rows // 2, cols), jnp.bfloat16)
    half_out = shape((half, block, n_traits))
    give_outs = [shape((count, block, n_traits)) for count in (half // 2, half - half // 2)]
    packed_cols = shape((cols, 2 * n_traits), jnp.bfloat16)
    packed_rows = shape((2 * n_traits, rows), jnp.bfloat16)
    rows_buffer = [pltpu.VMEM((rows, 2 * n_traits), jnp.bfloat16)]
    grad_block = shape((width, n_traits))
    score_block = shape((test_width + STATS, n_traits))
    coef_out = shape((cols, n_traits))
    group_rows = groups.reshape(cols // 128, 128)
    owner_rows = owners.reshape(n_samp, 1, test_width)

    def rest(high, low, packed):
        return call(rest_kernel, half_out, [whole()] * 3, (), flops, moved)(high, low, packed)

    def own_residual(summands, after=()):
        return call(
            functools.partial(residual_kernel, len(summands)),
            shape((block, n_traits)),
            [whole()] * (1 + len(summands)) + [anywhere()] * len(after),
        )(traits, *summands, *after)

    coefficients = start_coef
    kept_shape = (half, block, cols)
    high1, low1, *gives, packed, kept = call(
        first_kernel,
        [part, part] + give_outs + [packed_cols, shape(kept_shape)],
        [pl.BlockSpec(memory_space=pltpu.HBM)] * 2,
        [pltpu.VMEM(kept_shape, jnp.float32), pltpu.VMEM(coefficients.shape, jnp.float32), pltpu.SemaphoreType.DMA((n_chrom * PARTS + 1,))],
        flops,
        4 * moved,
    )(
        pltpu.with_memory_space_constraint(dosages.reshape(half, 2, block, cols), pltpu.HBM),
        pltpu.with_memory_space_constraint(coefficients, pltpu.HBM),
    )
    high0, low0, keep = call(second_kernel, [part, part, half_out], [whole()] * 2, (), flops, moved)(kept, packed)
    summands = chrom_scatter(gives, keep)
    parts = [high0, low0, high1, low1]
    tested_sq = call(square_kernel, shape((n_samp, test_width // 128, 128)), [whole()], (), 0, 2 * rows * tests)(tested)

    for iteration in range(ITERS):
        own = own_residual(summands)
        pieces = chrom_gather(own)
        packed, *far_out = call(
            functools.partial(grad_far_kernel, n_chrom, far),
            [packed_rows] + [grad_block] * len(far),
            [whole()] * (n_chrom + 4),
            rows_buffer,
            flops,
            moved,
        )(*pieces, *parts)
        near_out = call(
            functools.partial(grad_near_kernel, near), [grad_block] * len(near), [whole()] * 5, (), flops, moved
        )(packed, *parts)
        received = [swap(piece, "samp", partner) for partner, piece in zip(order, far_out)]
        own_grad = call(functools.partial(mean_kernel, total_rows), grad_block, [whole()] * n_samp)(
            near_out[-1], *received[::-1]
        )
        pieces = samp_gather(own_grad)
        after = (tested_sq,) if iteration == 0 else ()
        gradient, packed, *gives = call(
            functools.partial(image_kernel, n_samp),
            [coef_out, packed_cols] + give_outs,
            [whole()] * (n_samp + 2) + [anywhere()] * len(after),
            (),
            flops,
            moved,
        )(*pieces, high1, low1, *after)
        summands = chrom_scatter(gives, rest(high0, low0, packed))
        size = n_samp * n_chrom
        sums = call(
            functools.partial(norm_kernel, half), shape((size, 2, n_traits)), [whole()] * (half + 1)
        )(own_grad, *summands)
        sums = lax.all_to_all(sums, ("samp", "chrom"), 0, 0)
        coefficients, packed, *gives = call(
            functools.partial(prox_kernel, total_rows),
            [coef_out, packed_cols] + give_outs,
            [whole()] * 5,
            (),
            flops,
            moved,
        )(coefficients, gradient, sums, high1, low1)
        summands = chrom_scatter(gives, rest(high0, low0, packed))

    own_parts = call(own_kernel, [shape((rows, n_traits))] * GPD, [whole()] * 6, (), 4 * flops, 4 * moved)(
        coefficients, group_rows, *parts
    )
    pieces = chrom_gather(own_residual(summands, own_parts))
    loco, loco_sq, *far_out = call(
        functools.partial(loco_kernel, n_chrom, far),
        [shape((GPD * n_traits, rows), jnp.bfloat16), shape((8, n_traits))]
        + [score_block] * len(far),
        [whole()] * (n_chrom + GPD + 3),
        [pltpu.VMEM((rows, GPD * n_traits), jnp.bfloat16)],
        flops,
        moved,
    )(*pieces, *own_parts, tested, tested_sq, owner_rows)
    residual, *near_out = call(
        functools.partial(loco_near_kernel, n_chrom, near),
        [shape((rows, n_traits))] + [score_block] * len(near),
        [whole()] * (n_chrom + 5),
        (),
        flops // 2,
        moved,
    )(*pieces, tested, tested_sq, owner_rows, loco, loco_sq)
    received = [swap(piece, "samp", partner) for partner, piece in zip(order, far_out)]
    own_scores = call(
        functools.partial(score_kernel, total_rows), shape((test_width, n_traits)), [whole()] * (n_samp + 1)
    )(owner_rows, near_out[-1], *received[::-1])
    scores = pl.pallas_call(
        place_kernel,
        out_shape=shape((tests, n_traits)),
        in_specs=[whole()] * n_samp,
        out_specs=anywhere(),
        scratch_shapes=[pltpu.SemaphoreType.DMA((n_samp,))],
        compiler_params=pltpu.CompilerParams(vmem_limit_bytes=VMEM_LIMIT),
    )(*samp_gather(own_scores))
    return (scores, residual)


def solution(mesh):
    placed = (
        P("samp", "chrom"),
        P("samp", None),
        P("chrom", None),
        P("chrom"),
        P("samp", "chrom"),
        P("chrom"),
    )
    return jax.shard_map(
        body,
        mesh=mesh,
        in_specs=placed,
        out_specs=(P("chrom", None), P("samp", None)),
        check_vma=False,
    )
```

```python
import functools
import math

import jax
import jax.numpy as jnp
from jax import lax
from jax.experimental import pallas as pl
from jax.experimental.pallas import tpu as pltpu
from jax.sharding import PartitionSpec as P

GPD = 2
ITERS = 2
STATS = 8
PARTS = 2
VMEM_LIMIT = 10 * 1024 * 1024


def swap(value, axis, bits):
    size = lax.axis_size(axis)
    return lax.ppermute(value, axis, [(i, i ^ bits) for i in range(size)])


def split(value):
    high = value.astype(jnp.bfloat16)
    low = (value - high.astype(jnp.float32)).astype(jnp.bfloat16)
    return high, low


def pack(value):
    return jnp.concatenate(split(value), axis=1)


def wide_dot(high, low, packed):
    total = jnp.dot(high, packed, preferred_element_type=jnp.float32)
    total = total + jnp.dot(low, packed, preferred_element_type=jnp.float32)
    traits = packed.shape[1] // 2
    return total[:, :traits] + total[:, traits:]


def whole():
    return pl.BlockSpec(memory_space=pltpu.VMEM)


def anywhere():
    return pl.BlockSpec(memory_space=pl.ANY)


def shape(dims, dtype=jnp.float32):
    return jax.ShapeDtypeStruct(dims, dtype)


def call(kernel, outs, specs, scratch=(), flops=0, moved=0):
    return pl.pallas_call(
        kernel,
        out_shape=outs,
        in_specs=specs,
        out_specs=jax.tree.map(lambda _: whole(), outs),
        scratch_shapes=list(scratch),
        compiler_params=pltpu.CompilerParams(vmem_limit_bytes=VMEM_LIMIT),
        cost_estimate=pl.CostEstimate(flops=flops, bytes_accessed=moved, transcendentals=0),
    )


def store_places(total, out_refs, first=0):
    block = out_refs[0].shape[1]
    for k in range(total.shape[0] // block):
        place = first + k
        for out in out_refs:
            if 0 <= place < out.shape[0]:
                out[place] = total[k * block : (k + 1) * block]
            place -= out.shape[0]


def split_rows(source_ref, ready, packed_ref, high_ref, low_ref, out_refs):
    half, block = source_ref.shape[0], source_ref.shape[1]
    group = max(1, half // 2)
    for first in range(0, half, group):
        for k in range(first, first + group):
            ready(k)
            high, low = split(source_ref[k])
            high_ref[k * block : (k + 1) * block] = high
            low_ref[k * block : (k + 1) * block] = low
        rows = slice(first * block, (first + group) * block)
        total = wide_dot(high_ref[rows], low_ref[rows], packed_ref[...])
        store_places(total, out_refs, first)


def first_kernel(dosage_ref, coef_ref, high_ref, low_ref, *refs):
    *out_refs, packed_ref, kept_ref, buffer_ref, coef_buffer, sems = refs
    me = lax.axis_index("chrom")
    place, core = me // 2, me % 2
    half = buffer_ref.shape[0]
    coef_copy = pltpu.make_async_copy(coef_ref, coef_buffer, sems.at[2 * half * PARTS])
    part = buffer_ref.shape[1] // PARTS
    copies = [
        [
            pltpu.make_async_copy(
                dosage_ref.at[place ^ k, core ^ bits, pl.ds(p * part, part)],
                target.at[k, pl.ds(p * part, part)],
                sems.at[(bits * half + k) * PARTS + p],
            )
            for p in range(PARTS)
        ]
        for bits, target in ((1, buffer_ref), (0, kept_ref))
        for k in range(half)
    ]
    coef_copy.start()
    for group in copies:
        for copy in group:
            copy.start()

    def ready(k):
        for copy in copies[k]:
            copy.wait()

    coef_copy.wait()
    packed_ref[...] = pack(coef_buffer[...])
    split_rows(buffer_ref, ready, packed_ref, high_ref, low_ref, out_refs)
    for group in copies[half:]:
        for copy in group:
            copy.wait()


def second_kernel(kept_ref, packed_ref, high_ref, low_ref, out_ref):
    split_rows(kept_ref, lambda k: None, packed_ref, high_ref, low_ref, [out_ref])


def square_kernel(tested_ref, square_ref):
    for place in range(square_ref.shape[0]):
        width = square_ref.shape[1] * square_ref.shape[2]
        value = tested_ref[:, place * width : (place + 1) * width].astype(jnp.float32)
        square_ref[place] = jnp.sum(value * value, axis=0).reshape(square_ref.shape[1:])


def column(row):
    down = lax.broadcasted_iota(jnp.int32, (128, 128), 0)
    across = lax.broadcasted_iota(jnp.int32, (128, 128), 1)
    return jnp.sum(jnp.where(down == across, row, 0.0), axis=1, keepdims=True)


def columns(ref):
    return jnp.concatenate([column(ref[k : k + 1]) for k in range(ref.shape[0])])


def residual_kernel(count, traits_ref, *refs):
    out = refs[-1]
    block = out.shape[0]
    total = refs[0][...]
    for piece in refs[1:count]:
        total = total + piece[...]
    start = pl.multiple_of(lax.axis_index("chrom") * block, block)
    out[...] = traits_ref[pl.ds(start, block)] - total


def grad_dot(packed_ref, parts, which, width):
    half = packed_ref.shape[1] // 2
    cols = pl.ds(pl.multiple_of(which * width, width), width)
    total = None
    for place, part in enumerate(parts):
        left = packed_ref[:, (place // 2) * half : (place // 2 + 1) * half]
        term = jnp.dot(left, part[:, cols], preferred_element_type=jnp.float32)
        total = term if total is None else total + term
    traits = packed_ref.shape[0] // 2
    return (total[:traits] + total[traits:]).T


def grad_far_kernel(count, partners, *refs):
    pieces, parts, (packed_ref, *outs) = refs[:count], refs[count : count + 4], refs[count + 4 : -1]
    rows_ref = refs[-1]
    samp = lax.axis_index("samp")
    block = pieces[0].shape[0]
    for bits, piece in zip(chrom_order(count), pieces):
        start = ((bits % 2) * (count // 2) + bits // 2) * block
        rows_ref[start : start + block] = pack(piece[...])
    packed_ref[...] = rows_ref[...].T
    for partner, out in zip(partners, outs):
        out[...] = grad_dot(packed_ref, parts, samp ^ partner, out.shape[0])


def grad_near_kernel(partners, *refs):
    packed_ref, parts, outs = refs[0], refs[1:5], refs[5:]
    samp = lax.axis_index("samp")
    for partner, out in zip(partners, outs):
        out[...] = grad_dot(packed_ref, parts, samp ^ partner, out.shape[0])


def image_kernel(count, *refs):
    pieces = refs[:count]
    high_ref, low_ref = refs[count : count + 2]
    grad_ref, packed_ref, far_ref = refs[-3:]
    samp = lax.axis_index("samp")
    block = pieces[0].shape[0]
    for bits, piece in enumerate(pieces):
        rows = pl.ds(pl.multiple_of((samp ^ bits) * block, block), block)
        value = piece[...]
        grad_ref[rows] = value
        packed_ref[rows] = pack(value)
    far_kernel(high_ref, low_ref, packed_ref, far_ref)


def norm_kernel(count, *refs):
    grad_ref, pieces, out = refs[0], refs[1 : count + 1], refs[-1]
    total = pieces[0][...]
    for piece in pieces[1:]:
        total = total + piece[...]
    grad = grad_ref[...]
    grad_sq = jnp.sum(grad * grad, axis=0, keepdims=True)
    image_sq = jnp.sum(total * total, axis=0, keepdims=True)
    sums = jnp.concatenate([grad_sq, image_sq])
    for place in range(out.shape[0]):
        out[place] = sums


def far_kernel(high_ref, low_ref, packed_ref, out_ref):
    rows = pl.ds(high_ref.shape[0] - out_ref.shape[0] * out_ref.shape[1], out_ref.shape[0] * out_ref.shape[1])
    store_places(wide_dot(high_ref[rows], low_ref[rows], packed_ref[...]), [out_ref])


def near_kernel(high1_ref, low1_ref, high0_ref, low0_ref, packed_ref, near_ref, keep_ref):
    rows = pl.ds(0, near_ref.shape[0] * near_ref.shape[1])
    store_places(wide_dot(high1_ref[rows], low1_ref[rows], packed_ref[...]), [near_ref])
    store_places(wide_dot(high0_ref[...], low0_ref[...], packed_ref[...]), [keep_ref])


def prox_kernel(total_rows, coef_ref, grad_ref, sums_ref, high_ref, low_ref, new_ref, packed_ref, far_ref):
    sums = sums_ref[0]
    for place in range(1, sums_ref.shape[0]):
        sums = sums + sums_ref[place]
    grad_sq = jnp.sum(sums[0:1], axis=1, keepdims=True)
    image_sq = jnp.sum(sums[1:2], axis=1, keepdims=True)
    step_size = grad_sq / (image_sq / total_rows + 1e-06)
    penalty = 1.5 * math.sqrt(coef_ref.shape[1] / total_rows)
    moved = coef_ref[...] + step_size * grad_ref[...]
    length = jnp.sqrt(jnp.sum(moved * moved, axis=1, keepdims=True))
    cut = step_size * penalty
    new = moved * (jnp.maximum(length - cut, 0.0) / jnp.maximum(length, cut))
    new_ref[...] = new
    packed_ref[...] = pack(new)
    far_kernel(high_ref, low_ref, packed_ref, far_ref)


def own_kernel(coef_ref, group_ref, *refs):
    parts, outs = refs[:4], refs[4:]
    coef = coef_ref[...]
    base = lax.axis_index("chrom") * GPD
    local = columns((group_ref[...] - base).astype(jnp.float32))
    half = parts[0].shape[0]
    for which, out in enumerate(outs):
        packed = pack(jnp.where(local == which, coef, 0.0))
        out[0:half] = wide_dot(parts[0][...], parts[1][...], packed)
        out[half:] = wide_dot(parts[2][...], parts[3][...], packed)


def score_products(partner, out, tested_ref, square_ref, owner_ref, loco_ref, sums_ref):
    width, traits = out.shape[0] - STATS, out.shape[1]
    cols = pl.ds(pl.multiple_of(partner * width, width), width)
    products = jnp.dot(loco_ref[...], tested_ref[:, cols], preferred_element_type=jnp.float32)
    local = owner_ref[partner] - lax.axis_index("chrom") * GPD
    chosen = products[:traits]
    for which in range(1, GPD):
        chosen = jnp.where(local == which, products[which * traits : (which + 1) * traits], chosen)
    out[0:width] = chosen.T
    out[width : width + STATS] = sums_ref[...]
    out[width + GPD : width + GPD + square_ref.shape[1]] = square_ref[partner]


def loco_kernel(count, partners, *refs):
    pieces, own_refs = refs[:count], refs[count : count + GPD]
    tested_ref, square_ref, owner_ref, loco_ref, sums_ref = refs[count + GPD : count + GPD + 5]
    outs, rows_ref = refs[count + GPD + 5 : -1], refs[-1]
    me, samp = lax.axis_index("chrom"), lax.axis_index("samp")
    block, traits = pieces[0].shape
    sums_ref[...] = jnp.zeros_like(sums_ref)
    for bits, piece in zip(chrom_order(count), pieces):
        rows = pl.ds(pl.multiple_of((me ^ bits) * block, block), block)
        start = ((bits % 2) * (count // 2) + bits // 2) * block
        value = piece[...]
        for which in range(GPD):
            loco = value + own_refs[which][start : start + block]
            sums_ref[which : which + 1] += jnp.sum(loco * loco, axis=0, keepdims=True)
            rows_ref[rows, which * traits : (which + 1) * traits] = loco.astype(jnp.bfloat16)
    loco_ref[...] = rows_ref[...].T
    for partner, out in zip(partners, outs):
        score_products(samp ^ partner, out, tested_ref, square_ref, owner_ref, loco_ref, sums_ref)


def loco_near_kernel(count, partners, *refs):
    pieces, operands, residual_ref, outs = refs[:count], refs[count : count + 5], refs[count + 5], refs[count + 6 :]
    me, samp = lax.axis_index("chrom"), lax.axis_index("samp")
    block = pieces[0].shape[0]
    for bits, piece in zip(chrom_order(count), pieces):
        residual_ref[pl.ds(pl.multiple_of((me ^ bits) * block, block), block)] = piece[...]
    for partner, out in zip(partners, outs):
        score_products(samp ^ partner, out, *operands)


def score_kernel(total_rows, owner_ref, *refs):
    pieces, out = refs[:-1], refs[-1]
    total = pieces[0][...]
    for piece in pieces[1:]:
        total = total + piece[...]
    cols, traits = out.shape
    base = lax.axis_index("chrom") * GPD
    owner = (owner_ref[lax.axis_index("samp")] - base).astype(jnp.float32)
    local = jnp.concatenate([column(owner[:, k * 128 : (k + 1) * 128]) for k in range(cols // 128)])
    loco_sq = jnp.broadcast_to(total[cols : cols + 1], (cols, traits))
    for which in range(1, GPD):
        loco_sq = jnp.where(local == which, total[cols + which : cols + which + 1], loco_sq)
    tested_sq = columns(total[cols + GPD : cols + GPD + cols // 128])
    denom = math.sqrt(total_rows) * jnp.sqrt((tested_sq / total_rows + 1e-06) * (loco_sq / total_rows + 1e-06))
    out[...] = total[:cols] / denom


def place_kernel(*refs):
    pieces, out, sems = refs[:-2], refs[-2], refs[-1]
    samp = lax.axis_index("samp")
    block = pieces[0].shape[0]
    copies = [
        pltpu.make_async_copy(
            piece, out.at[pl.ds(pl.multiple_of((samp ^ bits) * block, block), block)], sems.at[bits]
        )
        for bits, piece in enumerate(pieces)
    ]
    for copy in copies:
        copy.start()
    for copy in copies:
        copy.wait()


def chip_kernel(first, keep_ref, got_ref, *outs):
    for k, out in enumerate(outs):
        out[...] = keep_ref[first + k] + got_ref[k]


def mean_kernel(total_rows, *refs):
    total = refs[0][...]
    for piece in refs[1:-1]:
        total = total + piece[...]
    refs[-1][...] = total / total_rows


def chrom_scatter(gives, keep):
    sums, first = [], keep.shape[0]
    for part in gives[::-1]:
        count = part.shape[0]
        first -= count
        kernel = functools.partial(chip_kernel, first)
        sums = list(call(kernel, [shape(keep.shape[1:])] * count, [whole()] * 2)(keep, swap(part, "chrom", 1))) + sums
    return [sums[0]] + [swap(sums[k], "chrom", 2 * k) for k in reversed(range(1, len(sums)))]


def chrom_order(size):
    return list(reversed(range(size)))


def chrom_gather(own):
    size = lax.axis_size("chrom")
    direct = {bits: swap(own, "chrom", bits) for bits in chrom_order(size)[:-1] if bits < 4 or bits % 2 == 0}
    direct[0] = own
    return [direct[bits] if bits in direct else swap(direct[bits - 1], "chrom", 1) for bits in chrom_order(size)]


def samp_order(size):
    return list(reversed(range(size)))


def samp_gather(own):
    size = lax.axis_size("samp")
    return [own] + [swap(own, "samp", k) for k in samp_order(size)[:-1]][::-1]


def body(dosages, traits, start_coef, groups, tested, owners):
    n_samp, n_chrom = lax.axis_size("samp"), lax.axis_size("chrom")
    rows, cols = dosages.shape
    tests, n_traits = tested.shape[1], traits.shape[1]
    total_rows = rows * n_samp
    half, block, width, test_width = n_chrom // 2, rows // n_chrom, cols // n_samp, tests // n_samp
    flops = 4 * rows * cols * n_traits
    moved = 2 * rows * cols
    order = samp_order(n_samp)
    others, own = order[:-1], order[-1:]

    part = shape((rows // 2, cols), jnp.bfloat16)
    half_out = shape((half, block, n_traits))
    give_outs = [shape((count, block, n_traits)) for count in (half // 2, half - half // 2)]
    packed_cols = shape((cols, 2 * n_traits), jnp.bfloat16)
    packed_rows = shape((2 * n_traits, rows), jnp.bfloat16)
    rows_buffer = [pltpu.VMEM((rows, 2 * n_traits), jnp.bfloat16)]
    grad_block = shape((width, n_traits))
    score_block = shape((test_width + STATS, n_traits))
    coef_out = shape((cols, n_traits))
    group_rows = groups.reshape(cols // 128, 128)
    owner_rows = owners.reshape(n_samp, 1, test_width)

    def near(packed):
        return call(near_kernel, [give_outs[0], half_out], [whole()] * 5, (), 2 * flops, 2 * moved)(
            high1, low1, high0, low0, packed
        )

    def own_residual(summands, after=()):
        return call(
            functools.partial(residual_kernel, len(summands)),
            shape((block, n_traits)),
            [whole()] * (1 + len(summands)) + [anywhere()] * len(after),
        )(traits, *summands, *after)

    coefficients = start_coef
    kept_shape = (half, block, cols)
    high1, low1, *gives, packed, kept = call(
        first_kernel,
        [part, part] + give_outs + [packed_cols, shape(kept_shape)],
        [pl.BlockSpec(memory_space=pltpu.HBM)] * 2,
        [pltpu.VMEM(kept_shape, jnp.float32), pltpu.VMEM(coefficients.shape, jnp.float32), pltpu.SemaphoreType.DMA((n_chrom * PARTS + 1,))],
        flops,
        4 * moved,
    )(
        pltpu.with_memory_space_constraint(dosages.reshape(half, 2, block, cols), pltpu.HBM),
        pltpu.with_memory_space_constraint(coefficients, pltpu.HBM),
    )
    high0, low0, keep = call(second_kernel, [part, part, half_out], [whole()] * 2, (), flops, moved)(kept, packed)
    summands = chrom_scatter(gives, keep)
    parts = [high0, low0, high1, low1]
    tested_sq = call(square_kernel, shape((n_samp, test_width // 128, 128)), [whole()], (), 0, 2 * rows * tests)(tested)

    for iteration in range(ITERS):
        pieces = chrom_gather(own_residual(summands))
        packed, *far_out = call(
            functools.partial(grad_far_kernel, n_chrom, others),
            [packed_rows] + [grad_block] * len(others),
            [whole()] * (n_chrom + 4),
            rows_buffer,
            flops,
            moved,
        )(*pieces, *parts)
        near_out = call(
            functools.partial(grad_near_kernel, own), [grad_block] * len(own), [whole()] * 5, (), flops, moved
        )(packed, *parts)
        received = [swap(piece, "samp", partner) for partner, piece in zip(order, far_out)]
        own_grad = call(functools.partial(mean_kernel, total_rows), grad_block, [whole()] * n_samp)(
            near_out[-1], *received[::-1]
        )
        pieces = samp_gather(own_grad)
        after = (tested_sq,) if iteration == 0 else ()
        gradient, packed, far_give = call(
            functools.partial(image_kernel, n_samp),
            [coef_out, packed_cols, give_outs[1]],
            [whole()] * (n_samp + 2) + [anywhere()] * len(after),
            (),
            flops,
            moved,
        )(*pieces, high1, low1, *after)
        near_give, keep = near(packed)
        summands = chrom_scatter([near_give, far_give], keep)
        size = n_samp * n_chrom
        sums = call(
            functools.partial(norm_kernel, half), shape((size, 2, n_traits)), [whole()] * (half + 1)
        )(own_grad, *summands)
        sums = lax.all_to_all(sums, ("samp", "chrom"), 0, 0)
        coefficients, packed, far_give = call(
            functools.partial(prox_kernel, total_rows),
            [coef_out, packed_cols, give_outs[1]],
            [whole()] * 5,
            (),
            flops,
            moved,
        )(coefficients, gradient, sums, high1, low1)
        near_give, keep = near(packed)
        summands = chrom_scatter([near_give, far_give], keep)

    own_parts = call(own_kernel, [shape((rows, n_traits))] * GPD, [whole()] * 6, (), 4 * flops, 4 * moved)(
        coefficients, group_rows, *parts
    )
    pieces = chrom_gather(own_residual(summands, own_parts))
    loco, loco_sq, *far_out = call(
        functools.partial(loco_kernel, n_chrom, others),
        [shape((GPD * n_traits, rows), jnp.bfloat16), shape((STATS, n_traits))]
        + [score_block] * len(others),
        [whole()] * (n_chrom + GPD + 3),
        [pltpu.VMEM((rows, GPD * n_traits), jnp.bfloat16)],
        flops,
        moved,
    )(*pieces, *own_parts, tested, tested_sq, owner_rows)
    residual, *near_out = call(
        functools.partial(loco_near_kernel, n_chrom, own),
        [shape((rows, n_traits))] + [score_block] * len(own),
        [whole()] * (n_chrom + 5),
        (),
        flops // 2,
        moved,
    )(*pieces, tested, tested_sq, owner_rows, loco, loco_sq)
    received = [swap(piece, "samp", partner) for partner, piece in zip(order, far_out)]
    own_scores = call(
        functools.partial(score_kernel, total_rows), shape((test_width, n_traits)), [whole()] * (n_samp + 1)
    )(owner_rows, near_out[-1], *received[::-1])
    scores = pl.pallas_call(
        place_kernel,
        out_shape=shape((tests, n_traits)),
        in_specs=[whole()] * n_samp,
        out_specs=anywhere(),
        scratch_shapes=[pltpu.SemaphoreType.DMA((n_samp,))],
        compiler_params=pltpu.CompilerParams(vmem_limit_bytes=VMEM_LIMIT),
    )(*samp_gather(own_scores))
    return (scores, residual)


def solution(mesh):
    placed = (
        P("samp", "chrom"),
        P("samp", None),
        P("chrom", None),
        P("chrom"),
        P("samp", "chrom"),
        P("chrom"),
    )
    return jax.shard_map(
        body,
        mesh=mesh,
        in_specs=placed,
        out_specs=(P("chrom", None), P("samp", None)),
        check_vma=False,
    )
```

```python
import functools
import math

import jax
import jax.numpy as jnp
from jax import lax
from jax.experimental import pallas as pl
from jax.experimental.pallas import tpu as pltpu
from jax.sharding import PartitionSpec as P

GPD = 2
ITERS = 2
STATS = 8
PARTS = 2
VMEM_LIMIT = 10 * 1024 * 1024


def swap(value, axis, bits):
    size = lax.axis_size(axis)
    return lax.ppermute(value, axis, [(i, i ^ bits) for i in range(size)])


def split(value):
    high = value.astype(jnp.bfloat16)
    low = (value - high.astype(jnp.float32)).astype(jnp.bfloat16)
    return high, low


def pack(value):
    return jnp.concatenate(split(value), axis=1)


def wide_dot(high, low, packed):
    total = jnp.dot(high, packed, preferred_element_type=jnp.float32)
    total = total + jnp.dot(low, packed, preferred_element_type=jnp.float32)
    traits = packed.shape[1] // 2
    return total[:, :traits] + total[:, traits:]


def whole():
    return pl.BlockSpec(memory_space=pltpu.VMEM)


def anywhere():
    return pl.BlockSpec(memory_space=pl.ANY)


def shape(dims, dtype=jnp.float32):
    return jax.ShapeDtypeStruct(dims, dtype)


def call(kernel, outs, specs, scratch=(), flops=0, moved=0):
    return pl.pallas_call(
        kernel,
        out_shape=outs,
        in_specs=specs,
        out_specs=jax.tree.map(lambda _: whole(), outs),
        scratch_shapes=list(scratch),
        compiler_params=pltpu.CompilerParams(vmem_limit_bytes=VMEM_LIMIT),
        cost_estimate=pl.CostEstimate(flops=flops, bytes_accessed=moved, transcendentals=0),
    )


def store_places(total, out_refs, first=0):
    block = out_refs[0].shape[1]
    for k in range(total.shape[0] // block):
        place = first + k
        for out in out_refs:
            if 0 <= place < out.shape[0]:
                out[place] = total[k * block : (k + 1) * block]
            place -= out.shape[0]


def split_rows(source_ref, ready, packed_ref, high_ref, low_ref, out_refs):
    half, block = source_ref.shape[0], source_ref.shape[1]
    group = max(1, half // 2)
    for first in range(0, half, group):
        for k in range(first, first + group):
            ready(k)
            high, low = split(source_ref[k])
            high_ref[k * block : (k + 1) * block] = high
            low_ref[k * block : (k + 1) * block] = low
        rows = slice(first * block, (first + group) * block)
        total = wide_dot(high_ref[rows], low_ref[rows], packed_ref[...])
        store_places(total, out_refs, first)


def first_kernel(dosage_ref, coef_ref, high_ref, low_ref, *refs):
    *out_refs, packed_ref, kept_ref, buffer_ref, coef_buffer, sems = refs
    me = lax.axis_index("chrom")
    place, core = me // 2, me % 2
    half = buffer_ref.shape[0]
    coef_copy = pltpu.make_async_copy(coef_ref, coef_buffer, sems.at[2 * half * PARTS])
    part = buffer_ref.shape[1] // PARTS
    copies = [
        [
            pltpu.make_async_copy(
                dosage_ref.at[place ^ k, core ^ bits, pl.ds(p * part, part)],
                target.at[k, pl.ds(p * part, part)],
                sems.at[(bits * half + k) * PARTS + p],
            )
            for p in range(PARTS)
        ]
        for bits, target in ((1, buffer_ref), (0, kept_ref))
        for k in range(half)
    ]
    coef_copy.start()
    for group in copies:
        for copy in group:
            copy.start()

    def ready(k):
        for copy in copies[k]:
            copy.wait()

    coef_copy.wait()
    packed_ref[...] = pack(coef_buffer[...])
    split_rows(buffer_ref, ready, packed_ref, high_ref, low_ref, out_refs)
    for group in copies[half:]:
        for copy in group:
            copy.wait()


def second_kernel(kept_ref, packed_ref, high_ref, low_ref, out_ref):
    split_rows(kept_ref, lambda k: None, packed_ref, high_ref, low_ref, [out_ref])


def square_kernel(tested_ref, square_ref):
    for place in range(square_ref.shape[0]):
        width = square_ref.shape[1] * square_ref.shape[2]
        value = tested_ref[:, place * width : (place + 1) * width].astype(jnp.float32)
        square_ref[place] = jnp.sum(value * value, axis=0).reshape(square_ref.shape[1:])


def column(row):
    down = lax.broadcasted_iota(jnp.int32, (128, 128), 0)
    across = lax.broadcasted_iota(jnp.int32, (128, 128), 1)
    return jnp.sum(jnp.where(down == across, row, 0.0), axis=1, keepdims=True)


def columns(ref):
    return jnp.concatenate([column(ref[k : k + 1]) for k in range(ref.shape[0])])


def residual_kernel(count, traits_ref, *refs):
    out = refs[-1]
    block = out.shape[0]
    total = refs[0][...]
    for piece in refs[1:count]:
        total = total + piece[...]
    start = pl.multiple_of(lax.axis_index("chrom") * block, block)
    out[...] = traits_ref[pl.ds(start, block)] - total


def grad_dot(packed_ref, parts, which, width):
    half = packed_ref.shape[1] // 2
    cols = pl.ds(pl.multiple_of(which * width, width), width)
    total = None
    for place, part in enumerate(parts):
        left = packed_ref[:, (place // 2) * half : (place // 2 + 1) * half]
        term = jnp.dot(left, part[:, cols], preferred_element_type=jnp.float32)
        total = term if total is None else total + term
    traits = packed_ref.shape[0] // 2
    return (total[:traits] + total[traits:]).T


def grad_far_kernel(count, partners, *refs):
    pieces, parts, (packed_ref, *outs) = refs[:count], refs[count : count + 4], refs[count + 4 : -1]
    rows_ref = refs[-1]
    samp = lax.axis_index("samp")
    block = pieces[0].shape[0]
    for bits, piece in zip(chrom_order(count), pieces):
        start = ((bits % 2) * (count // 2) + bits // 2) * block
        rows_ref[start : start + block] = pack(piece[...])
    packed_ref[...] = rows_ref[...].T
    for place, partner in enumerate(partners):
        first, second = outs[2 * place : 2 * place + 2]
        rows = first.shape[0]
        total = grad_dot(packed_ref, parts, samp ^ partner, 2 * rows)
        first[...] = total[:rows]
        second[...] = total[rows:]


def grad_near_kernel(partners, *refs):
    packed_ref, parts, outs = refs[0], refs[1:5], refs[5:]
    samp = lax.axis_index("samp")
    for place, partner in enumerate(partners):
        first, second = outs[2 * place : 2 * place + 2]
        rows = first.shape[0]
        total = grad_dot(packed_ref, parts, samp ^ partner, 2 * rows)
        first[...] = total[:rows]
        second[...] = total[rows:]


def image_kernel(count, *refs):
    pieces = refs[:count]
    high_ref, low_ref = refs[count : count + 2]
    grad_ref, packed_ref, far_ref = refs[-3:]
    samp = lax.axis_index("samp")
    block = pieces[0].shape[0]
    for place, piece in enumerate(pieces):
        bits, second = place % (count // 2), place // (count // 2)
        rows = pl.ds(pl.multiple_of(((samp ^ bits) * 2 + second) * block, block), block)
        value = piece[...]
        grad_ref[rows] = value
        packed_ref[rows] = pack(value)
    far_kernel(high_ref, low_ref, packed_ref, far_ref)


def norm_kernel(count, *refs):
    grad_refs, pieces, out = refs[:2], refs[2 : count + 2], refs[-1]
    total = pieces[0][...]
    for piece in pieces[1:]:
        total = total + piece[...]
    grad_sq = sum(jnp.sum(ref[...] * ref[...], axis=0, keepdims=True) for ref in grad_refs)
    image_sq = jnp.sum(total * total, axis=0, keepdims=True)
    sums = jnp.concatenate([grad_sq, image_sq])
    for place in range(out.shape[0]):
        out[place] = sums


def far_kernel(high_ref, low_ref, packed_ref, out_ref):
    rows = pl.ds(high_ref.shape[0] - out_ref.shape[0] * out_ref.shape[1], out_ref.shape[0] * out_ref.shape[1])
    store_places(wide_dot(high_ref[rows], low_ref[rows], packed_ref[...]), [out_ref])


def near_kernel(high1_ref, low1_ref, high0_ref, low0_ref, packed_ref, near_ref, keep_ref):
    rows = pl.ds(0, near_ref.shape[0] * near_ref.shape[1])
    store_places(wide_dot(high1_ref[rows], low1_ref[rows], packed_ref[...]), [near_ref])
    store_places(wide_dot(high0_ref[...], low0_ref[...], packed_ref[...]), [keep_ref])


def prox_kernel(total_rows, coef_ref, grad_ref, sums_ref, high_ref, low_ref, new_ref, packed_ref, far_ref):
    sums = sums_ref[0]
    for place in range(1, sums_ref.shape[0]):
        sums = sums + sums_ref[place]
    grad_sq = jnp.sum(sums[0:1], axis=1, keepdims=True)
    image_sq = jnp.sum(sums[1:2], axis=1, keepdims=True)
    step_size = grad_sq / (image_sq / total_rows + 1e-06)
    penalty = 1.5 * math.sqrt(coef_ref.shape[1] / total_rows)
    moved = coef_ref[...] + step_size * grad_ref[...]
    length = jnp.sqrt(jnp.sum(moved * moved, axis=1, keepdims=True))
    cut = step_size * penalty
    new = moved * (jnp.maximum(length - cut, 0.0) / jnp.maximum(length, cut))
    new_ref[...] = new
    packed_ref[...] = pack(new)
    far_kernel(high_ref, low_ref, packed_ref, far_ref)


def own_kernel(coef_ref, group_ref, *refs):
    parts, outs = refs[:4], refs[4:]
    coef = coef_ref[...]
    base = lax.axis_index("chrom") * GPD
    local = columns((group_ref[...] - base).astype(jnp.float32))
    half = parts[0].shape[0]
    for which, out in enumerate(outs):
        packed = pack(jnp.where(local == which, coef, 0.0))
        out[0:half] = wide_dot(parts[0][...], parts[1][...], packed)
        out[half:] = wide_dot(parts[2][...], parts[3][...], packed)


def score_products(partner, out, tested_ref, square_ref, owner_ref, loco_ref, sums_ref):
    width, traits = out.shape[0] - STATS, out.shape[1]
    cols = pl.ds(pl.multiple_of(partner * width, width), width)
    products = jnp.dot(loco_ref[...], tested_ref[:, cols], preferred_element_type=jnp.float32)
    local = owner_ref[partner] - lax.axis_index("chrom") * GPD
    chosen = products[:traits]
    for which in range(1, GPD):
        chosen = jnp.where(local == which, products[which * traits : (which + 1) * traits], chosen)
    out[0:width] = chosen.T
    out[width : width + STATS] = sums_ref[...]
    out[width + GPD : width + GPD + square_ref.shape[1]] = square_ref[partner]


def loco_kernel(count, partners, *refs):
    pieces, own_refs = refs[:count], refs[count : count + GPD]
    tested_ref, square_ref, owner_ref, loco_ref, sums_ref = refs[count + GPD : count + GPD + 5]
    outs, rows_ref = refs[count + GPD + 5 : -1], refs[-1]
    me, samp = lax.axis_index("chrom"), lax.axis_index("samp")
    block, traits = pieces[0].shape
    sums_ref[...] = jnp.zeros_like(sums_ref)
    for bits, piece in zip(chrom_order(count), pieces):
        rows = pl.ds(pl.multiple_of((me ^ bits) * block, block), block)
        start = ((bits % 2) * (count // 2) + bits // 2) * block
        value = piece[...]
        for which in range(GPD):
            loco = value + own_refs[which][start : start + block]
            sums_ref[which : which + 1] += jnp.sum(loco * loco, axis=0, keepdims=True)
            rows_ref[rows, which * traits : (which + 1) * traits] = loco.astype(jnp.bfloat16)
    loco_ref[...] = rows_ref[...].T
    for partner, out in zip(partners, outs):
        score_products(samp ^ partner, out, tested_ref, square_ref, owner_ref, loco_ref, sums_ref)


def loco_near_kernel(count, partners, *refs):
    pieces, operands, residual_ref, outs = refs[:count], refs[count : count + 5], refs[count + 5], refs[count + 6 :]
    me, samp = lax.axis_index("chrom"), lax.axis_index("samp")
    block = pieces[0].shape[0]
    for bits, piece in zip(chrom_order(count), pieces):
        residual_ref[pl.ds(pl.multiple_of((me ^ bits) * block, block), block)] = piece[...]
    for partner, out in zip(partners, outs):
        score_products(samp ^ partner, out, *operands)


def score_kernel(total_rows, owner_ref, *refs):
    pieces, out = refs[:-1], refs[-1]
    total = pieces[0][...]
    for piece in pieces[1:]:
        total = total + piece[...]
    cols, traits = out.shape
    base = lax.axis_index("chrom") * GPD
    owner = (owner_ref[lax.axis_index("samp")] - base).astype(jnp.float32)
    local = jnp.concatenate([column(owner[:, k * 128 : (k + 1) * 128]) for k in range(cols // 128)])
    loco_sq = jnp.broadcast_to(total[cols : cols + 1], (cols, traits))
    for which in range(1, GPD):
        loco_sq = jnp.where(local == which, total[cols + which : cols + which + 1], loco_sq)
    tested_sq = columns(total[cols + GPD : cols + GPD + cols // 128])
    denom = math.sqrt(total_rows) * jnp.sqrt((tested_sq / total_rows + 1e-06) * (loco_sq / total_rows + 1e-06))
    out[...] = total[:cols] / denom


def place_kernel(*refs):
    pieces, out, sems = refs[:-2], refs[-2], refs[-1]
    samp = lax.axis_index("samp")
    block = pieces[0].shape[0]
    copies = [
        pltpu.make_async_copy(
            piece, out.at[pl.ds(pl.multiple_of((samp ^ bits) * block, block), block)], sems.at[bits]
        )
        for bits, piece in enumerate(pieces)
    ]
    for copy in copies:
        copy.start()
    for copy in copies:
        copy.wait()


def chip_kernel(first, keep_ref, got_ref, *outs):
    for k, out in enumerate(outs):
        out[...] = keep_ref[first + k] + got_ref[k]


def mean_kernel(total_rows, *refs):
    total = refs[0][...]
    for piece in refs[1:-1]:
        total = total + piece[...]
    refs[-1][...] = total / total_rows


def chrom_scatter(gives, keep):
    sums, first = [], keep.shape[0]
    for part in gives[::-1]:
        count = part.shape[0]
        first -= count
        kernel = functools.partial(chip_kernel, first)
        sums = list(call(kernel, [shape(keep.shape[1:])] * count, [whole()] * 2)(keep, swap(part, "chrom", 1))) + sums
    return [sums[0]] + [swap(sums[k], "chrom", 2 * k) for k in reversed(range(1, len(sums)))]


def chrom_order(size):
    return list(reversed(range(size)))


def chrom_gather(own):
    size = lax.axis_size("chrom")
    direct = {bits: swap(own, "chrom", bits) for bits in chrom_order(size)[:-1] if bits < 4 or bits % 2 == 0}
    direct[0] = own
    return [direct[bits] if bits in direct else swap(direct[bits - 1], "chrom", 1) for bits in chrom_order(size)]


def samp_order(size):
    return list(reversed(range(size)))


def samp_gather(own):
    size = lax.axis_size("samp")
    return [own] + [swap(own, "samp", k) for k in samp_order(size)[:-1]][::-1]


def body(dosages, traits, start_coef, groups, tested, owners):
    n_samp, n_chrom = lax.axis_size("samp"), lax.axis_size("chrom")
    rows, cols = dosages.shape
    tests, n_traits = tested.shape[1], traits.shape[1]
    total_rows = rows * n_samp
    half, block, width, test_width = n_chrom // 2, rows // n_chrom, cols // n_samp, tests // n_samp
    flops = 4 * rows * cols * n_traits
    moved = 2 * rows * cols
    order = samp_order(n_samp)
    others, own = order[:-1], order[-1:]

    part = shape((rows // 2, cols), jnp.bfloat16)
    half_out = shape((half, block, n_traits))
    give_outs = [shape((count, block, n_traits)) for count in (half // 2, half - half // 2)]
    packed_cols = shape((cols, 2 * n_traits), jnp.bfloat16)
    packed_rows = shape((2 * n_traits, rows), jnp.bfloat16)
    rows_buffer = [pltpu.VMEM((rows, 2 * n_traits), jnp.bfloat16)]
    grad_block = shape((width // 2, n_traits))
    score_block = shape((test_width + STATS, n_traits))
    coef_out = shape((cols, n_traits))
    group_rows = groups.reshape(cols // 128, 128)
    owner_rows = owners.reshape(n_samp, 1, test_width)

    def near(packed):
        return call(near_kernel, [give_outs[0], half_out], [whole()] * 5, (), 2 * flops, 2 * moved)(
            high1, low1, high0, low0, packed
        )

    def own_residual(summands, after=()):
        return call(
            functools.partial(residual_kernel, len(summands)),
            shape((block, n_traits)),
            [whole()] * (1 + len(summands)) + [anywhere()] * len(after),
        )(traits, *summands, *after)

    coefficients = start_coef
    kept_shape = (half, block, cols)
    high1, low1, *gives, packed, kept = call(
        first_kernel,
        [part, part] + give_outs + [packed_cols, shape(kept_shape)],
        [pl.BlockSpec(memory_space=pltpu.HBM)] * 2,
        [pltpu.VMEM(kept_shape, jnp.float32), pltpu.VMEM(coefficients.shape, jnp.float32), pltpu.SemaphoreType.DMA((n_chrom * PARTS + 1,))],
        flops,
        4 * moved,
    )(
        pltpu.with_memory_space_constraint(dosages.reshape(half, 2, block, cols), pltpu.HBM),
        pltpu.with_memory_space_constraint(coefficients, pltpu.HBM),
    )
    high0, low0, keep = call(second_kernel, [part, part, half_out], [whole()] * 2, (), flops, moved)(kept, packed)
    summands = chrom_scatter(gives, keep)
    parts = [high0, low0, high1, low1]
    tested_sq = call(square_kernel, shape((n_samp, test_width // 128, 128)), [whole()], (), 0, 2 * rows * tests)(tested)

    for iteration in range(ITERS):
        pieces = chrom_gather(own_residual(summands))
        packed, *far_out = call(
            functools.partial(grad_far_kernel, n_chrom, others),
            [packed_rows] + [grad_block] * (2 * len(others)),
            [whole()] * (n_chrom + 4),
            rows_buffer,
            flops,
            moved,
        )(*pieces, *parts)
        near_out = call(
            functools.partial(grad_near_kernel, own), [grad_block] * (2 * len(own)), [whole()] * 5, (), flops, moved
        )(packed, *parts)
        received = [
            [swap(piece, "samp", partner) for partner, piece in zip(order, far_out[second::2])][::-1]
            for second in range(2)
        ]
        mean = call(functools.partial(mean_kernel, total_rows), grad_block, [whole()] * n_samp)
        own_grad = [mean(near_out[second], *received[second]) for second in range(2)]
        pieces = samp_gather(own_grad[0]) + samp_gather(own_grad[1])
        after = (tested_sq,) if iteration == 0 else ()
        gradient, packed, far_give = call(
            functools.partial(image_kernel, 2 * n_samp),
            [coef_out, packed_cols, give_outs[1]],
            [whole()] * (2 * n_samp + 2) + [anywhere()] * len(after),
            (),
            flops,
            moved,
        )(*pieces, high1, low1, *after)
        near_give, keep = near(packed)
        summands = chrom_scatter([near_give, far_give], keep)
        size = n_samp * n_chrom
        sums = call(
            functools.partial(norm_kernel, half), shape((size, 2, n_traits)), [whole()] * (half + 2)
        )(*own_grad, *summands)
        sums = lax.all_to_all(sums, ("samp", "chrom"), 0, 0)
        coefficients, packed, far_give = call(
            functools.partial(prox_kernel, total_rows),
            [coef_out, packed_cols, give_outs[1]],
            [whole()] * 5,
            (),
            flops,
            moved,
        )(coefficients, gradient, sums, high1, low1)
        near_give, keep = near(packed)
        summands = chrom_scatter([near_give, far_give], keep)

    own_parts = call(own_kernel, [shape((rows, n_traits))] * GPD, [whole()] * 6, (), 4 * flops, 4 * moved)(
        coefficients, group_rows, *parts
    )
    pieces = chrom_gather(own_residual(summands, own_parts))
    loco, loco_sq, *far_out = call(
        functools.partial(loco_kernel, n_chrom, others),
        [shape((GPD * n_traits, rows), jnp.bfloat16), shape((STATS, n_traits))]
        + [score_block] * len(others),
        [whole()] * (n_chrom + GPD + 3),
        [pltpu.VMEM((rows, GPD * n_traits), jnp.bfloat16)],
        flops,
        moved,
    )(*pieces, *own_parts, tested, tested_sq, owner_rows)
    residual, *near_out = call(
        functools.partial(loco_near_kernel, n_chrom, own),
        [shape((rows, n_traits))] + [score_block] * len(own),
        [whole()] * (n_chrom + 5),
        (),
        flops // 2,
        moved,
    )(*pieces, tested, tested_sq, owner_rows, loco, loco_sq)
    received = [swap(piece, "samp", partner) for partner, piece in zip(order, far_out)]
    own_scores = call(
        functools.partial(score_kernel, total_rows), shape((test_width, n_traits)), [whole()] * (n_samp + 1)
    )(owner_rows, near_out[-1], *received[::-1])
    scores = pl.pallas_call(
        place_kernel,
        out_shape=shape((tests, n_traits)),
        in_specs=[whole()] * n_samp,
        out_specs=anywhere(),
        scratch_shapes=[pltpu.SemaphoreType.DMA((n_samp,))],
        compiler_params=pltpu.CompilerParams(vmem_limit_bytes=VMEM_LIMIT),
    )(*samp_gather(own_scores))
    return (scores, residual)


def solution(mesh):
    placed = (
        P("samp", "chrom"),
        P("samp", None),
        P("chrom", None),
        P("chrom"),
        P("samp", "chrom"),
        P("chrom"),
    )
    return jax.shard_map(
        body,
        mesh=mesh,
        in_specs=placed,
        out_specs=(P("chrom", None), P("samp", None)),
        check_vma=False,
    )
```

```python
import functools
import math

import jax
import jax.numpy as jnp
from jax import lax
from jax.experimental import pallas as pl
from jax.experimental.pallas import tpu as pltpu
from jax.sharding import PartitionSpec as P

GPD = 2
ITERS = 2
STATS = 8
PARTS = 2
VMEM_LIMIT = 10 * 1024 * 1024


def swap(value, axis, bits):
    size = lax.axis_size(axis)
    return lax.ppermute(value, axis, [(i, i ^ bits) for i in range(size)])


def split(value):
    high = value.astype(jnp.bfloat16)
    low = (value - high.astype(jnp.float32)).astype(jnp.bfloat16)
    return high, low


def pack(value):
    return jnp.concatenate(split(value), axis=1)


def wide_dot(high, low, packed):
    total = jnp.dot(high, packed, preferred_element_type=jnp.float32)
    total = total + jnp.dot(low, packed, preferred_element_type=jnp.float32)
    traits = packed.shape[1] // 2
    return total[:, :traits] + total[:, traits:]


def whole():
    return pl.BlockSpec(memory_space=pltpu.VMEM)


def anywhere():
    return pl.BlockSpec(memory_space=pl.ANY)


def shape(dims, dtype=jnp.float32):
    return jax.ShapeDtypeStruct(dims, dtype)


def call(kernel, outs, specs, scratch=(), flops=0, moved=0):
    return pl.pallas_call(
        kernel,
        out_shape=outs,
        in_specs=specs,
        out_specs=jax.tree.map(lambda _: whole(), outs),
        scratch_shapes=list(scratch),
        compiler_params=pltpu.CompilerParams(vmem_limit_bytes=VMEM_LIMIT),
        cost_estimate=pl.CostEstimate(flops=flops, bytes_accessed=moved, transcendentals=0),
    )


def store_places(total, out_refs, first=0):
    block = out_refs[0].shape[1]
    for k in range(total.shape[0] // block):
        place = first + k
        for out in out_refs:
            if 0 <= place < out.shape[0]:
                out[place] = total[k * block : (k + 1) * block]
            place -= out.shape[0]


def split_rows(source_ref, ready, packed_ref, high_ref, low_ref, out_refs):
    half, block = source_ref.shape[0], source_ref.shape[1]
    group = max(1, half // 2)
    for first in range(0, half, group):
        for k in range(first, first + group):
            ready(k)
            high, low = split(source_ref[k])
            high_ref[k * block : (k + 1) * block] = high
            low_ref[k * block : (k + 1) * block] = low
        rows = slice(first * block, (first + group) * block)
        total = wide_dot(high_ref[rows], low_ref[rows], packed_ref[...])
        store_places(total, out_refs, first)


def first_kernel(dosage_ref, coef_ref, high_ref, low_ref, *refs):
    *out_refs, packed_ref, kept_ref, buffer_ref, coef_buffer, sems = refs
    me = lax.axis_index("chrom")
    place, core = me // 2, me % 2
    half = buffer_ref.shape[0]
    coef_copy = pltpu.make_async_copy(coef_ref, coef_buffer, sems.at[2 * half * PARTS])
    part = buffer_ref.shape[1] // PARTS
    copies = [
        [
            pltpu.make_async_copy(
                dosage_ref.at[place ^ k, core ^ bits, pl.ds(p * part, part)],
                target.at[k, pl.ds(p * part, part)],
                sems.at[(bits * half + k) * PARTS + p],
            )
            for p in range(PARTS)
        ]
        for bits, target in ((1, buffer_ref), (0, kept_ref))
        for k in range(half)
    ]
    coef_copy.start()
    for group in copies:
        for copy in group:
            copy.start()

    def ready(k):
        for copy in copies[k]:
            copy.wait()

    coef_copy.wait()
    packed_ref[...] = pack(coef_buffer[...])
    split_rows(buffer_ref, ready, packed_ref, high_ref, low_ref, out_refs)
    for group in copies[half:]:
        for copy in group:
            copy.wait()


def second_kernel(kept_ref, packed_ref, high_ref, low_ref, out_ref):
    split_rows(kept_ref, lambda k: None, packed_ref, high_ref, low_ref, [out_ref])


def square_kernel(tested_ref, square_ref):
    for place in range(square_ref.shape[0]):
        width = square_ref.shape[1] * square_ref.shape[2]
        value = tested_ref[:, place * width : (place + 1) * width].astype(jnp.float32)
        square_ref[place] = jnp.sum(value * value, axis=0).reshape(square_ref.shape[1:])


def column(row):
    down = lax.broadcasted_iota(jnp.int32, (128, 128), 0)
    across = lax.broadcasted_iota(jnp.int32, (128, 128), 1)
    return jnp.sum(jnp.where(down == across, row, 0.0), axis=1, keepdims=True)


def columns(ref):
    return jnp.concatenate([column(ref[k : k + 1]) for k in range(ref.shape[0])])


def residual_kernel(count, traits_ref, *refs):
    out = refs[-1]
    block = out.shape[0]
    total = refs[0][...]
    for piece in refs[1:count]:
        total = total + piece[...]
    start = pl.multiple_of(lax.axis_index("chrom") * block, block)
    out[...] = traits_ref[pl.ds(start, block)] - total


def grad_dot(packed_ref, parts, which, width):
    half = packed_ref.shape[1] // 2
    cols = pl.ds(pl.multiple_of(which * width, width), width)
    total = None
    for place, part in enumerate(parts):
        left = packed_ref[:, (place // 2) * half : (place // 2 + 1) * half]
        term = jnp.dot(left, part[:, cols], preferred_element_type=jnp.float32)
        total = term if total is None else total + term
    traits = packed_ref.shape[0] // 2
    return (total[:traits] + total[traits:]).T


def grad_far_kernel(count, partners, *refs):
    pieces, parts, (packed_ref, *outs) = refs[:count], refs[count : count + 4], refs[count + 4 : -1]
    rows_ref = refs[-1]
    samp = lax.axis_index("samp")
    block = pieces[0].shape[0]
    for bits, piece in zip(chrom_order(count), pieces):
        start = ((bits % 2) * (count // 2) + bits // 2) * block
        rows_ref[start : start + block] = pack(piece[...])
    packed_ref[...] = rows_ref[...].T
    for partner, out in zip(partners, outs):
        out[...] = grad_dot(packed_ref, parts, samp ^ partner, out.shape[0])


def grad_near_kernel(partners, *refs):
    packed_ref, parts, outs = refs[0], refs[1:5], refs[5:]
    samp = lax.axis_index("samp")
    for partner, out in zip(partners, outs):
        out[...] = grad_dot(packed_ref, parts, samp ^ partner, out.shape[0])


def image_kernel(count, *refs):
    pieces = refs[:count]
    high_ref, low_ref = refs[count : count + 2]
    grad_ref, packed_ref, far_ref = refs[-3:]
    samp = lax.axis_index("samp")
    block = pieces[0].shape[0]
    for bits, piece in enumerate(pieces):
        rows = pl.ds(pl.multiple_of((samp ^ bits) * block, block), block)
        value = piece[...]
        grad_ref[rows] = value
        packed_ref[rows] = pack(value)
    far_kernel(high_ref, low_ref, packed_ref, far_ref)


def norm_kernel(count, *refs):
    grad_ref, pieces, out = refs[0], refs[1 : count + 1], refs[-1]
    total = pieces[0][...]
    for piece in pieces[1:]:
        total = total + piece[...]
    grad = grad_ref[...]
    grad_sq = jnp.sum(grad * grad, axis=0, keepdims=True)
    image_sq = jnp.sum(total * total, axis=0, keepdims=True)
    sums = jnp.concatenate([grad_sq, image_sq])
    for place in range(out.shape[0]):
        out[place] = sums


def far_kernel(high_ref, low_ref, packed_ref, out_ref):
    rows = pl.ds(high_ref.shape[0] - out_ref.shape[0] * out_ref.shape[1], out_ref.shape[0] * out_ref.shape[1])
    store_places(wide_dot(high_ref[rows], low_ref[rows], packed_ref[...]), [out_ref])


def near_kernel(high1_ref, low1_ref, high0_ref, low0_ref, packed_ref, near_ref, keep_ref):
    rows = pl.ds(0, near_ref.shape[0] * near_ref.shape[1])
    store_places(wide_dot(high1_ref[rows], low1_ref[rows], packed_ref[...]), [near_ref])
    store_places(wide_dot(high0_ref[...], low0_ref[...], packed_ref[...]), [keep_ref])


def prox_kernel(total_rows, coef_ref, grad_ref, sums_ref, high_ref, low_ref, new_ref, packed_ref, far_ref):
    sums = sums_ref[0]
    for place in range(1, sums_ref.shape[0]):
        sums = sums + sums_ref[place]
    grad_sq = jnp.sum(sums[0:1], axis=1, keepdims=True)
    image_sq = jnp.sum(sums[1:2], axis=1, keepdims=True)
    step_size = grad_sq / (image_sq / total_rows + 1e-06)
    penalty = 1.5 * math.sqrt(coef_ref.shape[1] / total_rows)
    moved = coef_ref[...] + step_size * grad_ref[...]
    length = jnp.sqrt(jnp.sum(moved * moved, axis=1, keepdims=True))
    cut = step_size * penalty
    new = moved * (jnp.maximum(length - cut, 0.0) / jnp.maximum(length, cut))
    new_ref[...] = new
    packed_ref[...] = pack(new)
    far_kernel(high_ref, low_ref, packed_ref, far_ref)


def own_kernel(coef_ref, group_ref, *refs):
    parts, outs = refs[:4], refs[4:]
    coef = coef_ref[...]
    base = lax.axis_index("chrom") * GPD
    local = columns((group_ref[...] - base).astype(jnp.float32))
    half = parts[0].shape[0]
    for which, out in enumerate(outs):
        packed = pack(jnp.where(local == which, coef, 0.0))
        out[0:half] = wide_dot(parts[0][...], parts[1][...], packed)
        out[half:] = wide_dot(parts[2][...], parts[3][...], packed)


def score_products(partner, out, tested_ref, square_ref, owner_ref, loco_ref, sums_ref):
    width, traits = out.shape[0] - STATS, out.shape[1]
    cols = pl.ds(pl.multiple_of(partner * width, width), width)
    products = jnp.dot(loco_ref[...], tested_ref[:, cols], preferred_element_type=jnp.float32)
    local = owner_ref[partner] - lax.axis_index("chrom") * GPD
    chosen = products[:traits]
    for which in range(1, GPD):
        chosen = jnp.where(local == which, products[which * traits : (which + 1) * traits], chosen)
    out[0:width] = chosen.T
    out[width : width + STATS] = sums_ref[...]
    out[width + GPD : width + GPD + square_ref.shape[1]] = square_ref[partner]


def loco_kernel(count, partners, *refs):
    pieces, own_refs = refs[:count], refs[count : count + GPD]
    tested_ref, square_ref, owner_ref, loco_ref, sums_ref = refs[count + GPD : count + GPD + 5]
    outs, rows_ref = refs[count + GPD + 5 : -1], refs[-1]
    me, samp = lax.axis_index("chrom"), lax.axis_index("samp")
    block, traits = pieces[0].shape
    sums_ref[...] = jnp.zeros_like(sums_ref)
    for bits, piece in zip(chrom_order(count), pieces):
        rows = pl.ds(pl.multiple_of((me ^ bits) * block, block), block)
        start = ((bits % 2) * (count // 2) + bits // 2) * block
        value = piece[...]
        for which in range(GPD):
            loco = value + own_refs[which][start : start + block]
            sums_ref[which : which + 1] += jnp.sum(loco * loco, axis=0, keepdims=True)
            rows_ref[rows, which * traits : (which + 1) * traits] = loco.astype(jnp.bfloat16)
    loco_ref[...] = rows_ref[...].T
    for partner, out in zip(partners, outs):
        score_products(samp ^ partner, out, tested_ref, square_ref, owner_ref, loco_ref, sums_ref)


def loco_near_kernel(count, partners, *refs):
    pieces, operands, residual_ref, outs = refs[:count], refs[count : count + 5], refs[count + 5], refs[count + 6 :]
    me, samp = lax.axis_index("chrom"), lax.axis_index("samp")
    block = pieces[0].shape[0]
    for bits, piece in zip(chrom_order(count), pieces):
        residual_ref[pl.ds(pl.multiple_of((me ^ bits) * block, block), block)] = piece[...]
    for partner, out in zip(partners, outs):
        score_products(samp ^ partner, out, *operands)


def score_kernel(total_rows, owner_ref, *refs):
    pieces, out = refs[:-1], refs[-1]
    total = pieces[0][...]
    for piece in pieces[1:]:
        total = total + piece[...]
    cols, traits = out.shape
    base = lax.axis_index("chrom") * GPD
    owner = (owner_ref[lax.axis_index("samp")] - base).astype(jnp.float32)
    local = jnp.concatenate([column(owner[:, k * 128 : (k + 1) * 128]) for k in range(cols // 128)])
    loco_sq = jnp.broadcast_to(total[cols : cols + 1], (cols, traits))
    for which in range(1, GPD):
        loco_sq = jnp.where(local == which, total[cols + which : cols + which + 1], loco_sq)
    tested_sq = columns(total[cols + GPD : cols + GPD + cols // 128])
    denom = math.sqrt(total_rows) * jnp.sqrt((tested_sq / total_rows + 1e-06) * (loco_sq / total_rows + 1e-06))
    out[...] = total[:cols] / denom


def place_kernel(*refs):
    pieces, out, sems = refs[:-2], refs[-2], refs[-1]
    samp = lax.axis_index("samp")
    block = pieces[0].shape[0]
    copies = [
        pltpu.make_async_copy(
            piece, out.at[pl.ds(pl.multiple_of((samp ^ bits) * block, block), block)], sems.at[bits]
        )
        for bits, piece in enumerate(pieces)
    ]
    for copy in copies:
        copy.start()
    for copy in copies:
        copy.wait()


def chip_kernel(first, keep_ref, got_ref, *outs):
    for k, out in enumerate(outs):
        out[...] = keep_ref[first + k] + got_ref[k]


def mean_kernel(total_rows, *refs):
    total = refs[0][...]
    for piece in refs[1:-1]:
        total = total + piece[...]
    refs[-1][...] = total / total_rows


def chrom_scatter(gives, keep):
    sums, first = [], keep.shape[0]
    for part in gives[::-1]:
        count = part.shape[0]
        first -= count
        kernel = functools.partial(chip_kernel, first)
        sums = list(call(kernel, [shape(keep.shape[1:])] * count, [whole()] * 2)(keep, swap(part, "chrom", 1))) + sums
    return [sums[0]] + [swap(sums[k], "chrom", 2 * k) for k in chip_order(len(sums))[:-1]]


def chip_order(count):
    order = list(reversed(range(count)))
    return order[1::-1] + order[2:] if count > 2 else order


def chrom_order(size):
    return [2 * k + bits for k in chip_order(size // 2) for bits in (range(2) if k > 1 else (1, 0))]


def chrom_gather(own):
    size = lax.axis_size("chrom")
    direct = {bits: swap(own, "chrom", bits) for bits in chrom_order(size)[:-1] if bits < 4 or bits % 2 == 0}
    direct[0] = own
    return [direct[bits] if bits in direct else swap(direct[bits - 1], "chrom", 1) for bits in chrom_order(size)]


def samp_order(size):
    return list(reversed(range(size)))


def samp_gather(own):
    size = lax.axis_size("samp")
    return [own] + [swap(own, "samp", k) for k in samp_order(size)[:-1]][::-1]


def body(dosages, traits, start_coef, groups, tested, owners):
    n_samp, n_chrom = lax.axis_size("samp"), lax.axis_size("chrom")
    rows, cols = dosages.shape
    tests, n_traits = tested.shape[1], traits.shape[1]
    total_rows = rows * n_samp
    half, block, width, test_width = n_chrom // 2, rows // n_chrom, cols // n_samp, tests // n_samp
    flops = 4 * rows * cols * n_traits
    moved = 2 * rows * cols
    order = samp_order(n_samp)
    others, own = order[:-1], order[-1:]

    part = shape((rows // 2, cols), jnp.bfloat16)
    half_out = shape((half, block, n_traits))
    give_outs = [shape((count, block, n_traits)) for count in (half // 2, half - half // 2)]
    packed_cols = shape((cols, 2 * n_traits), jnp.bfloat16)
    packed_rows = shape((2 * n_traits, rows), jnp.bfloat16)
    rows_buffer = [pltpu.VMEM((rows, 2 * n_traits), jnp.bfloat16)]
    grad_block = shape((width, n_traits))
    score_block = shape((test_width + STATS, n_traits))
    coef_out = shape((cols, n_traits))
    group_rows = groups.reshape(cols // 128, 128)
    owner_rows = owners.reshape(n_samp, 1, test_width)

    def near(packed):
        return call(near_kernel, [give_outs[0], half_out], [whole()] * 5, (), 2 * flops, 2 * moved)(
            high1, low1, high0, low0, packed
        )

    def own_residual(summands, after=()):
        return call(
            functools.partial(residual_kernel, len(summands)),
            shape((block, n_traits)),
            [whole()] * (1 + len(summands)) + [anywhere()] * len(after),
        )(traits, *summands, *after)

    coefficients = start_coef
    kept_shape = (half, block, cols)
    high1, low1, *gives, packed, kept = call(
        first_kernel,
        [part, part] + give_outs + [packed_cols, shape(kept_shape)],
        [pl.BlockSpec(memory_space=pltpu.HBM)] * 2,
        [pltpu.VMEM(kept_shape, jnp.float32), pltpu.VMEM(coefficients.shape, jnp.float32), pltpu.SemaphoreType.DMA((n_chrom * PARTS + 1,))],
        flops,
        4 * moved,
    )(
        pltpu.with_memory_space_constraint(dosages.reshape(half, 2, block, cols), pltpu.HBM),
        pltpu.with_memory_space_constraint(coefficients, pltpu.HBM),
    )
    high0, low0, keep = call(second_kernel, [part, part, half_out], [whole()] * 2, (), flops, moved)(kept, packed)
    summands = chrom_scatter(gives, keep)
    parts = [high0, low0, high1, low1]
    tested_sq = call(square_kernel, shape((n_samp, test_width // 128, 128)), [whole()], (), 0, 2 * rows * tests)(tested)

    for iteration in range(ITERS):
        pieces = chrom_gather(own_residual(summands))
        packed, *far_out = call(
            functools.partial(grad_far_kernel, n_chrom, others),
            [packed_rows] + [grad_block] * len(others),
            [whole()] * (n_chrom + 4),
            rows_buffer,
            flops,
            moved,
        )(*pieces, *parts)
        near_out = call(
            functools.partial(grad_near_kernel, own), [grad_block] * len(own), [whole()] * 5, (), flops, moved
        )(packed, *parts)
        received = [swap(piece, "samp", partner) for partner, piece in zip(order, far_out)]
        own_grad = call(functools.partial(mean_kernel, total_rows), grad_block, [whole()] * n_samp)(
            near_out[-1], *received[::-1]
        )
        pieces = samp_gather(own_grad)
        after = (tested_sq,) if iteration == 0 else ()
        gradient, packed, far_give = call(
            functools.partial(image_kernel, n_samp),
            [coef_out, packed_cols, give_outs[1]],
            [whole()] * (n_samp + 2) + [anywhere()] * len(after),
            (),
            flops,
            moved,
        )(*pieces, high1, low1, *after)
        near_give, keep = near(packed)
        summands = chrom_scatter([near_give, far_give], keep)
        size = n_samp * n_chrom
        sums = call(
            functools.partial(norm_kernel, half), shape((size, 2, n_traits)), [whole()] * (half + 1)
        )(own_grad, *summands)
        sums = lax.all_to_all(sums, ("samp", "chrom"), 0, 0)
        coefficients, packed, far_give = call(
            functools.partial(prox_kernel, total_rows),
            [coef_out, packed_cols, give_outs[1]],
            [whole()] * 5,
            (),
            flops,
            moved,
        )(coefficients, gradient, sums, high1, low1)
        near_give, keep = near(packed)
        summands = chrom_scatter([near_give, far_give], keep)

    own_parts = call(own_kernel, [shape((rows, n_traits))] * GPD, [whole()] * 6, (), 4 * flops, 4 * moved)(
        coefficients, group_rows, *parts
    )
    pieces = chrom_gather(own_residual(summands, own_parts))
    loco, loco_sq, *far_out = call(
        functools.partial(loco_kernel, n_chrom, others),
        [shape((GPD * n_traits, rows), jnp.bfloat16), shape((STATS, n_traits))]
        + [score_block] * len(others),
        [whole()] * (n_chrom + GPD + 3),
        [pltpu.VMEM((rows, GPD * n_traits), jnp.bfloat16)],
        flops,
        moved,
    )(*pieces, *own_parts, tested, tested_sq, owner_rows)
    residual, *near_out = call(
        functools.partial(loco_near_kernel, n_chrom, own),
        [shape((rows, n_traits))] + [score_block] * len(own),
        [whole()] * (n_chrom + 5),
        (),
        flops // 2,
        moved,
    )(*pieces, tested, tested_sq, owner_rows, loco, loco_sq)
    received = [swap(piece, "samp", partner) for partner, piece in zip(order, far_out)]
    own_scores = call(
        functools.partial(score_kernel, total_rows), shape((test_width, n_traits)), [whole()] * (n_samp + 1)
    )(owner_rows, near_out[-1], *received[::-1])
    scores = pl.pallas_call(
        place_kernel,
        out_shape=shape((tests, n_traits)),
        in_specs=[whole()] * n_samp,
        out_specs=anywhere(),
        scratch_shapes=[pltpu.SemaphoreType.DMA((n_samp,))],
        compiler_params=pltpu.CompilerParams(vmem_limit_bytes=VMEM_LIMIT),
    )(*samp_gather(own_scores))
    return (scores, residual)


def solution(mesh):
    placed = (
        P("samp", "chrom"),
        P("samp", None),
        P("chrom", None),
        P("chrom"),
        P("samp", "chrom"),
        P("chrom"),
    )
    return jax.shard_map(
        body,
        mesh=mesh,
        in_specs=placed,
        out_specs=(P("chrom", None), P("samp", None)),
        check_vma=False,
    )
```

```python
import functools
import math

import jax
import jax.numpy as jnp
from jax import lax
from jax.experimental import pallas as pl
from jax.experimental.pallas import tpu as pltpu
from jax.sharding import PartitionSpec as P

GPD = 2
ITERS = 2
STATS = 8
PARTS = 2
VMEM_LIMIT = 10 * 1024 * 1024


def swap(value, axis, bits):
    size = lax.axis_size(axis)
    return lax.ppermute(value, axis, [(i, i ^ bits) for i in range(size)])


def split(value):
    high = value.astype(jnp.bfloat16)
    low = (value - high.astype(jnp.float32)).astype(jnp.bfloat16)
    return high, low


def pack(value):
    return jnp.concatenate(split(value), axis=1)


def wide_dot(high, low, packed):
    total = jnp.dot(high, packed, preferred_element_type=jnp.float32)
    total = total + jnp.dot(low, packed, preferred_element_type=jnp.float32)
    traits = packed.shape[1] // 2
    return total[:, :traits] + total[:, traits:]


def whole():
    return pl.BlockSpec(memory_space=pltpu.VMEM)


def anywhere():
    return pl.BlockSpec(memory_space=pl.ANY)


def shape(dims, dtype=jnp.float32):
    return jax.ShapeDtypeStruct(dims, dtype)


def call(kernel, outs, specs, scratch=(), flops=0, moved=0):
    return pl.pallas_call(
        kernel,
        out_shape=outs,
        in_specs=specs,
        out_specs=jax.tree.map(lambda _: whole(), outs),
        scratch_shapes=list(scratch),
        compiler_params=pltpu.CompilerParams(vmem_limit_bytes=VMEM_LIMIT),
        cost_estimate=pl.CostEstimate(flops=flops, bytes_accessed=moved, transcendentals=0),
    )


def store_places(total, out_refs, first=0):
    block = out_refs[0].shape[1]
    for k in range(total.shape[0] // block):
        place = first + k
        for out in out_refs:
            if 0 <= place < out.shape[0]:
                out[place] = total[k * block : (k + 1) * block]
            place -= out.shape[0]


def split_rows(source_ref, ready, packed_ref, high_ref, low_ref, out_refs):
    half, block = source_ref.shape[0], source_ref.shape[1]
    group = max(1, half // 2)
    for first in range(0, half, group):
        for k in range(first, first + group):
            ready(k)
            high, low = split(source_ref[k])
            high_ref[k * block : (k + 1) * block] = high
            low_ref[k * block : (k + 1) * block] = low
        rows = slice(first * block, (first + group) * block)
        total = wide_dot(high_ref[rows], low_ref[rows], packed_ref[...])
        store_places(total, out_refs, first)


def first_kernel(dosage_ref, coef_ref, high_ref, low_ref, *refs):
    *out_refs, packed_ref, kept_ref, buffer_ref, coef_buffer, sems = refs
    me = lax.axis_index("chrom")
    place, core = me // 2, me % 2
    half = buffer_ref.shape[0]
    coef_copy = pltpu.make_async_copy(coef_ref, coef_buffer, sems.at[2 * half * PARTS])
    part = buffer_ref.shape[1] // PARTS
    copies = [
        [
            pltpu.make_async_copy(
                dosage_ref.at[place ^ k, core ^ bits, pl.ds(p * part, part)],
                target.at[k, pl.ds(p * part, part)],
                sems.at[(bits * half + k) * PARTS + p],
            )
            for p in range(PARTS)
        ]
        for bits, target in ((1, buffer_ref), (0, kept_ref))
        for k in range(half)
    ]
    coef_copy.start()
    for group in copies:
        for copy in group:
            copy.start()

    def ready(k):
        for copy in copies[k]:
            copy.wait()

    coef_copy.wait()
    packed_ref[...] = pack(coef_buffer[...])
    split_rows(buffer_ref, ready, packed_ref, high_ref, low_ref, out_refs)
    for group in copies[half:]:
        for copy in group:
            copy.wait()


def second_kernel(kept_ref, packed_ref, high_ref, low_ref, out_ref):
    split_rows(kept_ref, lambda k: None, packed_ref, high_ref, low_ref, [out_ref])


def square_kernel(tested_ref, square_ref):
    for place in range(square_ref.shape[0]):
        width = square_ref.shape[1] * square_ref.shape[2]
        value = tested_ref[:, place * width : (place + 1) * width].astype(jnp.float32)
        square_ref[place] = jnp.sum(value * value, axis=0).reshape(square_ref.shape[1:])


def column(row):
    down = lax.broadcasted_iota(jnp.int32, (128, 128), 0)
    across = lax.broadcasted_iota(jnp.int32, (128, 128), 1)
    return jnp.sum(jnp.where(down == across, row, 0.0), axis=1, keepdims=True)


def columns(ref):
    return jnp.concatenate([column(ref[k : k + 1]) for k in range(ref.shape[0])])


def residual_kernel(count, traits_ref, *refs):
    out = refs[-1]
    block = out.shape[0]
    total = refs[0][...]
    for piece in refs[1:count]:
        total = total + piece[...]
    start = pl.multiple_of(lax.axis_index("chrom") * block, block)
    out[...] = traits_ref[pl.ds(start, block)] - total


def grad_dot(packed_ref, parts, which, width):
    half = packed_ref.shape[1] // 2
    cols = pl.ds(pl.multiple_of(which * width, width), width)
    total = None
    for place, part in enumerate(parts):
        left = packed_ref[:, (place // 2) * half : (place // 2 + 1) * half]
        term = jnp.dot(left, part[:, cols], preferred_element_type=jnp.float32)
        total = term if total is None else total + term
    traits = packed_ref.shape[0] // 2
    return (total[:traits] + total[traits:]).T


def grad_far_kernel(count, partners, *refs):
    pieces, parts, (packed_ref, *outs) = refs[:count], refs[count : count + 4], refs[count + 4 : -1]
    rows_ref = refs[-1]
    samp = lax.axis_index("samp")
    block = pieces[0].shape[0]
    for bits, piece in zip(chrom_order(count), pieces):
        start = ((bits % 2) * (count // 2) + bits // 2) * block
        rows_ref[start : start + block] = pack(piece[...])
    packed_ref[...] = rows_ref[...].T
    for partner, out in zip(partners, outs):
        out[...] = grad_dot(packed_ref, parts, samp ^ partner, out.shape[0])


def grad_near_kernel(partners, *refs):
    packed_ref, parts, outs = refs[0], refs[1:5], refs[5:]
    samp = lax.axis_index("samp")
    for partner, out in zip(partners, outs):
        out[...] = grad_dot(packed_ref, parts, samp ^ partner, out.shape[0])


def image_kernel(count, *refs):
    pieces = refs[:count]
    high_ref, low_ref = refs[count : count + 2]
    grad_ref, packed_ref, far_ref = refs[-3:]
    samp = lax.axis_index("samp")
    block = pieces[0].shape[0]
    for bits, piece in enumerate(pieces):
        rows = pl.ds(pl.multiple_of((samp ^ bits) * block, block), block)
        value = piece[...]
        grad_ref[rows] = value
        packed_ref[rows] = pack(value)
    far_kernel(high_ref, low_ref, packed_ref, far_ref)


def norm_kernel(count, *refs):
    grad_ref, pieces, out = refs[0], refs[1 : count + 1], refs[-1]
    total = pieces[0][...]
    for piece in pieces[1:]:
        total = total + piece[...]
    grad = grad_ref[...]
    grad_sq = jnp.sum(grad * grad, axis=0, keepdims=True)
    image_sq = jnp.sum(total * total, axis=0, keepdims=True)
    sums = jnp.concatenate([grad_sq, image_sq])
    for place in range(out.shape[0]):
        out[place] = sums


def far_kernel(high_ref, low_ref, packed_ref, out_ref):
    rows = pl.ds(high_ref.shape[0] - out_ref.shape[0] * out_ref.shape[1], out_ref.shape[0] * out_ref.shape[1])
    store_places(wide_dot(high_ref[rows], low_ref[rows], packed_ref[...]), [out_ref])


def near_kernel(high1_ref, low1_ref, high0_ref, low0_ref, packed_ref, near_ref, keep_ref):
    rows = pl.ds(0, near_ref.shape[0] * near_ref.shape[1])
    store_places(wide_dot(high1_ref[rows], low1_ref[rows], packed_ref[...]), [near_ref])
    store_places(wide_dot(high0_ref[...], low0_ref[...], packed_ref[...]), [keep_ref])


def prox_kernel(total_rows, coef_ref, grad_ref, sums_ref, high_ref, low_ref, new_ref, packed_ref, far_ref):
    sums = sums_ref[0]
    for place in range(1, sums_ref.shape[0]):
        sums = sums + sums_ref[place]
    grad_sq = jnp.sum(sums[0:1], axis=1, keepdims=True)
    image_sq = jnp.sum(sums[1:2], axis=1, keepdims=True)
    step_size = grad_sq / (image_sq / total_rows + 1e-06)
    penalty = 1.5 * math.sqrt(coef_ref.shape[1] / total_rows)
    moved = coef_ref[...] + step_size * grad_ref[...]
    length = jnp.sqrt(jnp.sum(moved * moved, axis=1, keepdims=True))
    cut = step_size * penalty
    new = moved * (jnp.maximum(length - cut, 0.0) / jnp.maximum(length, cut))
    new_ref[...] = new
    packed_ref[...] = pack(new)
    far_kernel(high_ref, low_ref, packed_ref, far_ref)


def own_kernel(coef_ref, group_ref, *refs):
    parts, outs = refs[:4], refs[4:]
    coef = coef_ref[...]
    base = lax.axis_index("chrom") * GPD
    local = columns((group_ref[...] - base).astype(jnp.float32))
    half = parts[0].shape[0]
    for which, out in enumerate(outs):
        packed = pack(jnp.where(local == which, coef, 0.0))
        out[0:half] = wide_dot(parts[0][...], parts[1][...], packed)
        out[half:] = wide_dot(parts[2][...], parts[3][...], packed)


def score_products(partner, out, tested_ref, square_ref, owner_ref, loco_ref, sums_ref):
    width, traits = out.shape[0] - STATS, out.shape[1]
    cols = pl.ds(pl.multiple_of(partner * width, width), width)
    products = jnp.dot(loco_ref[...], tested_ref[:, cols], preferred_element_type=jnp.float32)
    local = owner_ref[partner] - lax.axis_index("chrom") * GPD
    chosen = products[:traits]
    for which in range(1, GPD):
        chosen = jnp.where(local == which, products[which * traits : (which + 1) * traits], chosen)
    out[0:width] = chosen.T
    out[width : width + STATS] = sums_ref[...]
    out[width + GPD : width + GPD + square_ref.shape[1]] = square_ref[partner]


def loco_kernel(count, partners, *refs):
    pieces, own_refs = refs[:count], refs[count : count + GPD]
    tested_ref, square_ref, owner_ref, loco_ref, sums_ref = refs[count + GPD : count + GPD + 5]
    outs, rows_ref = refs[count + GPD + 5 : -1], refs[-1]
    me, samp = lax.axis_index("chrom"), lax.axis_index("samp")
    block, traits = pieces[0].shape
    sums_ref[...] = jnp.zeros_like(sums_ref)
    for bits, piece in zip(chrom_order(count), pieces):
        rows = pl.ds(pl.multiple_of((me ^ bits) * block, block), block)
        start = ((bits % 2) * (count // 2) + bits // 2) * block
        value = piece[...]
        for which in range(GPD):
            loco = value + own_refs[which][start : start + block]
            sums_ref[which : which + 1] += jnp.sum(loco * loco, axis=0, keepdims=True)
            rows_ref[rows, which * traits : (which + 1) * traits] = loco.astype(jnp.bfloat16)
    loco_ref[...] = rows_ref[...].T
    for partner, out in zip(partners, outs):
        score_products(samp ^ partner, out, tested_ref, square_ref, owner_ref, loco_ref, sums_ref)


def loco_near_kernel(count, partners, *refs):
    pieces, operands, residual_ref, outs = refs[:count], refs[count : count + 5], refs[count + 5], refs[count + 6 :]
    me, samp = lax.axis_index("chrom"), lax.axis_index("samp")
    block = pieces[0].shape[0]
    for bits, piece in zip(chrom_order(count), pieces):
        residual_ref[pl.ds(pl.multiple_of((me ^ bits) * block, block), block)] = piece[...]
    for partner, out in zip(partners, outs):
        score_products(samp ^ partner, out, *operands)


def score_kernel(total_rows, owner_ref, *refs):
    pieces, out = refs[:-1], refs[-1]
    total = pieces[0][...]
    for piece in pieces[1:]:
        total = total + piece[...]
    cols, traits = out.shape
    base = lax.axis_index("chrom") * GPD
    owner = (owner_ref[lax.axis_index("samp")] - base).astype(jnp.float32)
    local = jnp.concatenate([column(owner[:, k * 128 : (k + 1) * 128]) for k in range(cols // 128)])
    loco_sq = jnp.broadcast_to(total[cols : cols + 1], (cols, traits))
    for which in range(1, GPD):
        loco_sq = jnp.where(local == which, total[cols + which : cols + which + 1], loco_sq)
    tested_sq = columns(total[cols + GPD : cols + GPD + cols // 128])
    denom = math.sqrt(total_rows) * jnp.sqrt((tested_sq / total_rows + 1e-06) * (loco_sq / total_rows + 1e-06))
    out[...] = total[:cols] / denom


def place_kernel(*refs):
    pieces, out, sems = refs[:-2], refs[-2], refs[-1]
    samp = lax.axis_index("samp")
    block = pieces[0].shape[0]
    copies = [
        pltpu.make_async_copy(
            piece, out.at[pl.ds(pl.multiple_of((samp ^ bits) * block, block), block)], sems.at[bits]
        )
        for bits, piece in enumerate(pieces)
    ]
    for copy in copies:
        copy.start()
    for copy in copies:
        copy.wait()


def chip_kernel(first, keep_ref, got_ref, *outs):
    for k, out in enumerate(outs):
        out[...] = keep_ref[first + k] + got_ref[k]


def mean_kernel(total_rows, *refs):
    total = refs[0][...]
    for piece in refs[1:-1]:
        total = total + piece[...]
    refs[-1][...] = total / total_rows


def chrom_scatter(gives, keep):
    sums, first = [], keep.shape[0]
    for part in gives[::-1]:
        count = part.shape[0]
        first -= count
        kernel = functools.partial(chip_kernel, first)
        sums = list(call(kernel, [shape(keep.shape[1:])] * count, [whole()] * 2)(keep, swap(part, "chrom", 1))) + sums
    return [sums[0]] + [swap(sums[k], "chrom", 2 * k) for k in reversed(range(1, len(sums)))]


def chip_order(count):
    order = list(reversed(range(count)))
    return order[1::-1] + order[2:] if count > 2 else order


def chrom_order(size):
    return [2 * k + bits for k in chip_order(size // 2) for bits in (range(2) if k > 1 else (1, 0))]


def chrom_gather(own):
    size = lax.axis_size("chrom")
    direct = {bits: swap(own, "chrom", bits) for bits in chrom_order(size)[:-1] if bits < 4 or bits % 2 == 0}
    direct[0] = own
    return [direct[bits] if bits in direct else swap(direct[bits - 1], "chrom", 1) for bits in chrom_order(size)]


def samp_order(size):
    return list(reversed(range(size)))


def samp_gather(own):
    size = lax.axis_size("samp")
    return [own] + [swap(own, "samp", k) for k in samp_order(size)[:-1]][::-1]


def body(dosages, traits, start_coef, groups, tested, owners):
    n_samp, n_chrom = lax.axis_size("samp"), lax.axis_size("chrom")
    rows, cols = dosages.shape
    tests, n_traits = tested.shape[1], traits.shape[1]
    total_rows = rows * n_samp
    half, block, width, test_width = n_chrom // 2, rows // n_chrom, cols // n_samp, tests // n_samp
    flops = 4 * rows * cols * n_traits
    moved = 2 * rows * cols
    order = samp_order(n_samp)
    others, own = order[:-1], order[-1:]

    part = shape((rows // 2, cols), jnp.bfloat16)
    half_out = shape((half, block, n_traits))
    give_outs = [shape((count, block, n_traits)) for count in (half // 2, half - half // 2)]
    packed_cols = shape((cols, 2 * n_traits), jnp.bfloat16)
    packed_rows = shape((2 * n_traits, rows), jnp.bfloat16)
    rows_buffer = [pltpu.VMEM((rows, 2 * n_traits), jnp.bfloat16)]
    grad_block = shape((width, n_traits))
    score_block = shape((test_width + STATS, n_traits))
    coef_out = shape((cols, n_traits))
    group_rows = groups.reshape(cols // 128, 128)
    owner_rows = owners.reshape(n_samp, 1, test_width)

    def near(packed):
        return call(near_kernel, [give_outs[0], half_out], [whole()] * 5, (), 2 * flops, 2 * moved)(
            high1, low1, high0, low0, packed
        )

    def own_residual(summands, after=()):
        return call(
            functools.partial(residual_kernel, len(summands)),
            shape((block, n_traits)),
            [whole()] * (1 + len(summands)) + [anywhere()] * len(after),
        )(traits, *summands, *after)

    coefficients = start_coef
    kept_shape = (half, block, cols)
    high1, low1, *gives, packed, kept = call(
        first_kernel,
        [part, part] + give_outs + [packed_cols, shape(kept_shape)],
        [pl.BlockSpec(memory_space=pltpu.HBM)] * 2,
        [pltpu.VMEM(kept_shape, jnp.float32), pltpu.VMEM(coefficients.shape, jnp.float32), pltpu.SemaphoreType.DMA((n_chrom * PARTS + 1,))],
        flops,
        4 * moved,
    )(
        pltpu.with_memory_space_constraint(dosages.reshape(half, 2, block, cols), pltpu.HBM),
        pltpu.with_memory_space_constraint(coefficients, pltpu.HBM),
    )
    high0, low0, keep = call(second_kernel, [part, part, half_out], [whole()] * 2, (), flops, moved)(kept, packed)
    summands = chrom_scatter(gives, keep)
    parts = [high0, low0, high1, low1]
    tested_sq = call(square_kernel, shape((n_samp, test_width // 128, 128)), [whole()], (), 0, 2 * rows * tests)(tested)

    for iteration in range(ITERS):
        pieces = chrom_gather(own_residual(summands))
        packed, *far_out = call(
            functools.partial(grad_far_kernel, n_chrom, others),
            [packed_rows] + [grad_block] * len(others),
            [whole()] * (n_chrom + 4),
            rows_buffer,
            flops,
            moved,
        )(*pieces, *parts)
        near_out = call(
            functools.partial(grad_near_kernel, own), [grad_block] * len(own), [whole()] * 5, (), flops, moved
        )(packed, *parts)
        received = [swap(piece, "samp", partner) for partner, piece in zip(order, far_out)]
        own_grad = call(functools.partial(mean_kernel, total_rows), grad_block, [whole()] * n_samp)(
            near_out[-1], *received[::-1]
        )
        pieces = samp_gather(own_grad)
        after = (tested_sq,) if iteration == 0 else ()
        gradient, packed, far_give = call(
            functools.partial(image_kernel, n_samp),
            [coef_out, packed_cols, give_outs[1]],
            [whole()] * (n_samp + 2) + [anywhere()] * len(after),
            (),
            flops,
            moved,
        )(*pieces, high1, low1, *after)
        near_give, keep = near(packed)
        summands = chrom_scatter([near_give, far_give], keep)
        size = n_samp * n_chrom
        sums = call(
            functools.partial(norm_kernel, half), shape((size, 2, n_traits)), [whole()] * (half + 1)
        )(own_grad, *summands)
        sums = lax.all_to_all(sums, ("samp", "chrom"), 0, 0)
        coefficients, packed, far_give = call(
            functools.partial(prox_kernel, total_rows),
            [coef_out, packed_cols, give_outs[1]],
            [whole()] * 5,
            (),
            flops,
            moved,
        )(coefficients, gradient, sums, high1, low1)
        near_give, keep = near(packed)
        summands = chrom_scatter([near_give, far_give], keep)

    own_parts = call(own_kernel, [shape((rows, n_traits))] * GPD, [whole()] * 6, (), 4 * flops, 4 * moved)(
        coefficients, group_rows, *parts
    )
    pieces = chrom_gather(own_residual(summands, own_parts))
    loco, loco_sq, *far_out = call(
        functools.partial(loco_kernel, n_chrom, others),
        [shape((GPD * n_traits, rows), jnp.bfloat16), shape((STATS, n_traits))]
        + [score_block] * len(others),
        [whole()] * (n_chrom + GPD + 3),
        [pltpu.VMEM((rows, GPD * n_traits), jnp.bfloat16)],
        flops,
        moved,
    )(*pieces, *own_parts, tested, tested_sq, owner_rows)
    residual, *near_out = call(
        functools.partial(loco_near_kernel, n_chrom, own),
        [shape((rows, n_traits))] + [score_block] * len(own),
        [whole()] * (n_chrom + 5),
        (),
        flops // 2,
        moved,
    )(*pieces, tested, tested_sq, owner_rows, loco, loco_sq)
    received = [swap(piece, "samp", partner) for partner, piece in zip(order, far_out)]
    own_scores = call(
        functools.partial(score_kernel, total_rows), shape((test_width, n_traits)), [whole()] * (n_samp + 1)
    )(owner_rows, near_out[-1], *received[::-1])
    scores = pl.pallas_call(
        place_kernel,
        out_shape=shape((tests, n_traits)),
        in_specs=[whole()] * n_samp,
        out_specs=anywhere(),
        scratch_shapes=[pltpu.SemaphoreType.DMA((n_samp,))],
        compiler_params=pltpu.CompilerParams(vmem_limit_bytes=VMEM_LIMIT),
    )(*samp_gather(own_scores))
    return (scores, residual)


def solution(mesh):
    placed = (
        P("samp", "chrom"),
        P("samp", None),
        P("chrom", None),
        P("chrom"),
        P("samp", "chrom"),
        P("chrom"),
    )
    return jax.shard_map(
        body,
        mesh=mesh,
        in_specs=placed,
        out_specs=(P("chrom", None), P("samp", None)),
        check_vma=False,
    )
```
